32 devices in a mesh: dp: 16 (over z, y, core), mp: 2 (over x).
Axes of the slice: x: 2, y: 2, z: 4, core: 2. Of those that a mesh axis runs over, the one named last changes fastest.
Arguments:
- byte_ids: int32 [2, 16384, 8], P(None, ('dp', 'mp')), may hold values from 0 to 255
- segment_ids: int32 [2, 16384], P(None, ('dp', 'mp')), may hold values from 0 to 1023, as said below
- embed_table: bfloat16 [256, 1024], P('dp'), may hold values from -6 to 6
- patch_weight: bfloat16 [8192, 1024], P('mp', 'dp'), may hold values from -0.0625 to 0.0625
- norm1_gain: float32 [1024], replicated, may hold values from 0.5 to 1.5
- mamba_in: bfloat16 [1024, 2, 2048], P('dp', None, 'mp'), may hold values from -0.1875 to 0.1875
- mamba_dt: bfloat16 [1024, 32], P('dp', 'mp'), may hold values from -0.1875 to 0.1875
- mamba_bc: bfloat16 [1024, 256], P('dp'), may hold values from -0.1875 to 0.1875
- conv_x: float32 [4, 2048], P(None, 'mp'), may hold values from -3 to 3
- conv_bc: float32 [4, 256], replicated, may hold values from -3 to 3
- dt_bias: float32 [32], P('mp'), may hold values from -4 to -1
- a_log: float32 [32], P('mp'), may hold values from -3 to 1
- d_skip: float32 [32], P('mp'), may hold values from 0.5 to 1.5
- gate_gain: float32 [2048], P('mp'), may hold values from 0.5 to 1.5
- mamba_out: bfloat16 [2048, 1024], P('mp', 'dp'), may hold values from -0.125 to 0.125
- norm2_gain: float32 [1024], replicated, may hold values from 0.5 to 1.5
- attn_qkv: bfloat16 [1024, 3, 1024], P('dp', None, 'mp'), may hold values from -0.1875 to 0.1875
- attn_out: bfloat16 [1024, 1024], P('mp', 'dp'), may hold values from -0.5 to 0.5
- norm3_gain: float32 [1024], replicated, may hold values from 0.5 to 1.5
- ffn_in: bfloat16 [1024, 2, 4096], P('dp', None, 'mp'), may hold values from -0.1875 to 0.1875
- ffn_out: bfloat16 [4096, 1024], P('mp', 'dp'), may hold values from -0.09375 to 0.09375
- d_out: float32 [2, 16384, 1024], P(None, ('dp', 'mp')), may hold values from -6 to 6
Outputs:
- mixed: float32 [2, 16384, 1024], P(None, ('dp', 'mp'))
- grad_embed_table: float32 [256, 1024], replicated
- grad_patch_weight: float32 [8192, 1024], P('mp')
- grad_norm1_gain: float32 [1024], replicated
- grad_mamba_in: float32 [1024, 2, 2048], P(None, None, 'mp')
- grad_mamba_dt: float32 [1024, 32], P(None, 'mp')
- grad_mamba_bc: float32 [1024, 256], replicated
- grad_conv_x: float32 [4, 2048], P(None, 'mp')
- grad_conv_bc: float32 [4, 256], replicated
- grad_dt_bias: float32 [32], P('mp')
- grad_a_log: float32 [32], P('mp')
- grad_d_skip: float32 [32], P('mp')
- grad_gate_gain: float32 [2048], P('mp')
- grad_mamba_out: float32 [2048, 1024], P('mp')
- grad_norm2_gain: float32 [1024], replicated
- grad_attn_qkv: float32 [1024, 3, 1024], P(None, None, 'mp')
- grad_attn_out: float32 [1024, 1024], P('mp')
- grad_norm3_gain: float32 [1024], replicated
- grad_ffn_in: float32 [1024, 2, 4096], P(None, None, 'mp')
- grad_ffn_out: float32 [4096, 1024], P('mp')
The draws below stay inside these ranges and needn't reach their ends.
Inputs may be any that keep to these rules, and one draw needn't show every extreme that they name: `segment_ids`: within each packed row of 1024 patches the ids never fall, start at 0 on the row's first patch and are 1023 on its last; in every row one segment starts within the row's first 512 patches and ends within its last 512.
All inputs are finite; a program needn't handle non-finite values.
Results may differ from the reference program's by a relative error of at most 0.028.
Values may be sent and summed in bfloat16 or wider, within the bound.
No kernel may reach another device: no remote copies, remote signals or barrier semaphores. Data moves between devices by JAX's collectives and lax.ppermute only.
A program may use at most 640 MiB of HBM per device.

```python
import jax
import jax.numpy as jnp
from jax import lax

D = 1024
PATCH = 8
VOCAB = 256
PM = 64
NS = 128
KC = 4
HA = 16
HD = 64
FF = 4096
LEN = 1024
MB = 2
DIN = 2048
HM = 32
PIECE = 512
ROWS = 16384


def draw_segment_ids(key, part):
    key = jax.random.fold_in(key, 11)
    count = MB * ROWS // LEN
    first_key, last_key, cut_key = jax.random.split(key, 3)
    first = jax.random.randint(first_key, (count, 1), 0, PIECE)
    last = LEN - jax.random.randint(last_key, (count, 1), 0, PIECE)
    spots = jnp.arange(LEN, dtype=jnp.int32)[None, :]
    cuts = jax.random.randint(cut_key, (count, LEN), 0, 40) == 0
    edges = (spots < first) & cuts | (spots == first) | (spots > last) & cuts | (spots == last)
    edges = edges & (spots > 0)
    ids = jnp.cumsum(edges.astype(jnp.int32), axis=1).astype(jnp.int32)
    highest = jnp.max(ids, axis=1, keepdims=True)
    ids = jnp.where(ids == highest, LEN - 1, ids).astype(jnp.int32)
    return ids.reshape(MB, ROWS).astype(jnp.int32)


def plant(values, key, smallest, top_value):
    place = [jax.random.randint(jax.random.fold_in(key, axis), (), 0, length) for axis, length in enumerate(values.shape)]
    main_axis = values.shape.index(max(values.shape))
    neighbour = place[:main_axis] + [(place[main_axis] + 1) % values.shape[main_axis]] + place[main_axis + 1:]
    return values.at[tuple(place)].set(smallest).at[tuple(neighbour)].set(top_value)


def level_of(stream_key, shape, cuts, low, largest):
    def one(axis_at, blocks):
        draws = jax.random.uniform(jax.random.fold_in(jax.random.fold_in(stream_key, 6), axis_at), (blocks,), jnp.float32, low / len(cuts), largest / len(cuts))
        return jnp.repeat(jnp.exp(draws), shape[axis_at] // blocks).reshape((-1,) + (1,) * (len(shape) - axis_at - 1))

    loudness = one(*cuts[0])
    for cut in cuts[1:]:
        loudness = loudness * one(*cut)
    return loudness


def centred(own_key, shape, width, reach, cuts=(), kind=jnp.bfloat16):
    level = level_of(own_key, shape, cuts, -0.22, 0.18) if cuts else 1.0
    array = jax.random.normal(own_key, shape, jnp.float32) * width * level
    return jnp.minimum(jnp.maximum(array, -reach), reach).astype(kind)


def setup_inputs(seed: int = 0) -> dict:
    key_list = jax.random.split(jax.random.key(seed), 23)
    byte_ids = plant(jax.random.randint(key_list[0], (MB, ROWS, PATCH), 0, 256), jax.random.fold_in(key_list[0], 1), 0, 255).astype(jnp.int32)
    segment_ids = draw_segment_ids(jax.random.fold_in(key_list[22], 71), 0)
    embed_table = centred(key_list[2], (VOCAB, D), 1.0, 6.0, ((0, 16),))
    patch_weight = centred(key_list[3], (PATCH * D, D), (PATCH * D) ** -0.5, 0.0625, ((0, 2), (1, 16)))
    norm1_gain = jnp.clip(1.0 + 0.1 * jax.random.normal(key_list[4], (D,), jnp.float32), 0.5, 1.5)
    mamba_in = centred(key_list[5], (D, 2, DIN), D ** -0.5, 0.1875, ((0, 16), (2, 2)))
    mamba_dt = centred(key_list[6], (D, HM), D ** -0.5, 0.1875, ((0, 16), (1, 2)))
    mamba_bc = centred(key_list[7], (D, 2 * NS), D ** -0.5, 0.1875, ((0, 16),))
    conv_x = centred(key_list[8], (KC, DIN), KC ** -0.5, 3.0, ((1, 2),), jnp.float32)
    conv_bc = centred(key_list[9], (KC, 2 * NS), KC ** -0.5, 3.0, (), jnp.float32)
    dt_bias = jnp.clip(-4.0 + 3.0 * jax.random.uniform(key_list[10], (HM,), jnp.float32) ** level_of(key_list[10], (HM,), ((0, 2),), -0.2, 0.2), -4.0, -1.0)
    a_log = jnp.clip(-3.0 + 4.0 * jax.random.uniform(key_list[11], (HM,), jnp.float32) ** level_of(key_list[11], (HM,), ((0, 2),), -0.2, 0.2), -3.0, 1.0)
    d_skip = jnp.clip(0.5 + 1.0 * jax.random.uniform(key_list[12], (HM,), jnp.float32) ** level_of(key_list[12], (HM,), ((0, 2),), -0.2, 0.2), 0.5, 1.5)
    gate_gain = jnp.clip(1.0 + 0.1 * jax.random.normal(key_list[13], (DIN,), jnp.float32), 0.5, 1.5)
    mamba_out = centred(key_list[14], (DIN, D), DIN ** -0.5, 0.125, ((0, 2), (1, 16)))
    norm2_gain = jnp.clip(1.0 + 0.1 * jax.random.normal(key_list[15], (D,), jnp.float32), 0.5, 1.5)
    attn_qkv = centred(key_list[16], (D, 3, HA * HD), D ** -0.5, 0.1875, ((0, 16), (2, 2)))
    attn_out = centred(key_list[17], (HA * HD, D), (HA * HD // 8) ** -0.5, 0.5, ((0, 2), (1, 16)))
    norm3_gain = jnp.clip(1.0 + 0.1 * jax.random.normal(key_list[18], (D,), jnp.float32), 0.5, 1.5)
    ffn_in = centred(key_list[19], (D, 2, FF), D ** -0.5, 0.1875, ((0, 16), (2, 2)))
    ffn_out = centred(key_list[20], (FF, D), FF ** -0.5, 0.09375, ((0, 2), (1, 16)))
    d_out = centred(key_list[21], (MB, ROWS, D), 1.0, 6.0, ((1, 32),), jnp.float32)
    return dict(byte_ids=byte_ids, segment_ids=segment_ids, embed_table=embed_table, patch_weight=patch_weight, norm1_gain=norm1_gain, mamba_in=mamba_in, mamba_dt=mamba_dt, mamba_bc=mamba_bc, conv_x=conv_x, conv_bc=conv_bc, dt_bias=dt_bias, a_log=a_log, d_skip=d_skip, gate_gain=gate_gain, mamba_out=mamba_out, norm2_gain=norm2_gain, attn_qkv=attn_qkv, attn_out=attn_out, norm3_gain=norm3_gain, ffn_in=ffn_in, ffn_out=ffn_out, d_out=d_out)


@jax.custom_vjp
def low(v):
    return lax.optimization_barrier(v.astype(jnp.bfloat16)).astype(jnp.float32)

@jax.custom_vjp
def low_back(v):
    return v

def low_keep(v):
    return (low(v), None)

def low_pass(kept, grad):
    return (grad,)

def back_keep(v):
    return (v, None)

def back_low(kept, grad):
    return (low(grad),)
low.defvjp(low_keep, low_pass)
low_back.defvjp(back_keep, back_low)

def exact(left, right):
    return jnp.dot(left, right, precision=lax.Precision.HIGHEST)

def rms_apply(hidden, gain):
    return hidden * lax.rsqrt(lax.optimization_barrier(jnp.mean(hidden * hidden, axis=-1, keepdims=True)) + 1e-05) * gain

def conv_rows(signal, weights, seg):
    taps = weights.shape[0]
    total = weights[taps - 1] * signal
    for lag in range(1, taps):
        moved = jnp.concatenate([jnp.zeros((lag, signal.shape[1]), signal.dtype), signal[:-lag]], axis=0)
        same = jnp.concatenate([jnp.zeros((lag,), dtype=bool), seg[lag:] == seg[:-lag]], axis=0)
        total = total + weights[taps - 1 - lag] * moved * same[:, None]
    return total

def mixer_core(gate_part, xin, bc, dtr, seg, conv_x, conv_bc, dt_bias, a_log, d_skip):
    length = gate_part.shape[0]
    heads = dtr.shape[1]
    xs = jax.nn.silu(conv_rows(xin, conv_x, seg))
    bcs = low(low_back(jax.nn.silu(conv_rows(bc, conv_bc, seg))))
    inner = exact(bcs[:, NS:], bcs[:, :NS].T)
    steps = jax.nn.softplus(dtr + dt_bias)
    cumul = jnp.cumsum(-jnp.exp(a_log) * steps, axis=0)
    spots = jnp.arange(length)
    keep = (spots[:, None] >= spots[None, :]) & (seg[:, None] == seg[None, :])
    channels = xs.reshape(length, heads, PM)

    def one_head(items):
        cum_head, step_head, chan_head, skip_head = items
        spread = cum_head[:, None] - cum_head[None, :]
        mixing = low(low_back(jnp.where(keep, jnp.exp(jnp.where(keep, spread, 0.0)), 0.0) * inner))
        driven = low(low_back(step_head[:, None] * chan_head))
        return exact(mixing, driven) + skip_head * chan_head
    result = lax.map(jax.checkpoint(one_head), (cumul.T, steps.T, channels.transpose(1, 0, 2), d_skip))
    return result.transpose(1, 0, 2).reshape(length, heads * PM) * jax.nn.silu(gate_part)

def attend_rows(query, keys, vals, seg):
    length = query.shape[0]
    heads = query.shape[1] // HD
    spots = jnp.arange(length)
    keep = (spots[:, None] >= spots[None, :]) & (seg[:, None] == seg[None, :])

    def one_head(items):
        q_head, k_head, v_head = items
        scores = exact(q_head, k_head.T) * HD ** (-0.5)
        scores = jnp.where(keep, scores, -1e+30)
        top = lax.optimization_barrier(jnp.max(scores, axis=-1, keepdims=True))
        weights = jnp.exp(scores - top)
        weights = low(low_back(weights / lax.optimization_barrier(jnp.sum(weights, axis=-1, keepdims=True))))
        return exact(weights, v_head)
    split = lambda block: block.reshape(length, heads, HD).transpose(1, 0, 2)
    result = lax.map(jax.checkpoint(one_head), (split(query), split(keys), split(vals)))
    return result.transpose(1, 0, 2).reshape(length, heads * HD)

def layer_rows(params, ids, seg):
    table, patch_weight, norm1_gain, mamba_in, mamba_dt, mamba_bc, conv_x, conv_bc, dt_bias, a_log, d_skip, gate_gain, mamba_out, norm2_gain, attn_qkv, attn_out, norm3_gain, ffn_in, ffn_out = params
    embedded = table[ids].reshape(ids.shape[0], PATCH * D)
    resid = low_back(exact(embedded, patch_weight))
    normed = low(rms_apply(resid, norm1_gain))
    gate_part = low_back(exact(normed, mamba_in[:, 0]))
    xin = low_back(exact(normed, mamba_in[:, 1]))
    bc = low_back(exact(normed, mamba_bc))
    dtr = low_back(exact(normed, mamba_dt))
    gated = mixer_core(gate_part, xin, bc, dtr, seg, conv_x, conv_bc, dt_bias, a_log, d_skip)
    gnormed = low(gated * lax.rsqrt(lax.optimization_barrier(jnp.mean(gated * gated, axis=-1, keepdims=True)) + 1e-05) * gate_gain)
    resid = resid + low_back(exact(gnormed, mamba_out))
    normed = low(rms_apply(resid, norm2_gain))
    query = low(low_back(exact(normed, attn_qkv[:, 0])))
    keys = low(low_back(exact(normed, attn_qkv[:, 1])))
    vals = low(low_back(exact(normed, attn_qkv[:, 2])))
    attended = low(attend_rows(query, keys, vals, seg))
    resid = resid + low_back(exact(attended, attn_out))
    normed = low(rms_apply(resid, norm3_gain))
    gate = low_back(exact(normed, ffn_in[:, 0]))
    upper = low_back(exact(normed, ffn_in[:, 1]))
    hidden = low(jax.nn.silu(gate) * upper)
    return resid + low_back(exact(hidden, ffn_out))

def reference(byte_ids, segment_ids, embed_table, patch_weight, norm1_gain, mamba_in, mamba_dt, mamba_bc, conv_x, conv_bc, dt_bias, a_log, d_skip, gate_gain, mamba_out, norm2_gain, attn_qkv, attn_out, norm3_gain, ffn_in, ffn_out, d_out):
    params = tuple((item.astype(jnp.float32) for item in (embed_table, patch_weight, norm1_gain, mamba_in, mamba_dt, mamba_bc, conv_x, conv_bc, dt_bias, a_log, d_skip, gate_gain, mamba_out, norm2_gain, attn_qkv, attn_out, norm3_gain, ffn_in, ffn_out)))
    id_rows = byte_ids.reshape(-1, LEN, PATCH)
    seg_rows = segment_ids.reshape(-1, LEN)

    def forward(weights):

        def one_row(items):
            return layer_rows(weights, items[0], items[1])
        result = lax.map(jax.checkpoint(one_row), (id_rows, seg_rows))
        return result.reshape(byte_ids.shape[0], byte_ids.shape[1], D)
    mixed, pull = jax.vjp(forward, params)
    grads = pull(d_out.astype(jnp.float32))[0]
    return (mixed, grads[0], grads[1], grads[2], grads[3], grads[4], grads[5], grads[6], grads[7], grads[8], grads[9], grads[10], grads[11], grads[12], grads[13], grads[14], grads[15], grads[16], grads[17], grads[18])
```

```python
import jax
import jax.numpy as jnp
from jax import lax
from jax.experimental import pallas as pl
from jax.experimental.pallas import tpu as pltpu
from jax.sharding import PartitionSpec as P

PATCH = 8
VOCAB = 256
HD = 64
MB = 2
DIN = 2048
PM = 64
TAPS = 4
VMEM_LIMIT = 56 * 1024 * 1024
LOG2E = 1.4426950408889634
BLK = 256


def dot_nn(a, b):
    return lax.dot_general(a, b, (((1,), (0,)), ((), ())), preferred_element_type=jnp.float32)


def dot_nt(a, b):
    return lax.dot_general(a, b, (((1,), (1,)), ((), ())), preferred_element_type=jnp.float32)


def dot_tn(a, b):
    return lax.dot_general(a, b, (((0,), (0,)), ((), ())), preferred_element_type=jnp.float32)


def sigmoid(v):
    return 0.5 * jnp.tanh(0.5 * v) + 0.5


def head_masks(width, size):
    lane = lax.broadcasted_iota(jnp.int32, (1, width), 1) // size
    return [lane == h for h in range(width // size)]


def spread_heads(cols, first, masks, width):
    rows = cols.shape[0]
    out = jnp.broadcast_to(cols[:, first : first + 1], (rows, width))
    for h in range(1, len(masks)):
        piece = jnp.broadcast_to(cols[:, first + h : first + h + 1], (rows, width))
        out = jnp.where(masks[h], piece, out)
    return out


def two_parts(v):
    upper = v.astype(jnp.bfloat16)
    return upper, (v - upper.astype(jnp.float32)).astype(jnp.bfloat16)


def attn_fwd_kernel(q_ref, k_ref, v_ref, pos_ref, o_ref, lse_ref, bias_ref):
    length = pos_ref.shape[0]
    width = q_ref.shape[2]

    @pl.when(pl.program_id(0) == 0)
    def _():
        for i in range(length // BLK):
            rows = pl.ds(i * BLK, BLK)
            n = (i + 1) * BLK
            spot = i * BLK + lax.broadcasted_iota(jnp.int32, (BLK, n), 0)
            other = lax.broadcasted_iota(jnp.int32, (BLK, n), 1)
            gap = (spot - other).astype(jnp.float32)
            keep = (gap >= 0.0) & (gap <= pos_ref[rows, 0:1])
            bias_ref[rows, 0:n] = jnp.where(keep, 0.0, -1e30)

    masks = head_masks(width, HD)
    spots = lax.broadcasted_iota(jnp.int32, (1, 128), 1)
    for i in range(length // BLK):
        rows = pl.ds(i * BLK, BLK)
        n = (i + 1) * BLK
        query = q_ref[0, rows, :] * jnp.bfloat16(HD**-0.5)
        keys = k_ref[0, 0:n, :]
        vals = v_ref[0, 0:n, :]
        bias = bias_ref[rows, 0:n]
        total = jnp.zeros((BLK, width), jnp.float32)
        logs = jnp.zeros((BLK, 128), jnp.float32)
        for h, mask in enumerate(masks):
            scores = dot_nt(jnp.where(mask, query, jnp.bfloat16(0)), keys) + bias
            top = jnp.max(scores, axis=1, keepdims=True)
            weights = jnp.exp(scores - top)
            norm = jnp.sum(weights, axis=1, keepdims=True)
            probs = (weights * (1.0 / norm)).astype(jnp.bfloat16)
            total = jnp.where(mask, dot_nn(probs, vals), total)
            logs = jnp.where(spots == h, top + jnp.log(norm), logs)
        o_ref[0, rows, :] = total.astype(jnp.bfloat16)
        lse_ref[0, rows, :] = logs


def attn_forward(qkv, posb):
    parts, length, width3 = qkv.shape
    width = width3 // 3
    lanes = min(256, width)
    per = width // lanes
    groups = parts * per
    block = (1, length, lanes)
    return pl.pallas_call(
        attn_fwd_kernel,
        grid=(groups,),
        in_specs=[
            pl.BlockSpec(block, lambda g: (g // per, 0, g % per)),
            pl.BlockSpec(block, lambda g: (g // per, 0, per + g % per)),
            pl.BlockSpec(block, lambda g: (g // per, 0, 2 * per + g % per)),
            pl.BlockSpec((length, 128), lambda g: (0, 0)),
        ],
        out_specs=[
            pl.BlockSpec(block, lambda g: (g // per, 0, g % per)),
            pl.BlockSpec((1, length, 128), lambda g: (g, 0, 0)),
        ],
        out_shape=[
            jax.ShapeDtypeStruct((parts, length, width), jnp.bfloat16),
            jax.ShapeDtypeStruct((groups, length, 128), jnp.float32),
        ],
        scratch_shapes=[pltpu.VMEM((length, length), jnp.float32)],
        compiler_params=pltpu.CompilerParams(vmem_limit_bytes=VMEM_LIMIT),
        cost_estimate=pl.CostEstimate(
            flops=30_000_000_000, bytes_accessed=10_000_000, transcendentals=0
        ),
        name="attn_fwd",
    )(qkv, qkv, qkv, posb)


def attn_bwd_kernel(
    q_ref, k_ref, v_ref, o_ref, do_ref, lse_ref, rem_ref, *others
):
    out_ref, bias_ref, dk_ref, dv_ref = others[-4:]
    length = rem_ref.shape[0]
    width = q_ref.shape[2]
    per = out_ref.shape[2] // (3 * width)
    step = pl.program_id(0)

    @pl.when(step == 0)
    def _():
        for i in range(length // BLK):
            cols = pl.ds(i * BLK, BLK)
            n = (i + 1) * BLK
            other = lax.broadcasted_iota(jnp.int32, (n, BLK), 0)
            spot = i * BLK + lax.broadcasted_iota(jnp.int32, (n, BLK), 1)
            gap = (spot - other).astype(jnp.float32)
            keep = (gap >= 0.0) & (gap <= rem_ref[0:n, 0:1])
            bias_ref[0:n, cols] = jnp.where(keep, 0.0, -1e30)

    masks = head_masks(width, HD)
    heads = len(masks)
    rows8 = lax.broadcasted_iota(jnp.int32, (8, width), 0)
    lane8 = lax.broadcasted_iota(jnp.int32, (8, width), 1) // HD
    picks = jnp.where(rows8 == lane8, 1.0, 0.0).astype(jnp.bfloat16)
    scale = jnp.bfloat16(HD**-0.5)
    zero = jnp.bfloat16(0)
    offset = pl.multiple_of((step % per) * width, width)
    nblocks = length // BLK
    for i in reversed(range(nblocks)):
        rows = pl.ds(i * BLK, BLK)
        n = (i + 1) * BLK
        query = q_ref[0, rows, :] * scale
        grad = do_ref[0, rows, :]
        prod = grad.astype(jnp.float32) * o_ref[0, rows, :].astype(jnp.float32)
        upper, lower = two_parts(prod)
        delta = dot_nt(picks, upper) + dot_nt(picks, lower)
        keys = k_ref[0, 0:n, :]
        vals = v_ref[0, 0:n, :]
        bias = bias_ref[0:n, rows]
        d_query = jnp.zeros((BLK, width), jnp.float32)
        d_keys = jnp.zeros((n, width), jnp.float32)
        d_vals = jnp.zeros((n, width), jnp.float32)
        for h, mask in enumerate(masks):
            q_head = jnp.where(mask, query, zero)
            g_head = jnp.where(mask, grad, zero)
            probs = jnp.exp(dot_nt(keys, q_head) + bias - lse_ref[0, h : h + 1, rows])
            d_probs = dot_nt(vals, g_head)
            d_scores = (probs * (d_probs - delta[h : h + 1, :])).astype(jnp.bfloat16)
            d_vals = d_vals + dot_nn(probs.astype(jnp.bfloat16), g_head)
            d_keys = d_keys + dot_nn(d_scores, q_head)
            d_query = jnp.where(mask, dot_tn(d_scores, keys), d_query)
        out_ref[0, rows, pl.ds(offset, width)] = (d_query * (HD**-0.5)).astype(jnp.bfloat16)
        if i == nblocks - 1:
            dk_ref[...] = d_keys
            dv_ref[...] = d_vals
        else:
            dk_ref[0:n, :] += d_keys
            dv_ref[0:n, :] += d_vals
    out_ref[0, :, pl.ds(per * width + offset, width)] = dk_ref[...].astype(jnp.bfloat16)
    out_ref[0, :, pl.ds(2 * per * width + offset, width)] = dv_ref[...].astype(jnp.bfloat16)


def attn_backward(qkv, attended, d_att, lse_rows, remb, deps):
    parts, length, width3 = qkv.shape
    width = width3 // 3
    lanes = min(256, width)
    per = width // lanes
    groups = parts * per
    block = (1, length, lanes)
    return pl.pallas_call(
        attn_bwd_kernel,
        grid=(groups,),
        in_specs=[
            pl.BlockSpec(block, lambda g: (g // per, 0, g % per)),
            pl.BlockSpec(block, lambda g: (g // per, 0, per + g % per)),
            pl.BlockSpec(block, lambda g: (g // per, 0, 2 * per + g % per)),
            pl.BlockSpec(block, lambda g: (g // per, 0, g % per)),
            pl.BlockSpec(block, lambda g: (g // per, 0, g % per)),
            pl.BlockSpec((1, 8, length), lambda g: (g, 0, 0)),
            pl.BlockSpec((length, 128), lambda g: (0, 0)),
        ]
        + [pl.BlockSpec(memory_space=pl.ANY)] * len(deps),
        out_specs=pl.BlockSpec((1, length, width3), lambda g: (g // per, 0, 0)),
        out_shape=jax.ShapeDtypeStruct(qkv.shape, jnp.bfloat16),
        scratch_shapes=[
            pltpu.VMEM((length, length), jnp.float32),
            pltpu.VMEM((length, lanes), jnp.float32),
            pltpu.VMEM((length, lanes), jnp.float32),
        ],
        compiler_params=pltpu.CompilerParams(vmem_limit_bytes=VMEM_LIMIT),
        cost_estimate=pl.CostEstimate(
            flops=70_000_000_000, bytes_accessed=20_000_000, transcendentals=0
        ),
        name="attn_bwd",
    )(qkv, qkv, qkv, attended, d_att, lse_rows, remb, *deps)


def conv_moved(ref, part, rows, first, pos):
    width = ref.shape[2]
    if first == 0:
        before = jnp.zeros((8, width), jnp.float32)
    else:
        before = ref[part, pl.ds(first - 8, 8), :]
    signal = jnp.concatenate([before, ref[part, pl.ds(first, rows), :]], axis=0)
    moved = [signal[8:]]
    for lag in range(1, TAPS):
        shifted = pltpu.roll(signal, lag, 0)[8:]
        moved.append(jnp.where(pos >= lag, shifted, 0.0))
    return moved


def wide_rows(ref, first, rows, width):
    block = ref[pl.ds(first, rows), :]
    return jnp.concatenate([block] * (width // block.shape[1]), axis=1)


def mix_fwd_kernel(
    z_ref, x_ref, cols_ref, cumt_ref, conv_ref, skip_ref, pos_ref, bs_ref, cs_ref, bst_ref,
    ssm_ref, state_ref, ssq_ref, inner_ref,
):
    length = pos_ref.shape[0]
    width = x_ref.shape[2]
    step = pl.program_id(0)
    chunks = length // BLK

    @pl.when(step == 0)
    def _():
        for k in range(chunks):
            rows = pl.ds(k * BLK, BLK)
            spot = lax.broadcasted_iota(jnp.int32, (BLK, BLK), 0)
            other = lax.broadcasted_iota(jnp.int32, (BLK, BLK), 1)
            gap = (spot - other).astype(jnp.float32)
            keep = (gap >= 0.0) & (gap <= pos_ref[rows, 0:1])
            inner_ref[k] = jnp.where(keep, dot_nt(cs_ref[rows, :], bs_ref[rows, :]), 0.0)

    masks = head_masks(width, PM)
    heads = len(masks)
    span = cols_ref.shape[1] // 4
    turn = lax.rem(4 * span - step * heads, 4 * span)
    state = jnp.zeros((bs_ref.shape[1], width), jnp.float32)
    for k in range(chunks):
        first = k * BLK
        rows = pl.ds(first, BLK)
        pos = wide_rows(pos_ref, first, BLK, width)
        moved = conv_moved(x_ref, 0, BLK, first, pos)
        pre = conv_ref[TAPS - 1 : TAPS, :] * moved[0]
        for lag in range(1, TAPS):
            pre = pre + conv_ref[TAPS - 1 - lag : TAPS - lag, :] * moved[lag]
        xs = pre * sigmoid(pre)
        cols = pltpu.roll(cols_ref[rows, :], turn, 1)
        driven = (spread_heads(cols, 0, masks, width) * xs).astype(jnp.bfloat16)
        out = skip_ref[...] * xs
        inner = inner_ref[k]
        for h, mask in enumerate(masks):
            gap = cols[:, span + h : span + h + 1] - cumt_ref[0, h : h + 1, rows]
            mixing = (jnp.exp2(jnp.minimum(gap, 0.0)) * inner).astype(jnp.bfloat16)
            out = out + dot_nn(mixing, jnp.where(mask, driven, jnp.bfloat16(0)))
        state_bf, state_rest = two_parts(state)
        state_ref[k] = state_bf
        if k > 0:
            carry = spread_heads(cols, 2 * span, masks, width)
            recalled = dot_nn(cs_ref[rows, :], state_bf) + dot_nn(cs_ref[rows, :], state_rest)
            out = out + carry * recalled
        if k < chunks - 1:
            last = spread_heads(cols, 3 * span, masks, width)
            fed, fed_rest = two_parts(last * driven.astype(jnp.float32))
            fresh = dot_nn(bst_ref[:, rows], fed) + dot_nn(bst_ref[:, rows], fed_rest)
            if k > 0:
                fresh = fresh + carry[BLK - 1 : BLK, :] * state
            state = fresh
        ssm_ref[0, rows, :] = out
        gate = z_ref[0, rows, :]
        gated = out * gate * sigmoid(gate)
        square = gated * gated
        total = square[:, 0:128]
        for lane in range(128, width, 128):
            total = total + square[:, lane : lane + 128]

        @pl.when(step == 0)
        def _():
            ssq_ref[rows, :] = total

        @pl.when(step > 0)
        def _():
            ssq_ref[rows, :] += total


def mix_forward(z, x, cols, cumt, conv, skip, posb, bs, cs, bst):
    parts, length, inner_width = z.shape
    state = bs.shape[1]
    lanes = 256
    per = inner_width // lanes
    groups = parts * per
    block = (1, length, lanes)
    whole = lambda g: (0, 0)
    return pl.pallas_call(
        mix_fwd_kernel,
        grid=(groups,),
        in_specs=[
            pl.BlockSpec(block, lambda g: (g // per, 0, g % per)),
            pl.BlockSpec(block, lambda g: (g // per, 0, g % per)),
            pl.BlockSpec(cols.shape, whole),
            pl.BlockSpec((1,) + cumt.shape[1:], lambda g: (g, 0, 0)),
            pl.BlockSpec((TAPS, lanes), lambda g: (0, g)),
            pl.BlockSpec((1, lanes), lambda g: (0, g)),
            pl.BlockSpec((length, 128), whole),
            pl.BlockSpec((length, state), whole),
            pl.BlockSpec((length, state), whole),
            pl.BlockSpec((state, length), whole),
        ],
        out_specs=[
            pl.BlockSpec(block, lambda g: (g // per, 0, g % per)),
            pl.BlockSpec((length // BLK, state, lanes), lambda g: (0, 0, g)),
            pl.BlockSpec((length, 128), whole),
        ],
        out_shape=[
            jax.ShapeDtypeStruct((parts, length, inner_width), jnp.float32),
            jax.ShapeDtypeStruct((length // BLK, state, parts * inner_width), jnp.bfloat16),
            jax.ShapeDtypeStruct((length, 128), jnp.float32),
        ],
        scratch_shapes=[pltpu.VMEM((length // BLK, BLK, BLK), jnp.float32)],
        compiler_params=pltpu.CompilerParams(vmem_limit_bytes=VMEM_LIMIT),
        cost_estimate=pl.CostEstimate(
            flops=20_000_000_000, bytes_accessed=30_000_000, transcendentals=0
        ),
        name="mix_fwd",
    )(z, x, cols, cumt, conv, skip, posb, bs, cs, bst)


def mix_bwd_kernel(
    z_ref, x_ref, ssm_ref, dgn_ref, cols_ref, cumt_ref, conv_ref, skip_ref, gain_ref,
    pos_ref, rem_ref, rg_ref, cross_ref, bs_ref, cs_ref, cst_ref, state_ref, *others,
):
    dz_ref, dx_ref, dcols_ref, sums_ref, dbs_ref, dcs_ref = others[-9:-3]
    inner_ref, dinner_ref, dpre_ref = others[-3:]
    length = pos_ref.shape[0]
    width = x_ref.shape[2]
    step = pl.program_id(0)
    chunks = length // BLK
    spot = lax.broadcasted_iota(jnp.int32, (BLK, BLK), 1)
    other = lax.broadcasted_iota(jnp.int32, (BLK, BLK), 0)
    gap = (spot - other).astype(jnp.float32)

    @pl.when(step == 0)
    def _():
        for k in range(chunks):
            rows = pl.ds(k * BLK, BLK)
            keep = (gap >= 0.0) & (gap <= rem_ref[rows, 0:1])
            inner_ref[k] = jnp.where(keep, dot_nt(bs_ref[rows, :], cs_ref[rows, :]), 0.0)
        dinner_ref[...] = jnp.zeros(dinner_ref.shape, jnp.float32)
        dbs_ref[...] = jnp.zeros(dbs_ref.shape, jnp.float32)
        dcs_ref[...] = jnp.zeros(dcs_ref.shape, jnp.float32)
        dcols_ref[...] = jnp.zeros(dcols_ref.shape, jnp.float32)

    masks = head_masks(width, PM)
    heads = len(masks)
    zero = jnp.bfloat16(0)
    head_of = lax.broadcasted_iota(jnp.int32, (width, 128), 0) // PM
    lane_of = lax.broadcasted_iota(jnp.int32, (width, 128), 1)
    span = cols_ref.shape[1] // 4
    turn = lax.rem(4 * span - step * heads, 4 * span)
    lane_of = lane_of - step * heads
    pick_cum = jnp.where(head_of == lane_of, 1.0, 0.0).astype(jnp.bfloat16)
    pick_step = jnp.where(head_of + span == lane_of, 1.0, 0.0).astype(jnp.bfloat16)
    dpre_ref[pl.ds(length, 8), :] = jnp.zeros((8, width), jnp.float32)
    sums_ref[...] = jnp.zeros(sums_ref.shape, jnp.float32)
    d_state = jnp.zeros((bs_ref.shape[1], width), jnp.float32)
    skip = skip_ref[...]
    gain = gain_ref[...]
    for k in reversed(range(chunks)):
        first = k * BLK
        rows = pl.ds(first, BLK)
        pos = wide_rows(pos_ref, first, BLK, width)
        moved = conv_moved(x_ref, 0, BLK, first, pos)
        pre = conv_ref[TAPS - 1 : TAPS, :] * moved[0]
        for lag in range(1, TAPS):
            pre = pre + conv_ref[TAPS - 1 - lag : TAPS - lag, :] * moved[lag]
        sig = sigmoid(pre)
        xs = pre * sig
        cols = pltpu.roll(cols_ref[rows, :], turn, 1)
        step_wide = spread_heads(cols, 0, masks, width)
        driven = (step_wide * xs).astype(jnp.bfloat16)
        gate = z_ref[0, rows, :]
        sig_z = sigmoid(gate)
        silu_z = gate * sig_z
        ssm = ssm_ref[0, rows, :]
        gated = ssm * silu_z
        d_gn = dgn_ref[0, rows, :]
        rg = wide_rows(rg_ref, first, BLK, width)
        cross = wide_rows(cross_ref, first, BLK, width)
        scaled = rg * d_gn
        d_gated = gain * scaled - gated * cross
        sums_ref[5:6, :] += jnp.sum(gated * scaled, axis=0, keepdims=True)
        dz_ref[0, rows, :] = (d_gated * ssm * (sig_z + silu_z * (1.0 - sig_z))).astype(jnp.bfloat16)
        d_out = d_gated * silu_z
        d_low = d_out.astype(jnp.bfloat16)
        sums_ref[4:5, :] += jnp.sum(d_out * xs, axis=0, keepdims=True)
        inner = inner_ref[k]
        d_inner = dinner_ref[k]
        d_driven = jnp.zeros((BLK, width), jnp.float32)
        for h, mask in enumerate(masks):
            gap_h = cumt_ref[0, h : h + 1, rows] - cols[:, span + h : span + h + 1]
            decay = jnp.exp2(jnp.minimum(gap_h, 0.0))
            mixing = (decay * inner).astype(jnp.bfloat16)
            d_driven = d_driven + dot_nn(mixing, jnp.where(mask, d_low, zero))
            d_inner = d_inner + decay * dot_nt(jnp.where(mask, driven, zero), d_low)
        dinner_ref[k] = d_inner
        if k > 0:
            carry = spread_heads(cols, 2 * span, masks, width)
            carried, carried_rest = two_parts(carry * d_low.astype(jnp.float32))
            dcs_ref[rows, :] += dot_nt(carried, state_ref[k])
        if k < chunks - 1:
            last = spread_heads(cols, 3 * span, masks, width)
            fed = (last * driven.astype(jnp.float32)).astype(jnp.bfloat16)
            d_state_bf, d_state_rest = two_parts(d_state)
            dbs_ref[rows, :] += dot_nt(fed, d_state_bf)
            recalled = dot_nn(bs_ref[rows, :], d_state_bf) + dot_nn(bs_ref[rows, :], d_state_rest)
            d_driven = d_driven + last * recalled
        if k > 0:
            fresh = dot_nn(cst_ref[:, rows], carried) + dot_nn(cst_ref[:, rows], carried_rest)
            if k < chunks - 1:
                fresh = fresh + carry[BLK - 1 : BLK, :] * d_state
            d_state = fresh
        moved_out = ssm - skip * xs
        balance = d_low.astype(jnp.float32) * moved_out - driven.astype(jnp.float32) * d_driven
        upper, lower = two_parts(balance)
        d_cum = dot_nn(upper, pick_cum) + dot_nn(lower, pick_cum)
        d_driven = d_driven.astype(jnp.bfloat16).astype(jnp.float32)
        upper, lower = two_parts(d_driven * xs)
        dcols_ref[rows, :] += d_cum + dot_nn(upper, pick_step) + dot_nn(lower, pick_step)
        d_xs = skip * d_out + step_wide * d_driven
        d_pre = d_xs * (sig + xs * (1.0 - sig))
        dpre_ref[rows, :] = d_pre
        for lag in range(TAPS):
            sums_ref[TAPS - 1 - lag : TAPS - lag, :] += jnp.sum(
                d_pre * moved[lag], axis=0, keepdims=True
            )
        after = jnp.concatenate([d_pre, dpre_ref[pl.ds(first + BLK, 8), :]], axis=0)
        rem = wide_rows(rem_ref, first, BLK, width)
        d_x = conv_ref[TAPS - 1 : TAPS, :] * d_pre
        for lag in range(1, TAPS):
            shifted = pltpu.roll(after, BLK + 8 - lag, 0)[0:BLK]
            d_x = d_x + conv_ref[TAPS - 1 - lag : TAPS - lag, :] * jnp.where(
                rem >= lag, shifted, 0.0
            )
        dx_ref[0, rows, :] = d_x.astype(jnp.bfloat16)

    @pl.when(step == pl.num_programs(0) - 1)
    def _():
        for k in range(chunks):
            rows = pl.ds(k * BLK, BLK)
            keep = (gap >= 0.0) & (gap <= rem_ref[rows, 0:1])
            d_inner = jnp.where(keep, dinner_ref[k], 0.0)
            dbs_ref[rows, :] += dot_nn(d_inner.astype(jnp.bfloat16), cs_ref[rows, :])
            dcs_ref[rows, :] += dot_nn(d_inner.T.astype(jnp.bfloat16), bs_ref[rows, :])


def mix_backward(
    z, x, ssm, d_gn, cols, cumt, conv, skip, gain, posb, remb, rgb, crossb, bs, cs, cst, states, deps
):
    parts, length, inner_width = ssm.shape
    state = bs.shape[1]
    lanes = 256
    per = inner_width // lanes
    groups = parts * per
    block = (1, length, lanes)
    whole = lambda g: (0, 0)
    own = lambda g: (g // per, 0, g % per)
    return pl.pallas_call(
        mix_bwd_kernel,
        grid=(groups,),
        in_specs=[
            pl.BlockSpec(block, own),
            pl.BlockSpec(block, own),
            pl.BlockSpec(block, own),
            pl.BlockSpec(block, own),
            pl.BlockSpec(cols.shape, whole),
            pl.BlockSpec((1,) + cumt.shape[1:], lambda g: (g, 0, 0)),
            pl.BlockSpec((TAPS, lanes), lambda g: (0, g)),
            pl.BlockSpec((1, lanes), lambda g: (0, g)),
            pl.BlockSpec((1, lanes), lambda g: (0, g)),
            pl.BlockSpec((length, 128), whole),
            pl.BlockSpec((length, 128), whole),
            pl.BlockSpec((length, 128), whole),
            pl.BlockSpec((length, 128), whole),
            pl.BlockSpec((length, state), whole),
            pl.BlockSpec((length, state), whole),
            pl.BlockSpec((state, length), whole),
            pl.BlockSpec((length // BLK, state, lanes), lambda g: (0, 0, g)),
        ]
        + [pl.BlockSpec(memory_space=pl.ANY)] * len(deps),
        out_specs=[
            pl.BlockSpec(block, own),
            pl.BlockSpec(block, own),
            pl.BlockSpec((length, 128), whole),
            pl.BlockSpec((8, lanes), lambda g: (0, g)),
            pl.BlockSpec((length, state), whole),
            pl.BlockSpec((length, state), whole),
        ],
        out_shape=[
            jax.ShapeDtypeStruct((parts, length, inner_width), jnp.bfloat16),
            jax.ShapeDtypeStruct(x.shape, jnp.bfloat16),
            jax.ShapeDtypeStruct((length, 128), jnp.float32),
            jax.ShapeDtypeStruct((8, parts * inner_width), jnp.float32),
            jax.ShapeDtypeStruct((length, state), jnp.float32),
            jax.ShapeDtypeStruct((length, state), jnp.float32),
        ],
        scratch_shapes=[
            pltpu.VMEM((length // BLK, BLK, BLK), jnp.float32),
            pltpu.VMEM((length // BLK, BLK, BLK), jnp.float32),
            pltpu.VMEM((length + 8, lanes), jnp.float32),
        ],
        compiler_params=pltpu.CompilerParams(vmem_limit_bytes=VMEM_LIMIT),
        cost_estimate=pl.CostEstimate(
            flops=50_000_000_000, bytes_accessed=50_000_000, transcendentals=0
        ),
        name="mix_bwd",
    )(
        z, x, ssm, d_gn, cols, cumt, conv, skip, gain, posb, remb, rgb, crossb, bs, cs, cst,
        states, *deps,
    )


def tile_of(columns, limit=512):
    size = limit
    while columns % size:
        size -= 128
    return size


def part_product(
    left, right, dtype, first=0, columns=None, extra=None, deps=(), fold=1, into=None, place=0, room=None
):
    parts, depth, whole = right.shape
    rows = left.shape[0]
    columns = whole - first if columns is None else columns
    tile = tile_of(columns)
    while first % tile or place % tile:
        tile = tile_of(columns, tile - 128)
    begin = first // tile
    count = columns // tile
    block = (1, rows, tile)
    shift = place // tile
    room = fold * columns if room is None else room
    in_specs = [
        pl.BlockSpec((rows, depth), lambda m, n: (0, 0)),
        pl.BlockSpec((1, depth, tile), lambda m, n: (m, 0, begin + n)),
    ]
    operands = [left, right]
    if extra is not None:
        in_specs.append(pl.BlockSpec(block, lambda m, n: (m, 0, n)))
        operands.append(extra)
    aliases = {}
    if into is not None:
        aliases = {len(operands): 0}
        deps = (into,) + tuple(deps)
        room = into.shape[2]
    in_specs += [pl.BlockSpec(memory_space=pl.ANY)] * len(deps)

    def body(left_ref, right_ref, *others):
        total = dot_nn(left_ref[...], right_ref[0])
        if extra is not None:
            total = total + others[0][0].astype(jnp.float32)
        others[-1][0] = total.astype(dtype)

    return pl.pallas_call(
        body,
        grid=(parts, count),
        in_specs=in_specs,
        out_specs=pl.BlockSpec(
            block, lambda m, n: (m // fold, 0, shift + (m % fold) * count + n)
        ),
        out_shape=jax.ShapeDtypeStruct((parts // fold, rows, room), dtype),
        input_output_aliases=aliases,
        compiler_params=pltpu.CompilerParams(vmem_limit_bytes=VMEM_LIMIT),
        cost_estimate=pl.CostEstimate(
            flops=2 * parts * rows * depth * columns,
            bytes_accessed=parts * depth * columns * 2 + parts * rows * columns * 4,
            transcendentals=0,
        ),
        name="part_product",
    )(*operands, *deps)


def part_back(left, right, first=0, start=None, deps=()):
    parts, rows, columns = left.shape
    width = right.shape[1]
    fold = parts // right.shape[0]
    tile = tile_of(columns)
    while first % tile:
        tile = tile_of(columns, tile - 128)
    begin = first // tile
    count = columns // tile
    in_specs = [
        pl.BlockSpec((1, rows, tile), lambda m, n: (m, 0, n)),
        pl.BlockSpec(
            (1, width, tile), lambda m, n: (m // fold, 0, begin + (m % fold) * count + n)
        ),
    ]
    operands = [left, right]
    if start is not None:
        in_specs.append(pl.BlockSpec((rows, width), lambda m, n: (0, 0)))
        operands.append(start)
    in_specs += [pl.BlockSpec(memory_space=pl.ANY)] * len(deps)

    def body(left_ref, right_ref, *others):
        out_ref = others[-1]
        total = dot_nt(left_ref[0], right_ref[0])
        opening = (pl.program_id(0) == 0) & (pl.program_id(1) == 0)

        @pl.when(opening)
        def _():
            out_ref[...] = total if start is None else total + others[0][...]

        @pl.when(jnp.logical_not(opening))
        def _():
            out_ref[...] += total

    return pl.pallas_call(
        body,
        grid=(parts, count),
        in_specs=in_specs,
        out_specs=pl.BlockSpec((rows, width), lambda m, n: (0, 0)),
        out_shape=jax.ShapeDtypeStruct((rows, width), jnp.float32),
        compiler_params=pltpu.CompilerParams(vmem_limit_bytes=VMEM_LIMIT),
        cost_estimate=pl.CostEstimate(
            flops=2 * parts * rows * columns * width,
            bytes_accessed=2 * parts * columns * (rows + width) + 4 * rows * width,
            transcendentals=0,
        ),
        name="part_back",
    )(*operands, *deps)


def outer_kernel(left_ref, right_ref, out_ref):
    total = dot_tn(left_ref[0], right_ref[...]).astype(jnp.bfloat16)
    rows = out_ref.shape[1]
    width = right_ref.shape[1]
    wraps = total.shape[0] // rows
    piece = 64
    for i in range(rows // piece):
        for w in range(wraps):
            begin = (i * wraps + w) * piece
            out_ref[0, pl.ds(i * piece, piece), pl.ds(w * width, width)] = total[
                begin : begin + piece
            ]


def outer_into(left, right, wraps, place, room):
    parts, length, columns = left.shape
    width = right.shape[1]
    tile = 256 * wraps
    begin = place // (wraps * width)
    return pl.pallas_call(
        outer_kernel,
        grid=(parts, columns // tile),
        in_specs=[
            pl.BlockSpec((1, length, tile), lambda m, n: (m, 0, n)),
            pl.BlockSpec((length, width), lambda m, n: (0, 0)),
        ],
        out_specs=pl.BlockSpec((1, tile // wraps, wraps * width), lambda m, n: (m, n, begin)),
        out_shape=jax.ShapeDtypeStruct((parts, columns // wraps, room), jnp.bfloat16),
        compiler_params=pltpu.CompilerParams(vmem_limit_bytes=VMEM_LIMIT),
        cost_estimate=pl.CostEstimate(
            flops=2 * parts * length * columns * width,
            bytes_accessed=2 * parts * columns * (length + width),
            transcendentals=0,
        ),
        name="outer_into",
    )(left, right)


def unfold_kernel(in_ref, out_ref):
    count = out_ref.shape[1]
    width = out_ref.shape[2]
    for j in range(count):
        out_ref[:, j, :] = in_ref[:, j * width : (j + 1) * width].astype(jnp.float32)


def unfold(value, count, width):
    rows = value.shape[0]
    step = 128
    return pl.pallas_call(
        unfold_kernel,
        grid=(rows // step,),
        in_specs=[pl.BlockSpec((step, count * width), lambda n: (n, 0))],
        out_specs=pl.BlockSpec((step, count, width), lambda n: (n, 0, 0)),
        out_shape=jax.ShapeDtypeStruct((rows, count, width), jnp.float32),
        compiler_params=pltpu.CompilerParams(vmem_limit_bytes=VMEM_LIMIT),
        cost_estimate=pl.CostEstimate(
            flops=0, bytes_accessed=6 * rows * count * width, transcendentals=0
        ),
        name="unfold",
    )(value)


def ffn_in_kernel(left_ref, gate_w_ref, up_w_ref, gate_ref, up_ref, hidden_ref):
    gate = dot_nn(left_ref[...], gate_w_ref[0])
    upper = dot_nn(left_ref[...], up_w_ref[0])
    gate_ref[0] = gate.astype(jnp.bfloat16)
    up_ref[0] = upper.astype(jnp.bfloat16)
    hidden_ref[0] = (gate * sigmoid(gate) * upper).astype(jnp.bfloat16)


def ffn_forward(left, right, half):
    parts, depth, _ = right.shape
    rows = left.shape[0]
    tile = tile_of(half)
    count = half // tile
    block = pl.BlockSpec((1, rows, tile), lambda m, n: (m, 0, n))
    shape = jax.ShapeDtypeStruct((parts, rows, half), jnp.bfloat16)
    return pl.pallas_call(
        ffn_in_kernel,
        grid=(parts, count),
        in_specs=[
            pl.BlockSpec((rows, depth), lambda m, n: (0, 0)),
            pl.BlockSpec((1, depth, tile), lambda m, n: (m, 0, n)),
            pl.BlockSpec((1, depth, tile), lambda m, n: (m, 0, count + n)),
        ],
        out_specs=[block, block, block],
        out_shape=[shape, shape, shape],
        compiler_params=pltpu.CompilerParams(vmem_limit_bytes=VMEM_LIMIT),
        cost_estimate=pl.CostEstimate(
            flops=4 * parts * rows * depth * half,
            bytes_accessed=parts * half * (4 * depth + 6 * rows),
            transcendentals=0,
        ),
        name="ffn_in",
    )(left, right, right)


def ffn_back_kernel(left_ref, right_ref, gate_ref, up_ref, out_ref):
    grad = dot_nn(left_ref[...], right_ref[0])
    gate = gate_ref[0].astype(jnp.float32)
    sig = sigmoid(gate)
    act = gate * sig
    slope = sig + act * (1.0 - sig)
    out_ref[0, 0] = (grad * up_ref[0].astype(jnp.float32) * slope).astype(jnp.bfloat16)
    out_ref[0, 1] = (grad * act).astype(jnp.bfloat16)


def ffn_backward(left, right, first, gate, upper):
    parts, rows, half = gate.shape
    depth = left.shape[1]
    tile = tile_of(half)
    begin = first // tile
    block = pl.BlockSpec((1, rows, tile), lambda m, n: (m, 0, n))
    return pl.pallas_call(
        ffn_back_kernel,
        grid=(parts, half // tile),
        in_specs=[
            pl.BlockSpec((rows, depth), lambda m, n: (0, 0)),
            pl.BlockSpec((1, depth, tile), lambda m, n: (m, 0, begin + n)),
            block,
            block,
        ],
        out_specs=pl.BlockSpec((1, 2, rows, tile), lambda m, n: (m, 0, 0, n)),
        out_shape=jax.ShapeDtypeStruct((parts, 2, rows, half), jnp.bfloat16),
        compiler_params=pltpu.CompilerParams(vmem_limit_bytes=VMEM_LIMIT),
        cost_estimate=pl.CostEstimate(
            flops=2 * parts * rows * depth * half,
            bytes_accessed=parts * half * (2 * depth + 8 * rows),
            transcendentals=0,
        ),
        name="ffn_back",
    )(left, right, gate, upper)


def bit_of(index, bit):
    return (index >> bit) & 1


def swap(value, stage):
    if stage is None:
        return lax.ppermute(value, "mp", [(0, 1), (1, 0)])
    count = lax.axis_size("dp")
    return lax.ppermute(value, "dp", [(i, i ^ (1 << stage)) for i in range(count)])


def my_bit(stage):
    if stage is None:
        return lax.axis_index("mp")
    return bit_of(lax.axis_index("dp"), stage)


def take_half(value, which):
    half = value.shape[0] // 2
    return lax.dynamic_slice_in_dim(value, which * half, half, 0)


def join(own, other, bit):
    first = jnp.where(bit == 0, own, other)
    second = jnp.where(bit == 0, other, own)
    return jnp.concatenate([first, second], axis=0)


def add_low(left, right):
    return (left.astype(jnp.float32) + right.astype(jnp.float32)).astype(jnp.bfloat16)


def dp_bits():
    return lax.axis_size("dp").bit_length() - 1


def ring_order():
    order = []
    layers = lax.axis_size("dp") // 4
    for side in range(2):
        for spot in range(layers):
            layer = spot if side == 0 else layers - 1 - spot
            for core in range(2):
                order.append(layer * 4 + side * 2 + core)
    return order


def block_of(device, bits):
    value = 0
    for bit in range(bits):
        value = value * 2 + ((device >> bit) & 1)
    return value


def sum_stages(total, order):
    for stage in order:
        mine = my_bit(stage)
        if stage is None:
            received = swap(lax.dynamic_index_in_dim(total, 1 - mine, 0, keepdims=False), None)
            kept = lax.dynamic_index_in_dim(total, mine, 0, keepdims=False)
        else:
            axis = total.ndim - 2
            half = total.shape[axis] // 2
            received = swap(
                lax.dynamic_slice_in_dim(total, (1 - mine) * half, half, axis), stage
            )
            kept = lax.dynamic_slice_in_dim(total, mine * half, half, axis)
        total = add_low(kept, received)
    return total


def x_first():
    return [None] + list(range(1, dp_bits()))


def y_first():
    return [1, None] + list(range(2, dp_bits()))


def gather_sum(piece, reversed_blocks=True):
    bits = dp_bits()
    order = ring_order()
    ringed = lax.all_gather(piece, "dp", axis=0, axis_index_groups=[order])
    blocks = [None] * len(order)
    for place, device in enumerate(order):
        blocks[block_of(device, bits) if reversed_blocks else device] = ringed[place]
    return jnp.concatenate(blocks, axis=0)


def around_order(part):
    layers = lax.axis_size("dp") // 4
    order = []
    for turn in range(2):
        side = turn if part == 0 else 1 - turn
        for spot in range(layers):
            layer = layers - 1 - spot if turn == 0 else spot
            for core in range(2):
                order.append((layer * 4 + side * 2 + core) * 2 + part)
    return order


def ring_scatter(value):
    order = around_order(0) + around_order(1)
    return lax.psum_scatter(
        value,
        ("dp", "mp"),
        scatter_dimension=0,
        tiled=True,
        axis_index_groups=[order],
    )


def ring_gather(piece):
    return lax.all_gather(
        piece,
        ("dp", "mp"),
        axis=0,
        tiled=True,
        axis_index_groups=[around_order(0), around_order(1)],
    )


def gather_steps(shard, order):
    bits = dp_bits()
    value = shard.reshape((1,) * (bits + 1) + shard.shape)
    for stage in order:
        axis = 0 if stage is None else bits - stage
        other = swap(value, stage)
        bit = my_bit(stage)
        value = jnp.concatenate(
            [jnp.where(bit == 0, value, other), jnp.where(bit == 0, other, value)], axis=axis
        )
    return value.reshape(2, -1, shard.shape[1])


def gather_y_last():
    return list(range(dp_bits() - 1, 1, -1)) + [None, 1, 0]


def gather_x_last():
    return list(range(dp_bits() - 1, 1, -1)) + [1, None, 0]


def spread_all(value):
    for stage in [0, 1, None] + list(range(2, dp_bits())):
        value = value + swap(value, stage)
    return value


def reduce_table(value):
    stages = [0, None] + list(range(1, dp_bits()))
    for stage in stages:
        mine = my_bit(stage)
        value = take_half(value, mine) + swap(take_half(value, 1 - mine), stage)
    for stage in reversed(stages):
        value = join(value, swap(value, stage), my_bit(stage))
    return value


def gather_small(shard):
    bits = dp_bits()
    value = shard[None]
    for bit in range(bits):
        value = join(value, swap(value, bit), my_bit(bit))
    return value.reshape((-1,) + shard.shape[1:])


def gather_weight(shard):
    return lax.all_gather(shard, ("mp", "dp"), axis=0, tiled=True).reshape(
        lax.axis_size("mp"), -1, shard.shape[1]
    )


def rms_back(hidden, gain, grad):
    inv = lax.rsqrt(jnp.mean(hidden * hidden, axis=-1, keepdims=True) + 1e-05)
    weighted = grad * gain
    mean = jnp.mean(hidden * weighted, axis=-1, keepdims=True)
    d_gain = jnp.sum(hidden * inv * grad, axis=0)
    return inv * weighted - hidden * (inv * inv * inv * mean), d_gain


def in_groups(per_head, groups):
    length = per_head.shape[0]
    return per_head.reshape(length, groups, -1).transpose(1, 0, 2)


def wide128(column):
    return jnp.broadcast_to(column, (column.shape[0], 128))


def dot_parts(left, right):
    return lax.dot_general(
        left, right, (((1,), (1,)), ((), ())), preferred_element_type=jnp.float32
    ).transpose(1, 0, 2)


def dot_back(left, right):
    total = dot_nt(left[0], right[0])
    for part in range(1, left.shape[0]):
        total = total + dot_nt(left[part], right[part])
    return total


def on_device_rows(
    byte_ids,
    segment_ids,
    embed_table,
    patch_weight,
    norm1_gain,
    mamba_in,
    mamba_dt,
    mamba_bc,
    conv_x,
    conv_bc,
    dt_bias,
    a_log,
    d_skip,
    gate_gain,
    mamba_out,
    norm2_gain,
    attn_qkv,
    attn_out,
    norm3_gain,
    ffn_in,
    ffn_out,
    d_out,
):
    low = jnp.bfloat16
    parts = lax.axis_size("mp")
    part = lax.axis_index("mp")
    shard = mamba_in.shape[0]
    per_pos = PATCH // parts
    inner_width = mamba_in.shape[2]
    heads_part = mamba_dt.shape[1]
    state = mamba_bc.shape[1] // 2
    lanes = 256
    groups = parts * inner_width // lanes

    def exchange(value):
        own = lax.dynamic_index_in_dim(value, part, 0, keepdims=False)
        other = swap(lax.dynamic_index_in_dim(value, 1 - part, 0, keepdims=False), None)
        return join(own, other, part)

    ids = exchange(byte_ids)
    seg = exchange(segment_ids)
    length = seg.shape[0]

    def both_parts(value):
        own = value
        other = swap(value, None)
        return join(own[None], other[None], part)

    conv_full = jnp.concatenate(list(both_parts(conv_x)), axis=1)
    vectors = both_parts(jnp.concatenate([dt_bias, a_log, d_skip, gate_gain]))
    heads = parts * heads_part
    bias_full, alog_full, skip_full = (
        vectors[:, i * heads_part : (i + 1) * heads_part].reshape(heads) for i in range(3)
    )
    ggain_full = vectors[:, 3 * heads_part :].reshape(parts * inner_width)

    bc_half = lax.dynamic_slice_in_dim(mamba_bc, part * state, state, 1)
    pad = (-heads_part) % 128
    shard_z = mamba_in[:, 0]
    shard_x = jnp.concatenate(
        [mamba_in[:, 1], bc_half, mamba_dt, jnp.zeros((shard, pad), low)], axis=1
    )
    shard_qkv = attn_qkv.reshape(shard, -1)
    shard_mid = jnp.concatenate([shard_qkv, mamba_out.T, attn_out.T], axis=1)
    shard_ffn = jnp.concatenate([ffn_in.reshape(shard, -1), ffn_out.T], axis=1)
    width_in = ffn_in.shape[1] * ffn_in.shape[2]

    table = gather_small(embed_table)
    rows_by_pos = patch_weight.reshape(per_pos, -1, patch_weight.shape[1])
    mapped = lax.dot_general(
        rows_by_pos, table, (((1,), (1,)), ((), ())), preferred_element_type=jnp.float32
    ).astype(low)
    mapped = mapped.transpose(1, 0, 2).reshape(rows_by_pos.shape[2], -1)
    mapped = gather_steps(mapped, gather_y_last())
    w_z = gather_steps(shard_z, gather_x_last())
    w_x = gather_steps(shard_x, gather_y_last())
    mapped_ready = mapped[0, 0, 0] * 0
    ready = (w_z[0, 0, 0] + w_x[0, 0, 0]) * 0 + mapped_ready
    w_mid = gather_weight(shard_mid + ready)
    w_ffn = gather_weight(shard_ffn + ready)
    width_qkv = shard_qkv.shape[1]

    onehot = (ids[:, :, None] == jnp.arange(VOCAB, dtype=jnp.int32)[None, None, :]).astype(low)
    onehot = onehot.reshape(length, parts, per_pos * VOCAB).transpose(1, 0, 2)
    resid0 = dot_back(onehot, mapped)

    spots = jnp.arange(length, dtype=jnp.int32)
    changed = jnp.concatenate([jnp.ones((1,), bool), seg[1:] != seg[:-1]])
    same = seg[:, None] == seg[None, :]
    pos = jnp.sum((same & (spots[None, :] < spots[:, None])).astype(jnp.int32), axis=1)
    rem = jnp.sum((same & (spots[None, :] > spots[:, None])).astype(jnp.int32), axis=1)
    posb = wide128(pos.astype(jnp.float32)[:, None])
    remb = wide128(rem.astype(jnp.float32)[:, None])

    u1 = rms_apply(resid0, norm1_gain).astype(low)
    gate = part_product(u1, w_z, jnp.float32)
    fed = part_product(u1, w_x, jnp.float32)
    first_dt = inner_width + state
    bc = jnp.concatenate([fed[p, :, inner_width:first_dt] for p in range(parts)], axis=1)
    dtr = jnp.concatenate([fed[p, :, first_dt : first_dt + heads_part] for p in range(parts)], 1)
    bc_act, pull_bc = jax.vjp(
        lambda signal, taps: jax.nn.silu(conv_rows(signal, taps, seg)), bc, conv_bc
    )
    bcs = bc_act.astype(low)
    bs = bcs[:, :state]
    cs = bcs[:, state:]
    steps = jax.nn.softplus(dtr + bias_full)
    rate = -jnp.exp(alog_full)
    lower = (spots[:, None] >= spots[None, :]).astype(jnp.float32)
    cum = lax.dot_general(
        lower, rate * steps, (((1,), (0,)), ((), ())), precision=lax.Precision.HIGHEST
    )
    chunk = spots // BLK
    chunk_first = chunk * BLK
    ends = cum.reshape(length // BLK, BLK, heads)[:, BLK - 1]
    starts = jnp.concatenate([jnp.zeros((1, heads), jnp.float32), ends[:-1]], axis=0)
    start_wide = jnp.repeat(starts, BLK, axis=0)
    end_wide = jnp.repeat(ends, BLK, axis=0)
    carried = (pos > spots - chunk_first) & (chunk > 0)
    carry = jnp.where(carried[:, None], jnp.exp(cum - start_wide), 0.0)
    lasting = spots + rem >= chunk_first + BLK - 1
    last = jnp.where(lasting[:, None], jnp.exp(end_wide - cum), 0.0)
    cum2 = cum * LOG2E
    cols = jnp.concatenate([steps, cum2, carry, last], axis=1)
    cumt = cum2.T.reshape(groups, -1, length)
    skip_wide = jnp.repeat(skip_full, PM)[None]
    ssm, states, squares = mix_forward(
        gate, fed, cols, cumt, conv_full, skip_wide, posb, bs, cs, bs.T
    )
    factor = lax.rsqrt(jnp.sum(squares, axis=1, keepdims=True) / DIN + 1e-05)
    gain_parts = ggain_full.reshape(parts, 1, inner_width)
    gnormed = (ssm * gate * sigmoid(gate) * factor[None] * gain_parts).astype(low)
    resid1 = part_back(gnormed, w_mid, first=width_qkv, start=resid0)

    u2 = rms_apply(resid1, norm2_gain).astype(low)
    qkv = part_product(u2, w_mid, low, columns=width_qkv)
    attended, logs = attn_forward(qkv, posb)
    resid2 = part_back(attended, w_mid, first=width_qkv + inner_width, start=resid1)

    u3 = rms_apply(resid2, norm3_gain).astype(low)
    half = width_in // 2
    gate3, up3, hidden = ffn_forward(u3, w_ffn, half)
    mixed_row = part_back(hidden, w_ffn, first=width_in, start=resid2)

    piece = length // parts
    mine = lax.dynamic_slice_in_dim(mixed_row, part * piece, piece, 0)
    theirs = swap(lax.dynamic_slice_in_dim(mixed_row, (1 - part) * piece, piece, 0), None)
    mixed = join(mine[None], theirs[None], part)

    core = my_bit(0)

    def half_rows(value, which):
        count = value.shape[0] // 2
        return lax.dynamic_slice_in_dim(value, which * count, count, 0)

    def half_lanes(value, which):
        count = value.shape[2] // 2
        return lax.dynamic_slice_in_dim(value, which * count, count, 2)

    def sum_cores(left_t, right):
        received = swap(part_product(half_rows(left_t, 1 - core), right, low), 0)
        return part_product(half_rows(left_t, core), right, low, extra=received)

    def outer_parts(left, right):
        return lax.dot_general(
            left, right, (((1,), (0,)), ((), ())), preferred_element_type=jnp.float32
        )

    def sum_cores_back(left, right):
        received = swap(outer_parts(half_lanes(left, 1 - core), right).astype(low), 0)
        return add_low(outer_parts(half_lanes(left, core), right), received)

    cot = exchange(d_out + ssm[0, 0, 0] * 0)
    dm3 = cot.astype(low)
    d_gate_up = ffn_backward(dm3, w_ffn, width_in, gate3, up3)
    quarter = d_gate_up.reshape(2 * parts, length, half)
    part_ffn = outer_into(hidden, dm3, 2, width_in, 3 * width_in // 2)
    part_ffn = part_product(u3.T, quarter, low, fold=2, into=part_ffn)
    sum_ffn = ring_scatter(part_ffn.reshape(-1, part_ffn.shape[2]))
    back_u3 = part_back(quarter, w_ffn, deps=[part_ffn])
    back, d_gain3 = rms_back(resid2, norm3_gain, back_u3)
    cot = cot + back

    dm2 = cot.astype(low)
    d_att = part_product(dm2, w_mid, low, first=width_qkv + inner_width)
    part_aout = sum_cores_back(attended, dm2)
    log_rows = jnp.pad(logs[:, :, :4].transpose(0, 2, 1), ((0, 0), (0, 4), (0, 0)))
    d_qkv = attn_backward(
        qkv, attended, d_att, log_rows, remb, []
    )
    part_qkv = sum_cores(u2.T, d_qkv)
    back, d_gain2 = rms_back(resid1, norm2_gain, part_back(d_qkv, w_mid, deps=[part_qkv]))
    cot = cot + back

    dm1 = cot.astype(low)
    d_gn = part_product(dm1, w_mid, jnp.float32, first=width_qkv, columns=inner_width)
    part_mout = sum_cores_back(gnormed, dm1)
    gated = ssm * gate * sigmoid(gate)
    cross = jnp.sum(jnp.sum(gated * gain_parts * d_gn, axis=2), axis=0)[:, None]
    cross = factor * factor * factor * cross / DIN
    d_z, d_fed, d_cols, sums, d_bs, d_cs = mix_backward(
        gate,
        fed,
        ssm,
        d_gn,
        cols,
        cumt,
        conv_full,
        skip_wide,
        ggain_full[None],
        posb,
        remb,
        wide128(factor),
        wide128(cross),
        bs,
        cs,
        cs.T,
        states,
        [part_qkv, part_mout, part_aout, sum_ffn],
    )
    order = x_first()
    stage_qkv = sum_stages(part_qkv, order[:1])
    last_qkv = sum_stages(stage_qkv, order[1:2])
    piece_qkv = sum_stages(last_qkv, order[2:])
    order = y_first()
    stage_mout = sum_stages(part_mout, order[:1])
    last_mout = sum_stages(stage_mout, order[1:2])
    piece_mout = sum_stages(last_mout, order[2:])
    stage_aout = sum_stages(part_aout, order[:1])
    last_aout = sum_stages(stage_aout, order[1:2])
    piece_aout = sum_stages(last_aout, order[2:])
    rows_aout = jnp.concatenate(jnp.split(piece_aout, 2, axis=1), axis=0)
    grad_mid = gather_sum(jnp.concatenate([piece_qkv, piece_mout, rows_aout], axis=1))
    width_mout = piece_mout.shape[1]
    grad_qkv = grad_mid[:, :width_qkv]
    grad_mout = grad_mid[:, width_qkv : width_qkv + width_mout]
    count = rows_aout.shape[0]
    grad_aout = grad_mid[:, width_qkv + width_mout :].reshape(-1, 2, count // 2, width_mout // 2)
    grad_aout = grad_aout.transpose(0, 2, 1, 3).reshape(-1, width_mout)
    d_cum = d_cols[:, :heads]
    d_step = d_cols[:, heads : 2 * heads]
    d_decay = lax.dot_general(
        lower, d_cum, (((0,), (0,)), ((), ())), precision=lax.Precision.HIGHEST
    )
    d_alog = jnp.sum(d_decay * rate * steps, axis=0)
    d_dtr = (d_step + d_decay * rate) * sigmoid(dtr + bias_full)
    d_bias = jnp.sum(d_dtr, axis=0)
    d_bcs = jnp.concatenate([d_bs, d_cs], axis=1).astype(low).astype(jnp.float32)
    d_bc, d_convbc = pull_bc(d_bcs)
    d_rest = jnp.stack(
        [
            jnp.concatenate(
                [
                    d_bc[:, p * state : (p + 1) * state].astype(low),
                    d_dtr[:, p * heads_part : (p + 1) * heads_part].astype(low),
                    jnp.zeros((length, pad), low),
                ],
                axis=1,
            )
            for p in range(parts)
        ]
    )
    d_fed = lax.dynamic_update_slice(d_fed, d_rest, (0, 0, inner_width))
    u1_t = u1.T
    width_fed = d_fed.shape[2]
    part_mix = part_product(
        u1_t, d_fed, low, place=inner_width, room=inner_width + width_fed
    )
    part_mix = part_product(u1_t, d_z, low, into=part_mix)
    grad_mix = ring_gather(ring_scatter(part_mix.reshape(-1, inner_width + width_fed)))
    first_dt = 2 * inner_width + state
    grad_ffn = ring_gather(sum_ffn)
    back_u1 = part_back(
        d_z, w_z, deps=[part_mix, stage_qkv, stage_mout, stage_aout]
    )
    back_u1 = part_back(
        d_fed, w_x, start=back_u1, deps=[last_qkv, last_mout, last_aout, grad_ffn]
    )
    back, d_gain1 = rms_back(resid0, norm1_gain, back_u1)
    cot = cot + back

    bits = dp_bits()
    columns = cot.T.astype(low).reshape((2,) * bits + (shard, length))
    columns = columns.transpose(tuple(range(bits - 1, -1, -1)) + (bits, bits + 1))
    counted = sum_stages(sum_cores(columns.reshape(-1, length), onehot), y_first())
    counted_all = gather_sum(counted, reversed_blocks=False)
    grad_patch = jnp.einsum(
        "vd,cpv->pdc",
        table,
        counted_all.reshape(-1, per_pos, VOCAB),
        preferred_element_type=jnp.float32,
    ).reshape(patch_weight.shape[0], -1)
    grad_table = reduce_table(
        jnp.einsum(
            "cpv,pdc->vd",
            counted.reshape(-1, per_pos, VOCAB),
            rows_by_pos,
            preferred_element_type=jnp.float32,
        )
    )

    taps = conv_x.shape[0]
    small = [
        d_gain1,
        d_gain2,
        d_gain3,
        d_convbc.reshape(-1),
        d_bias,
        d_alog,
        sums[taps].reshape(heads, PM).sum(axis=1),
        sums[taps + 1],
        sums[:taps].reshape(-1),
    ]
    counts = [item.shape[0] for item in small]
    packed = jnp.concatenate(small)
    fill = (-packed.shape[0]) % 1024
    packed = spread_all(jnp.pad(packed, (0, fill)).reshape(-1, 1024)).reshape(-1)
    split = []
    begin = 0
    for count in counts:
        split.append(packed[begin : begin + count])
        begin += count
    d_gain1, d_gain2, d_gain3, d_convbc, d_bias, d_alog, d_skipped, d_ggain, d_convx = split

    def own_half(vector):
        count = vector.shape[-1] // parts
        return lax.dynamic_slice_in_dim(vector, part * count, count, vector.ndim - 1)

    model_width = grad_mix.shape[0]
    wide = jnp.float32
    half_bc = grad_mix[:, 2 * inner_width : 2 * inner_width + state]
    grad_bc = jnp.concatenate(list(both_parts(half_bc)), axis=1).astype(wide)
    grad_out = grad_ffn[:, width_in:].reshape(lax.axis_size("dp"), shard, 2, model_width)
    grad_out = grad_out.transpose(0, 2, 1, 3).reshape(-1, model_width)
    return (
        mixed,
        grad_table,
        grad_patch,
        d_gain1,
        unfold(grad_mix[:, : 2 * inner_width], 2, inner_width),
        grad_mix[:, first_dt : first_dt + heads_part].astype(wide),
        grad_bc,
        own_half(d_convx.reshape(taps, -1)),
        d_convbc.reshape(conv_bc.shape),
        own_half(d_bias),
        own_half(d_alog),
        own_half(d_skipped),
        own_half(d_ggain),
        grad_mout.astype(wide),
        d_gain2,
        unfold(grad_qkv, attn_qkv.shape[1], attn_qkv.shape[2]),
        grad_aout.astype(wide),
        d_gain3,
        unfold(grad_ffn[:, :width_in], ffn_in.shape[1], half),
        grad_out.astype(wide),
    )


def product(left, right):
    return jnp.dot(left, right, preferred_element_type=jnp.float32)


def product_left(left, right):
    return lax.dot_general(
        left, right, (((0,), (0,)), ((), ())), preferred_element_type=jnp.float32
    )


def product_right(left, right):
    return lax.dot_general(
        left, right, (((1,), (1,)), ((), ())), preferred_element_type=jnp.float32
    )


def rms_apply(hidden, gain):
    return hidden * lax.rsqrt(jnp.mean(hidden * hidden, axis=-1, keepdims=True) + 1e-05) * gain


def conv_rows(signal, weights, seg):
    taps = weights.shape[0]
    total = weights[taps - 1] * signal
    for lag in range(1, taps):
        moved = jnp.concatenate(
            [jnp.zeros((lag, signal.shape[1]), signal.dtype), signal[:-lag]], axis=0
        )
        same = jnp.concatenate([jnp.zeros((lag,), dtype=bool), seg[lag:] == seg[:-lag]], axis=0)
        total = total + weights[taps - 1 - lag] * moved * same[:, None]
    return total


def mixer_local(packed, seg, conv_x, conv_bc, dt_bias, a_log, d_skip):
    length = packed.shape[0]
    width = conv_x.shape[1]
    state = conv_bc.shape[1] // 2
    heads = dt_bias.shape[0]
    gate_part = packed[:, :width]
    xin = packed[:, width : 2 * width]
    bc = packed[:, 2 * width : 2 * width + 2 * state]
    dtr = packed[:, 2 * width + 2 * state :]
    xs = jax.nn.silu(conv_rows(xin, conv_x, seg))
    bcs = jax.nn.silu(conv_rows(bc, conv_bc, seg)).astype(jnp.bfloat16)
    inner = product_right(bcs[:, state:], bcs[:, :state])
    steps = jax.nn.softplus(dtr + dt_bias)
    cumul = jnp.cumsum(-jnp.exp(a_log) * steps, axis=0).T
    spots = jnp.arange(length)
    keep = ((spots[:, None] >= spots[None, :]) & (seg[:, None] == seg[None, :]))[None]
    spread = cumul[:, :, None] - cumul[:, None, :]
    mixing = (jnp.where(keep, jnp.exp(jnp.where(keep, spread, 0.0)), 0.0) * inner[None]).astype(
        jnp.bfloat16
    )
    channels = xs.reshape(length, heads, -1)
    driven = (steps[:, :, None] * channels).astype(jnp.bfloat16)
    moved = jnp.einsum("hts,shp->thp", mixing, driven, preferred_element_type=jnp.float32)
    result = moved + d_skip[None, :, None] * channels
    return result.reshape(length, width) * jax.nn.silu(gate_part)


def attend_local(packed, seg):
    length = packed.shape[0]
    width = packed.shape[1] // 3
    heads = width // HD
    rounded = packed.astype(jnp.bfloat16)
    query = rounded[:, :width].reshape(length, heads, HD)
    keys = rounded[:, width : 2 * width].reshape(length, heads, HD)
    vals = rounded[:, 2 * width :].reshape(length, heads, HD)
    spots = jnp.arange(length)
    keep = ((spots[:, None] >= spots[None, :]) & (seg[:, None] == seg[None, :]))[None]
    scores = jnp.einsum("thd,shd->hts", query, keys, preferred_element_type=jnp.float32) * HD ** (
        -0.5
    )
    scores = jnp.where(keep, scores, -1e30)
    top = jnp.max(scores, axis=-1, keepdims=True)
    weights = jnp.exp(scores - top)
    weights = (weights / jnp.sum(weights, axis=-1, keepdims=True)).astype(jnp.bfloat16)
    result = jnp.einsum("hts,shd->thd", weights, vals, preferred_element_type=jnp.float32)
    return result.reshape(length, width)


def swiglu_local(packed):
    half = packed.shape[1] // 2
    return jax.nn.silu(packed[:, :half]) * packed[:, half:]


def widen(block):
    return lax.all_gather(block, "mp", axis=0, tiled=True)


def narrow(term, count):
    return lax.psum_scatter(
        term(jnp.int32(0), count * lax.axis_size("mp")), "mp", scatter_dimension=0, tiled=True
    )


def widen_grad(block):
    return lax.all_gather(block, "mp", axis=0, tiled=True)


def narrow_grad(term, count):
    return lax.psum_scatter(
        term(jnp.int32(0), count * lax.axis_size("mp")), "mp", scatter_dimension=0, tiled=True
    )


def arrange(full):
    table, patch_rows, w_mix, w_dt, w_bc, w_mout, w_qkv, w_aout, w_ffin, w_ffout = full
    width = w_mix.shape[0]
    w_proj = jnp.concatenate([w_mix.reshape(width, -1), w_bc, w_dt], axis=1)
    return (
        table,
        patch_rows,
        w_proj,
        w_mout,
        w_qkv.reshape(width, -1),
        w_aout,
        w_ffin.reshape(width, -1),
        w_ffout,
    )


def table_terms(onehot, d_embed):
    upper = d_embed.astype(jnp.bfloat16)
    lower = (d_embed - upper.astype(jnp.float32)).astype(jnp.bfloat16)
    first = jnp.einsum("lpv,lpd->vd", onehot, upper, preferred_element_type=jnp.float32)
    return first + jnp.einsum("lpv,lpd->vd", onehot, lower, preferred_element_type=jnp.float32)


def on_device(
    byte_ids,
    segment_ids,
    embed_table,
    patch_weight,
    norm1_gain,
    mamba_in,
    mamba_dt,
    mamba_bc,
    conv_x,
    conv_bc,
    dt_bias,
    a_log,
    d_skip,
    gate_gain,
    mamba_out,
    norm2_gain,
    attn_qkv,
    attn_out,
    norm3_gain,
    ffn_in,
    ffn_out,
    d_out,
):
    parts = lax.axis_size("mp")
    index = lax.axis_index("mp")
    piece = byte_ids.shape[1]
    length = piece * parts
    per_pos = PATCH // parts
    inner_width = mamba_in.shape[2]
    state = mamba_bc.shape[1] // 2
    sharded = (
        embed_table,
        patch_weight,
        mamba_in,
        mamba_dt,
        mamba_bc,
        mamba_out,
        attn_qkv,
        attn_out,
        ffn_in,
        ffn_out,
    )
    fetched = (
        lax.all_gather(sharded[0], "dp", axis=0, tiled=True),
        lax.all_gather(sharded[1], "dp", axis=1, tiled=True),
        lax.all_gather(sharded[2], "dp", axis=0, tiled=True),
        lax.all_gather(sharded[3], "dp", axis=0, tiled=True),
        lax.all_gather(sharded[4], "dp", axis=0, tiled=True),
        lax.all_gather(sharded[5], "dp", axis=1, tiled=True),
        lax.all_gather(sharded[6], "dp", axis=0, tiled=True),
        lax.all_gather(sharded[7], "dp", axis=1, tiled=True),
        lax.all_gather(sharded[8], "dp", axis=0, tiled=True),
        lax.all_gather(sharded[9], "dp", axis=1, tiled=True),
    )
    table, patch_rows, w_proj, w_mout, w_qkv, w_aout, w_ffin, w_ffout = arrange(fetched)
    kept = []
    outputs = []
    for batch in range(MB):
        ids_all, seg_all = (
            lax.all_gather(byte_ids[batch], "mp", axis=0, tiled=True),
            lax.all_gather(segment_ids[batch], "mp", axis=0, tiled=True),
        )
        local_ids = lax.dynamic_slice_in_dim(ids_all, index * per_pos, per_pos, 1)
        onehot = (
            local_ids[:, :, None] == jnp.arange(VOCAB, dtype=jnp.int32)[None, None, :]
        ).astype(jnp.bfloat16)
        embedded = jnp.einsum("lpv,vd->lpd", onehot, table, preferred_element_type=jnp.float32)
        embedded = embedded.astype(jnp.bfloat16).reshape(length, -1)
        resid0 = narrow(lambda start, count: product(embedded, patch_rows), piece)
        wide1 = widen(rms_apply(resid0, norm1_gain).astype(jnp.bfloat16))
        proj = product(wide1, w_proj)
        gated = mixer_local(proj, seg_all, conv_x, conv_bc, dt_bias, a_log, d_skip)
        total = lax.psum(jnp.sum(gated * gated, axis=1), "mp")
        factor = lax.rsqrt(total / DIN + 1e-05)[:, None]
        gnormed = (gated * factor * gate_gain).astype(jnp.bfloat16)
        resid1 = resid0 + narrow(lambda start, count: product(gnormed, w_mout), piece)
        wide2 = widen(rms_apply(resid1, norm2_gain).astype(jnp.bfloat16))
        qkv = product(wide2, w_qkv)
        attended = attend_local(qkv, seg_all).astype(jnp.bfloat16)
        resid2 = resid1 + narrow(lambda start, count: product(attended, w_aout), piece)
        wide3 = widen(rms_apply(resid2, norm3_gain).astype(jnp.bfloat16))
        gate_up = product(wide3, w_ffin)
        hidden = swiglu_local(gate_up).astype(jnp.bfloat16)
        outputs.append(resid2 + narrow(lambda start, count: product(hidden, w_ffout), piece))
        kept.append(
            (
                seg_all,
                onehot,
                embedded,
                resid0,
                resid1,
                resid2,
                wide1,
                proj,
                gated,
                factor,
                gnormed,
                wide2,
                qkv,
                attended,
                wide3,
                gate_up,
                hidden,
            )
        )
    mixed = jnp.stack(outputs, axis=0)
    grad_resid = [d_out[batch] for batch in range(MB)]
    acc_ffin = jnp.zeros(w_ffin.shape, jnp.float32)
    acc_ffout = jnp.zeros(w_ffout.shape, jnp.float32)
    acc_gain3 = jnp.zeros(norm3_gain.shape, jnp.float32)
    for batch in range(MB):
        saved = kept[batch]
        wide_grad = widen_grad(grad_resid[batch].astype(jnp.bfloat16))
        acc_ffout = acc_ffout + product_left(saved[16], wide_grad)
        d_hidden = product_right(wide_grad, w_ffout)
        d_gate_up = jax.vjp(swiglu_local, saved[15])[1](d_hidden)[0].astype(jnp.bfloat16)
        acc_ffin = acc_ffin + product_left(saved[14], d_gate_up)
        d_norm = narrow_grad(lambda start, count: product_right(d_gate_up, w_ffin), piece)
        d_back, d_gain = jax.vjp(rms_apply, saved[5], norm3_gain)[1](d_norm)
        grad_resid[batch] = grad_resid[batch] + d_back
        acc_gain3 = acc_gain3 + d_gain
    acc_qkv = jnp.zeros(w_qkv.shape, jnp.float32)
    acc_aout = jnp.zeros(w_aout.shape, jnp.float32)
    acc_gain2 = jnp.zeros(norm2_gain.shape, jnp.float32)
    for batch in range(MB):
        saved = kept[batch]
        seg_all = saved[0]
        wide_grad = widen_grad(grad_resid[batch].astype(jnp.bfloat16))
        acc_aout = acc_aout + product_left(saved[13], wide_grad)
        d_att = product_right(wide_grad, w_aout)
        d_qkv = jax.vjp(lambda packed: attend_local(packed, seg_all), saved[12])[1](d_att)[0]
        d_qkv = d_qkv.astype(jnp.bfloat16)
        acc_qkv = acc_qkv + product_left(saved[11], d_qkv)
        d_norm = narrow_grad(lambda start, count: product_right(d_qkv, w_qkv), piece)
        d_back, d_gain = jax.vjp(rms_apply, saved[4], norm2_gain)[1](d_norm)
        grad_resid[batch] = grad_resid[batch] + d_back
        acc_gain2 = acc_gain2 + d_gain
    acc_proj = jnp.zeros(w_proj.shape, jnp.float32)
    acc_mout = jnp.zeros(w_mout.shape, jnp.float32)
    acc_ggain = jnp.zeros(gate_gain.shape, jnp.float32)
    acc_convx = jnp.zeros(conv_x.shape, jnp.float32)
    acc_convbc = jnp.zeros(conv_bc.shape, jnp.float32)
    acc_bias = jnp.zeros(dt_bias.shape, jnp.float32)
    acc_alog = jnp.zeros(a_log.shape, jnp.float32)
    acc_skip = jnp.zeros(d_skip.shape, jnp.float32)
    acc_gain1 = jnp.zeros(norm1_gain.shape, jnp.float32)
    for batch in range(MB):
        saved = kept[batch]
        seg_all = saved[0]
        gated = saved[8]
        factor = saved[9]
        wide_grad = widen_grad(grad_resid[batch].astype(jnp.bfloat16))
        acc_mout = acc_mout + product_left(saved[10], wide_grad)
        d_gn = product_right(wide_grad, w_mout)
        weighted = d_gn * gate_gain
        acc_ggain = acc_ggain + jnp.sum(gated * factor * d_gn, axis=0)
        cross = lax.psum(jnp.sum(gated * weighted, axis=1), "mp")
        d_gated = weighted * factor - gated * factor**3 * (cross / DIN)[:, None]
        pull = jax.vjp(
            lambda packed, taps_x, taps_bc, bias, decay, skip: mixer_local(
                packed, seg_all, taps_x, taps_bc, bias, decay, skip
            ),
            saved[7],
            conv_x,
            conv_bc,
            dt_bias,
            a_log,
            d_skip,
        )[1]
        d_proj, d_convx, d_convbc, d_bias, d_alog, d_skipped = pull(d_gated)
        d_proj = d_proj.astype(jnp.bfloat16)
        acc_convx = acc_convx + d_convx
        acc_convbc = acc_convbc + d_convbc
        acc_bias = acc_bias + d_bias
        acc_alog = acc_alog + d_alog
        acc_skip = acc_skip + d_skipped
        acc_proj = acc_proj + product_left(saved[6], d_proj)
        d_norm = narrow_grad(lambda start, count: product_right(d_proj, w_proj), piece)
        d_back, d_gain = jax.vjp(rms_apply, saved[3], norm1_gain)[1](d_norm)
        grad_resid[batch] = grad_resid[batch] + d_back
        acc_gain1 = acc_gain1 + d_gain
    acc_patch = jnp.zeros(patch_rows.shape, jnp.float32)
    acc_table = jnp.zeros(table.shape, jnp.float32)
    for batch in range(MB):
        saved = kept[batch]
        wide_grad = widen_grad(grad_resid[batch].astype(jnp.bfloat16))
        acc_patch = acc_patch + product_left(saved[2], wide_grad)
        d_embed = product_right(wide_grad, patch_rows).reshape(length, per_pos, -1)
        acc_table = acc_table + table_terms(saved[1], d_embed)
    model_width = w_proj.shape[0]
    grad_mix = acc_proj[:, : 2 * inner_width].reshape(model_width, 2, inner_width)
    grad_bc = acc_proj[:, 2 * inner_width : 2 * inner_width + 2 * state]
    grad_dt = acc_proj[:, 2 * inner_width + 2 * state :]
    (
        acc_patch,
        grad_mix,
        grad_dt,
        acc_mout,
        acc_convx,
        acc_bias,
        acc_alog,
        acc_skip,
        acc_ggain,
        acc_qkv,
        acc_aout,
        acc_ffin,
        acc_ffout,
    ) = lax.psum(
        (
            acc_patch,
            grad_mix,
            grad_dt,
            acc_mout,
            acc_convx,
            acc_bias,
            acc_alog,
            acc_skip,
            acc_ggain,
            acc_qkv,
            acc_aout,
            acc_ffin,
            acc_ffout,
        ),
        "dp",
    )
    acc_table, grad_bc, acc_convbc, acc_gain1, acc_gain2, acc_gain3 = lax.psum(
        (acc_table, grad_bc, acc_convbc, acc_gain1, acc_gain2, acc_gain3), ("dp", "mp")
    )
    grad_qkv = acc_qkv.reshape(model_width, 3, -1)
    grad_ffin = acc_ffin.reshape(model_width, 2, -1)
    return (
        mixed,
        acc_table,
        acc_patch,
        acc_gain1,
        grad_mix,
        grad_dt,
        grad_bc,
        acc_convx,
        acc_convbc,
        acc_bias,
        acc_alog,
        acc_skip,
        acc_ggain,
        acc_mout,
        acc_gain2,
        grad_qkv,
        acc_aout,
        acc_gain3,
        grad_ffin,
        acc_ffout,
    )


def solution(mesh):
    sizes = dict(mesh.shape)
    by_rows = sizes["mp"] == MB and sizes["dp"] == 16
    return jax.shard_map(
        on_device_rows if by_rows else on_device,
        mesh=mesh,
        in_specs=(
            P(None, ("dp", "mp"), None),
            P(None, ("dp", "mp")),
            P("dp", None),
            P("mp", "dp"),
            P(),
            P("dp", None, "mp"),
            P("dp", "mp"),
            P("dp", None),
            P(None, "mp"),
            P(),
            P("mp"),
            P("mp"),
            P("mp"),
            P("mp"),
            P("mp", "dp"),
            P(),
            P("dp", None, "mp"),
            P("mp", "dp"),
            P(),
            P("dp", None, "mp"),
            P("mp", "dp"),
            P(None, ("dp", "mp"), None),
        ),
        out_specs=(
            P(None, ("dp", "mp"), None),
            P(),
            P("mp", None),
            P(),
            P(None, None, "mp"),
            P(None, "mp"),
            P(),
            P(None, "mp"),
            P(),
            P("mp"),
            P("mp"),
            P("mp"),
            P("mp"),
            P("mp", None),
            P(),
            P(None, None, "mp"),
            P("mp", None),
            P(),
            P(None, None, "mp"),
            P("mp", None),
        ),
        check_vma=False,
    )
```

```python
import jax
import jax.numpy as jnp
from jax import lax
from jax.experimental import pallas as pl
from jax.experimental.pallas import tpu as pltpu
from jax.sharding import PartitionSpec as P

PATCH = 8
VOCAB = 256
HD = 64
MB = 2
DIN = 2048
PM = 64
TAPS = 4
VMEM_LIMIT = 56 * 1024 * 1024
LOG2E = 1.4426950408889634
BLK = 256


def dot_nn(a, b):
    return lax.dot_general(a, b, (((1,), (0,)), ((), ())), preferred_element_type=jnp.float32)


def dot_nt(a, b):
    return lax.dot_general(a, b, (((1,), (1,)), ((), ())), preferred_element_type=jnp.float32)


def dot_tn(a, b):
    return lax.dot_general(a, b, (((0,), (0,)), ((), ())), preferred_element_type=jnp.float32)


def sigmoid(v):
    return 0.5 * jnp.tanh(0.5 * v) + 0.5


def head_masks(width, size):
    lane = lax.broadcasted_iota(jnp.int32, (1, width), 1) // size
    return [lane == h for h in range(width // size)]


def spread_heads(cols, first, masks, width):
    rows = cols.shape[0]
    out = jnp.broadcast_to(cols[:, first : first + 1], (rows, width))
    for h in range(1, len(masks)):
        piece = jnp.broadcast_to(cols[:, first + h : first + h + 1], (rows, width))
        out = jnp.where(masks[h], piece, out)
    return out


def two_parts(v):
    upper = v.astype(jnp.bfloat16)
    return upper, (v - upper.astype(jnp.float32)).astype(jnp.bfloat16)


def attn_fwd_kernel(q_ref, k_ref, v_ref, pos_ref, o_ref, lse_ref, bias_ref):
    length = pos_ref.shape[0]
    width = q_ref.shape[2]

    @pl.when(pl.program_id(0) == 0)
    def _():
        for i in range(length // BLK):
            rows = pl.ds(i * BLK, BLK)
            n = (i + 1) * BLK
            spot = i * BLK + lax.broadcasted_iota(jnp.int32, (BLK, n), 0)
            other = lax.broadcasted_iota(jnp.int32, (BLK, n), 1)
            gap = (spot - other).astype(jnp.float32)
            keep = (gap >= 0.0) & (gap <= pos_ref[rows, 0:1])
            bias_ref[rows, 0:n] = jnp.where(keep, 0.0, -1e30)

    masks = head_masks(width, HD)
    spots = lax.broadcasted_iota(jnp.int32, (1, 128), 1)
    for i in range(length // BLK):
        rows = pl.ds(i * BLK, BLK)
        n = (i + 1) * BLK
        query = q_ref[0, rows, :] * jnp.bfloat16(HD**-0.5)
        keys = k_ref[0, 0:n, :]
        vals = v_ref[0, 0:n, :]
        bias = bias_ref[rows, 0:n]
        total = jnp.zeros((BLK, width), jnp.float32)
        logs = jnp.zeros((BLK, 128), jnp.float32)
        for h, mask in enumerate(masks):
            scores = dot_nt(jnp.where(mask, query, jnp.bfloat16(0)), keys) + bias
            top = jnp.max(scores, axis=1, keepdims=True)
            weights = jnp.exp(scores - top)
            norm = jnp.sum(weights, axis=1, keepdims=True)
            probs = (weights * (1.0 / norm)).astype(jnp.bfloat16)
            total = jnp.where(mask, dot_nn(probs, vals), total)
            logs = jnp.where(spots == h, top + jnp.log(norm), logs)
        o_ref[0, rows, :] = total.astype(jnp.bfloat16)
        lse_ref[0, rows, :] = logs


def attn_forward(qkv, posb):
    parts, length, width3 = qkv.shape
    width = width3 // 3
    lanes = min(256, width)
    per = width // lanes
    groups = parts * per
    block = (1, length, lanes)
    return pl.pallas_call(
        attn_fwd_kernel,
        grid=(groups,),
        in_specs=[
            pl.BlockSpec(block, lambda g: (g // per, 0, g % per)),
            pl.BlockSpec(block, lambda g: (g // per, 0, per + g % per)),
            pl.BlockSpec(block, lambda g: (g // per, 0, 2 * per + g % per)),
            pl.BlockSpec((length, 128), lambda g: (0, 0)),
        ],
        out_specs=[
            pl.BlockSpec(block, lambda g: (g // per, 0, g % per)),
            pl.BlockSpec((1, length, 128), lambda g: (g, 0, 0)),
        ],
        out_shape=[
            jax.ShapeDtypeStruct((parts, length, width), jnp.bfloat16),
            jax.ShapeDtypeStruct((groups, length, 128), jnp.float32),
        ],
        scratch_shapes=[pltpu.VMEM((length, length), jnp.float32)],
        compiler_params=pltpu.CompilerParams(vmem_limit_bytes=VMEM_LIMIT),
        cost_estimate=pl.CostEstimate(
            flops=30_000_000_000, bytes_accessed=10_000_000, transcendentals=0
        ),
        name="attn_fwd",
    )(qkv, qkv, qkv, posb)


def attn_bwd_kernel(
    q_ref, k_ref, v_ref, o_ref, do_ref, lse_ref, rem_ref, *others
):
    out_ref, bias_ref, dk_ref, dv_ref = others[-4:]
    length = rem_ref.shape[0]
    width = q_ref.shape[2]
    per = out_ref.shape[2] // (3 * width)
    step = pl.program_id(0)

    @pl.when(step == 0)
    def _():
        for i in range(length // BLK):
            cols = pl.ds(i * BLK, BLK)
            n = (i + 1) * BLK
            other = lax.broadcasted_iota(jnp.int32, (n, BLK), 0)
            spot = i * BLK + lax.broadcasted_iota(jnp.int32, (n, BLK), 1)
            gap = (spot - other).astype(jnp.float32)
            keep = (gap >= 0.0) & (gap <= rem_ref[0:n, 0:1])
            bias_ref[0:n, cols] = jnp.where(keep, 0.0, -1e30)

    masks = head_masks(width, HD)
    heads = len(masks)
    rows8 = lax.broadcasted_iota(jnp.int32, (8, width), 0)
    lane8 = lax.broadcasted_iota(jnp.int32, (8, width), 1) // HD
    picks = jnp.where(rows8 == lane8, 1.0, 0.0).astype(jnp.bfloat16)
    scale = jnp.bfloat16(HD**-0.5)
    zero = jnp.bfloat16(0)
    offset = pl.multiple_of((step % per) * width, width)
    nblocks = length // BLK
    for i in reversed(range(nblocks)):
        rows = pl.ds(i * BLK, BLK)
        n = (i + 1) * BLK
        query = q_ref[0, rows, :] * scale
        grad = do_ref[0, rows, :]
        prod = grad.astype(jnp.float32) * o_ref[0, rows, :].astype(jnp.float32)
        upper, lower = two_parts(prod)
        delta = dot_nt(picks, upper) + dot_nt(picks, lower)
        keys = k_ref[0, 0:n, :]
        vals = v_ref[0, 0:n, :]
        bias = bias_ref[0:n, rows]
        d_query = jnp.zeros((BLK, width), jnp.float32)
        d_keys = jnp.zeros((n, width), jnp.float32)
        d_vals = jnp.zeros((n, width), jnp.float32)
        for h, mask in enumerate(masks):
            q_head = jnp.where(mask, query, zero)
            g_head = jnp.where(mask, grad, zero)
            probs = jnp.exp(dot_nt(keys, q_head) + bias - lse_ref[0, h : h + 1, rows])
            d_probs = dot_nt(vals, g_head)
            d_scores = (probs * (d_probs - delta[h : h + 1, :])).astype(jnp.bfloat16)
            d_vals = d_vals + dot_nn(probs.astype(jnp.bfloat16), g_head)
            d_keys = d_keys + dot_nn(d_scores, q_head)
            d_query = jnp.where(mask, dot_tn(d_scores, keys), d_query)
        out_ref[0, rows, pl.ds(offset, width)] = (d_query * (HD**-0.5)).astype(jnp.bfloat16)
        if i == nblocks - 1:
            dk_ref[...] = d_keys
            dv_ref[...] = d_vals
        else:
            dk_ref[0:n, :] += d_keys
            dv_ref[0:n, :] += d_vals
    out_ref[0, :, pl.ds(per * width + offset, width)] = dk_ref[...].astype(jnp.bfloat16)
    out_ref[0, :, pl.ds(2 * per * width + offset, width)] = dv_ref[...].astype(jnp.bfloat16)


def attn_backward(qkv, attended, d_att, lse_rows, remb, deps):
    parts, length, width3 = qkv.shape
    width = width3 // 3
    lanes = min(256, width)
    per = width // lanes
    groups = parts * per
    block = (1, length, lanes)
    return pl.pallas_call(
        attn_bwd_kernel,
        grid=(groups,),
        in_specs=[
            pl.BlockSpec(block, lambda g: (g // per, 0, g % per)),
            pl.BlockSpec(block, lambda g: (g // per, 0, per + g % per)),
            pl.BlockSpec(block, lambda g: (g // per, 0, 2 * per + g % per)),
            pl.BlockSpec(block, lambda g: (g // per, 0, g % per)),
            pl.BlockSpec(block, lambda g: (g // per, 0, g % per)),
            pl.BlockSpec((1, 8, length), lambda g: (g, 0, 0)),
            pl.BlockSpec((length, 128), lambda g: (0, 0)),
        ]
        + [pl.BlockSpec(memory_space=pl.ANY)] * len(deps),
        out_specs=pl.BlockSpec((1, length, width3), lambda g: (g // per, 0, 0)),
        out_shape=jax.ShapeDtypeStruct(qkv.shape, jnp.bfloat16),
        scratch_shapes=[
            pltpu.VMEM((length, length), jnp.float32),
            pltpu.VMEM((length, lanes), jnp.float32),
            pltpu.VMEM((length, lanes), jnp.float32),
        ],
        compiler_params=pltpu.CompilerParams(vmem_limit_bytes=VMEM_LIMIT),
        cost_estimate=pl.CostEstimate(
            flops=70_000_000_000, bytes_accessed=20_000_000, transcendentals=0
        ),
        name="attn_bwd",
    )(qkv, qkv, qkv, attended, d_att, lse_rows, remb, *deps)


def conv_moved(ref, part, rows, first, pos):
    width = ref.shape[2]
    if first == 0:
        before = jnp.zeros((8, width), jnp.float32)
    else:
        before = ref[part, pl.ds(first - 8, 8), :]
    signal = jnp.concatenate([before, ref[part, pl.ds(first, rows), :]], axis=0)
    moved = [signal[8:]]
    for lag in range(1, TAPS):
        shifted = pltpu.roll(signal, lag, 0)[8:]
        moved.append(jnp.where(pos >= lag, shifted, 0.0))
    return moved


def wide_rows(ref, first, rows, width):
    block = ref[pl.ds(first, rows), :]
    return jnp.concatenate([block] * (width // block.shape[1]), axis=1)


def mix_fwd_kernel(
    z_ref, x_ref, cols_ref, cumt_ref, conv_ref, skip_ref, gain_ref, pos_ref, bs_ref, cs_ref,
    bst_ref, ssm_ref, scaled_ref, state_ref, ssq_ref, inner_ref,
):
    length = pos_ref.shape[0]
    width = x_ref.shape[2]
    step = pl.program_id(0)
    chunks = length // BLK

    @pl.when(step == 0)
    def _():
        for k in range(chunks):
            rows = pl.ds(k * BLK, BLK)
            spot = lax.broadcasted_iota(jnp.int32, (BLK, BLK), 0)
            other = lax.broadcasted_iota(jnp.int32, (BLK, BLK), 1)
            gap = (spot - other).astype(jnp.float32)
            keep = (gap >= 0.0) & (gap <= pos_ref[rows, 0:1])
            inner_ref[k] = jnp.where(keep, dot_nt(cs_ref[rows, :], bs_ref[rows, :]), 0.0)

    masks = head_masks(width, PM)
    heads = len(masks)
    span = cols_ref.shape[1] // 4
    turn = lax.rem(4 * span - step * heads, 4 * span)
    state = jnp.zeros((bs_ref.shape[1], width), jnp.float32)
    for k in range(chunks):
        first = k * BLK
        rows = pl.ds(first, BLK)
        pos = wide_rows(pos_ref, first, BLK, width)
        moved = conv_moved(x_ref, 0, BLK, first, pos)
        pre = conv_ref[TAPS - 1 : TAPS, :] * moved[0]
        for lag in range(1, TAPS):
            pre = pre + conv_ref[TAPS - 1 - lag : TAPS - lag, :] * moved[lag]
        xs = pre * sigmoid(pre)
        cols = pltpu.roll(cols_ref[rows, :], turn, 1)
        driven = (spread_heads(cols, 0, masks, width) * xs).astype(jnp.bfloat16)
        out = skip_ref[...] * xs
        inner = inner_ref[k]
        for h, mask in enumerate(masks):
            gap = cols[:, span + h : span + h + 1] - cumt_ref[0, h : h + 1, rows]
            mixing = (jnp.exp2(jnp.minimum(gap, 0.0)) * inner).astype(jnp.bfloat16)
            out = out + dot_nn(mixing, jnp.where(mask, driven, jnp.bfloat16(0)))
        state_bf, state_rest = two_parts(state)
        state_ref[k] = state_bf
        if k > 0:
            carry = spread_heads(cols, 2 * span, masks, width)
            recalled = dot_nn(cs_ref[rows, :], state_bf) + dot_nn(cs_ref[rows, :], state_rest)
            out = out + carry * recalled
        if k < chunks - 1:
            last = spread_heads(cols, 3 * span, masks, width)
            fed, fed_rest = two_parts(last * driven.astype(jnp.float32))
            fresh = dot_nn(bst_ref[:, rows], fed) + dot_nn(bst_ref[:, rows], fed_rest)
            if k > 0:
                fresh = fresh + carry[BLK - 1 : BLK, :] * state
            state = fresh
        ssm_ref[0, rows, :] = out
        gate = z_ref[0, rows, :]
        gated = out * gate * sigmoid(gate)
        scaled_ref[0, rows, :] = (gated * gain_ref[...]).astype(jnp.bfloat16)
        square = gated * gated
        total = square[:, 0:128]
        for lane in range(128, width, 128):
            total = total + square[:, lane : lane + 128]

        @pl.when(step == 0)
        def _():
            ssq_ref[rows, :] = total

        @pl.when(step > 0)
        def _():
            ssq_ref[rows, :] += total


def mix_forward(z, x, cols, cumt, conv, skip, gain, posb, bs, cs, bst):
    parts, length, inner_width = z.shape
    state = bs.shape[1]
    lanes = 256
    per = inner_width // lanes
    groups = parts * per
    block = (1, length, lanes)
    whole = lambda g: (0, 0)
    return pl.pallas_call(
        mix_fwd_kernel,
        grid=(groups,),
        in_specs=[
            pl.BlockSpec(block, lambda g: (g // per, 0, g % per)),
            pl.BlockSpec(block, lambda g: (g // per, 0, g % per)),
            pl.BlockSpec(cols.shape, whole),
            pl.BlockSpec((1,) + cumt.shape[1:], lambda g: (g, 0, 0)),
            pl.BlockSpec((TAPS, lanes), lambda g: (0, g)),
            pl.BlockSpec((1, lanes), lambda g: (0, g)),
            pl.BlockSpec((1, lanes), lambda g: (0, g)),
            pl.BlockSpec((length, 128), whole),
            pl.BlockSpec((length, state), whole),
            pl.BlockSpec((length, state), whole),
            pl.BlockSpec((state, length), whole),
        ],
        out_specs=[
            pl.BlockSpec(block, lambda g: (g // per, 0, g % per)),
            pl.BlockSpec(block, lambda g: (g // per, 0, g % per)),
            pl.BlockSpec((length // BLK, state, lanes), lambda g: (0, 0, g)),
            pl.BlockSpec((length, 128), whole),
        ],
        out_shape=[
            jax.ShapeDtypeStruct((parts, length, inner_width), jnp.float32),
            jax.ShapeDtypeStruct((parts, length, inner_width), jnp.bfloat16),
            jax.ShapeDtypeStruct((length // BLK, state, parts * inner_width), jnp.bfloat16),
            jax.ShapeDtypeStruct((length, 128), jnp.float32),
        ],
        scratch_shapes=[pltpu.VMEM((length // BLK, BLK, BLK), jnp.float32)],
        compiler_params=pltpu.CompilerParams(vmem_limit_bytes=VMEM_LIMIT),
        cost_estimate=pl.CostEstimate(
            flops=20_000_000_000, bytes_accessed=30_000_000, transcendentals=0
        ),
        name="mix_fwd",
    )(z, x, cols, cumt, conv, skip, gain, posb, bs, cs, bst)


def mix_bwd_kernel(
    z_ref, x_ref, ssm_ref, dgn_ref, cols_ref, cumt_ref, conv_ref, skip_ref, gain_ref,
    pos_ref, rem_ref, rg_ref, cross_ref, bs_ref, cs_ref, cst_ref, state_ref, *others,
):
    dz_ref, dx_ref, dcols_ref, sums_ref, dbs_ref, dcs_ref = others[-9:-3]
    inner_ref, dinner_ref, dpre_ref = others[-3:]
    length = pos_ref.shape[0]
    width = x_ref.shape[2]
    step = pl.program_id(0)
    chunks = length // BLK
    spot = lax.broadcasted_iota(jnp.int32, (BLK, BLK), 1)
    other = lax.broadcasted_iota(jnp.int32, (BLK, BLK), 0)
    gap = (spot - other).astype(jnp.float32)

    @pl.when(step == 0)
    def _():
        for k in range(chunks):
            rows = pl.ds(k * BLK, BLK)
            keep = (gap >= 0.0) & (gap <= rem_ref[rows, 0:1])
            inner_ref[k] = jnp.where(keep, dot_nt(bs_ref[rows, :], cs_ref[rows, :]), 0.0)
        dinner_ref[...] = jnp.zeros(dinner_ref.shape, jnp.float32)
        dbs_ref[...] = jnp.zeros(dbs_ref.shape, jnp.float32)
        dcs_ref[...] = jnp.zeros(dcs_ref.shape, jnp.float32)
        dcols_ref[...] = jnp.zeros(dcols_ref.shape, jnp.float32)

    masks = head_masks(width, PM)
    heads = len(masks)
    zero = jnp.bfloat16(0)
    head_of = lax.broadcasted_iota(jnp.int32, (width, 128), 0) // PM
    lane_of = lax.broadcasted_iota(jnp.int32, (width, 128), 1)
    span = cols_ref.shape[1] // 4
    turn = lax.rem(4 * span - step * heads, 4 * span)
    lane_of = lane_of - step * heads
    pick_cum = jnp.where(head_of == lane_of, 1.0, 0.0).astype(jnp.bfloat16)
    pick_step = jnp.where(head_of + span == lane_of, 1.0, 0.0).astype(jnp.bfloat16)
    dpre_ref[pl.ds(length, 8), :] = jnp.zeros((8, width), jnp.float32)
    sums_ref[...] = jnp.zeros(sums_ref.shape, jnp.float32)
    d_state = jnp.zeros((bs_ref.shape[1], width), jnp.float32)
    skip = skip_ref[...]
    gain = gain_ref[...]
    for k in reversed(range(chunks)):
        first = k * BLK
        rows = pl.ds(first, BLK)
        pos = wide_rows(pos_ref, first, BLK, width)
        moved = conv_moved(x_ref, 0, BLK, first, pos)
        pre = conv_ref[TAPS - 1 : TAPS, :] * moved[0]
        for lag in range(1, TAPS):
            pre = pre + conv_ref[TAPS - 1 - lag : TAPS - lag, :] * moved[lag]
        sig = sigmoid(pre)
        xs = pre * sig
        cols = pltpu.roll(cols_ref[rows, :], turn, 1)
        step_wide = spread_heads(cols, 0, masks, width)
        driven = (step_wide * xs).astype(jnp.bfloat16)
        gate = z_ref[0, rows, :]
        sig_z = sigmoid(gate)
        silu_z = gate * sig_z
        ssm = ssm_ref[0, rows, :]
        gated = ssm * silu_z
        d_gn = dgn_ref[0, rows, :]
        rg = wide_rows(rg_ref, first, BLK, width)
        cross = wide_rows(cross_ref, first, BLK, width)
        scaled = rg * d_gn
        d_gated = gain * scaled - gated * cross
        sums_ref[5:6, :] += jnp.sum(gated * scaled, axis=0, keepdims=True)
        dz_ref[0, rows, :] = (d_gated * ssm * (sig_z + silu_z * (1.0 - sig_z))).astype(jnp.bfloat16)
        d_out = d_gated * silu_z
        d_low = d_out.astype(jnp.bfloat16)
        sums_ref[4:5, :] += jnp.sum(d_out * xs, axis=0, keepdims=True)
        inner = inner_ref[k]
        d_inner = dinner_ref[k]
        d_driven = jnp.zeros((BLK, width), jnp.float32)
        for h, mask in enumerate(masks):
            gap_h = cumt_ref[0, h : h + 1, rows] - cols[:, span + h : span + h + 1]
            decay = jnp.exp2(jnp.minimum(gap_h, 0.0))
            mixing = (decay * inner).astype(jnp.bfloat16)
            d_driven = d_driven + dot_nn(mixing, jnp.where(mask, d_low, zero))
            d_inner = d_inner + decay * dot_nt(jnp.where(mask, driven, zero), d_low)
        dinner_ref[k] = d_inner
        if k > 0:
            carry = spread_heads(cols, 2 * span, masks, width)
            carried, carried_rest = two_parts(carry * d_low.astype(jnp.float32))
            dcs_ref[rows, :] += dot_nt(carried, state_ref[k])
        if k < chunks - 1:
            last = spread_heads(cols, 3 * span, masks, width)
            fed = (last * driven.astype(jnp.float32)).astype(jnp.bfloat16)
            d_state_bf, d_state_rest = two_parts(d_state)
            dbs_ref[rows, :] += dot_nt(fed, d_state_bf)
            recalled = dot_nn(bs_ref[rows, :], d_state_bf) + dot_nn(bs_ref[rows, :], d_state_rest)
            d_driven = d_driven + last * recalled
        if k > 0:
            fresh = dot_nn(cst_ref[:, rows], carried) + dot_nn(cst_ref[:, rows], carried_rest)
            if k < chunks - 1:
                fresh = fresh + carry[BLK - 1 : BLK, :] * d_state
            d_state = fresh
        moved_out = ssm - skip * xs
        balance = d_low.astype(jnp.float32) * moved_out - driven.astype(jnp.float32) * d_driven
        upper, lower = two_parts(balance)
        d_cum = dot_nn(upper, pick_cum) + dot_nn(lower, pick_cum)
        d_driven = d_driven.astype(jnp.bfloat16).astype(jnp.float32)
        upper, lower = two_parts(d_driven * xs)
        dcols_ref[rows, :] += d_cum + dot_nn(upper, pick_step) + dot_nn(lower, pick_step)
        d_xs = skip * d_out + step_wide * d_driven
        d_pre = d_xs * (sig + xs * (1.0 - sig))
        dpre_ref[rows, :] = d_pre
        for lag in range(TAPS):
            sums_ref[TAPS - 1 - lag : TAPS - lag, :] += jnp.sum(
                d_pre * moved[lag], axis=0, keepdims=True
            )
        after = jnp.concatenate([d_pre, dpre_ref[pl.ds(first + BLK, 8), :]], axis=0)
        rem = wide_rows(rem_ref, first, BLK, width)
        d_x = conv_ref[TAPS - 1 : TAPS, :] * d_pre
        for lag in range(1, TAPS):
            shifted = pltpu.roll(after, BLK + 8 - lag, 0)[0:BLK]
            d_x = d_x + conv_ref[TAPS - 1 - lag : TAPS - lag, :] * jnp.where(
                rem >= lag, shifted, 0.0
            )
        dx_ref[0, rows, :] = d_x.astype(jnp.bfloat16)

    @pl.when(step == pl.num_programs(0) - 1)
    def _():
        for k in range(chunks):
            rows = pl.ds(k * BLK, BLK)
            keep = (gap >= 0.0) & (gap <= rem_ref[rows, 0:1])
            d_inner = jnp.where(keep, dinner_ref[k], 0.0)
            dbs_ref[rows, :] += dot_nn(d_inner.astype(jnp.bfloat16), cs_ref[rows, :])
            dcs_ref[rows, :] += dot_nn(d_inner.T.astype(jnp.bfloat16), bs_ref[rows, :])


def mix_backward(
    z, x, ssm, d_gn, cols, cumt, conv, skip, gain, posb, remb, rgb, crossb, bs, cs, cst, states, deps
):
    parts, length, inner_width = ssm.shape
    state = bs.shape[1]
    lanes = 256
    per = inner_width // lanes
    groups = parts * per
    block = (1, length, lanes)
    whole = lambda g: (0, 0)
    own = lambda g: (g // per, 0, g % per)
    return pl.pallas_call(
        mix_bwd_kernel,
        grid=(groups,),
        in_specs=[
            pl.BlockSpec(block, own),
            pl.BlockSpec(block, own),
            pl.BlockSpec(block, own),
            pl.BlockSpec(block, own),
            pl.BlockSpec(cols.shape, whole),
            pl.BlockSpec((1,) + cumt.shape[1:], lambda g: (g, 0, 0)),
            pl.BlockSpec((TAPS, lanes), lambda g: (0, g)),
            pl.BlockSpec((1, lanes), lambda g: (0, g)),
            pl.BlockSpec((1, lanes), lambda g: (0, g)),
            pl.BlockSpec((length, 128), whole),
            pl.BlockSpec((length, 128), whole),
            pl.BlockSpec((length, 128), whole),
            pl.BlockSpec((length, 128), whole),
            pl.BlockSpec((length, state), whole),
            pl.BlockSpec((length, state), whole),
            pl.BlockSpec((state, length), whole),
            pl.BlockSpec((length // BLK, state, lanes), lambda g: (0, 0, g)),
        ]
        + [pl.BlockSpec(memory_space=pl.ANY)] * len(deps),
        out_specs=[
            pl.BlockSpec(block, own),
            pl.BlockSpec(block, own),
            pl.BlockSpec((length, 128), whole),
            pl.BlockSpec((8, lanes), lambda g: (0, g)),
            pl.BlockSpec((length, state), whole),
            pl.BlockSpec((length, state), whole),
        ],
        out_shape=[
            jax.ShapeDtypeStruct((parts, length, inner_width), jnp.bfloat16),
            jax.ShapeDtypeStruct(x.shape, jnp.bfloat16),
            jax.ShapeDtypeStruct((length, 128), jnp.float32),
            jax.ShapeDtypeStruct((8, parts * inner_width), jnp.float32),
            jax.ShapeDtypeStruct((length, state), jnp.float32),
            jax.ShapeDtypeStruct((length, state), jnp.float32),
        ],
        scratch_shapes=[
            pltpu.VMEM((length // BLK, BLK, BLK), jnp.float32),
            pltpu.VMEM((length // BLK, BLK, BLK), jnp.float32),
            pltpu.VMEM((length + 8, lanes), jnp.float32),
        ],
        compiler_params=pltpu.CompilerParams(vmem_limit_bytes=VMEM_LIMIT),
        cost_estimate=pl.CostEstimate(
            flops=50_000_000_000, bytes_accessed=50_000_000, transcendentals=0
        ),
        name="mix_bwd",
    )(
        z, x, ssm, d_gn, cols, cumt, conv, skip, gain, posb, remb, rgb, crossb, bs, cs, cst,
        states, *deps,
    )


def tile_of(columns, limit=512):
    size = limit
    while columns % size:
        size -= 128
    return size


def part_product(
    left, right, dtype, first=0, columns=None, extra=None, deps=(), fold=1, into=None, place=0, room=None
):
    parts, depth, whole = right.shape
    rows = left.shape[0]
    columns = whole - first if columns is None else columns
    tile = tile_of(columns)
    while first % tile or place % tile:
        tile = tile_of(columns, tile - 128)
    begin = first // tile
    count = columns // tile
    block = (1, rows, tile)
    shift = place // tile
    room = fold * columns if room is None else room
    in_specs = [
        pl.BlockSpec((rows, depth), lambda m, n: (0, 0)),
        pl.BlockSpec((1, depth, tile), lambda m, n: (m, 0, begin + n)),
    ]
    operands = [left, right]
    if extra is not None:
        in_specs.append(pl.BlockSpec(block, lambda m, n: (m, 0, n)))
        operands.append(extra)
    aliases = {}
    if into is not None:
        aliases = {len(operands): 0}
        deps = (into,) + tuple(deps)
        room = into.shape[2]
    in_specs += [pl.BlockSpec(memory_space=pl.ANY)] * len(deps)

    def body(left_ref, right_ref, *others):
        total = dot_nn(left_ref[...], right_ref[0])
        if extra is not None:
            total = total + others[0][0].astype(jnp.float32)
        others[-1][0] = total.astype(dtype)

    return pl.pallas_call(
        body,
        grid=(parts, count),
        in_specs=in_specs,
        out_specs=pl.BlockSpec(
            block, lambda m, n: (m // fold, 0, shift + (m % fold) * count + n)
        ),
        out_shape=jax.ShapeDtypeStruct((parts // fold, rows, room), dtype),
        input_output_aliases=aliases,
        compiler_params=pltpu.CompilerParams(vmem_limit_bytes=VMEM_LIMIT),
        cost_estimate=pl.CostEstimate(
            flops=2 * parts * rows * depth * columns,
            bytes_accessed=parts * depth * columns * 2 + parts * rows * columns * 4,
            transcendentals=0,
        ),
        name="part_product",
    )(*operands, *deps)


def part_back(left, right, first=0, start=None, scale=None, deps=()):
    parts, rows, columns = left.shape
    width = right.shape[1]
    fold = parts // right.shape[0]
    tile = tile_of(columns)
    while first % tile:
        tile = tile_of(columns, tile - 128)
    begin = first // tile
    count = columns // tile
    in_specs = [
        pl.BlockSpec((1, rows, tile), lambda m, n: (m, 0, n)),
        pl.BlockSpec(
            (1, width, tile), lambda m, n: (m // fold, 0, begin + (m % fold) * count + n)
        ),
    ]
    operands = [left, right]
    if start is not None:
        in_specs.append(pl.BlockSpec((rows, width), lambda m, n: (0, 0)))
        operands.append(start)
    if scale is not None:
        in_specs.append(pl.BlockSpec(scale.shape, lambda m, n: (0, 0)))
        operands.append(scale)
    in_specs += [pl.BlockSpec(memory_space=pl.ANY)] * len(deps)

    def body(left_ref, right_ref, *others):
        out_ref = others[-1]
        total = dot_nt(left_ref[0], right_ref[0])
        opening = (pl.program_id(0) == 0) & (pl.program_id(1) == 0)

        if scale is not None:
            total = total * others[1][:, 0:1]

        @pl.when(opening)
        def _():
            out_ref[...] = total if start is None else total + others[0][...]

        @pl.when(jnp.logical_not(opening))
        def _():
            out_ref[...] += total

    return pl.pallas_call(
        body,
        grid=(parts, count),
        in_specs=in_specs,
        out_specs=pl.BlockSpec((rows, width), lambda m, n: (0, 0)),
        out_shape=jax.ShapeDtypeStruct((rows, width), jnp.float32),
        compiler_params=pltpu.CompilerParams(vmem_limit_bytes=VMEM_LIMIT),
        cost_estimate=pl.CostEstimate(
            flops=2 * parts * rows * columns * width,
            bytes_accessed=2 * parts * columns * (rows + width) + 4 * rows * width,
            transcendentals=0,
        ),
        name="part_back",
    )(*operands, *deps)


def outer_kernel(left_ref, right_ref, *others):
    out_ref = others[-1]
    total = dot_tn(left_ref[0], right_ref[...]).astype(jnp.bfloat16)
    rows = out_ref.shape[1]
    width = right_ref.shape[1]
    wraps = total.shape[0] // rows
    piece = 64
    for i in range(rows // piece):
        for w in range(wraps):
            begin = (i * wraps + w) * piece
            out_ref[0, pl.ds(i * piece, piece), pl.ds(w * width, width)] = total[
                begin : begin + piece
            ]


def outer_into(left, right, wraps, place, room, into=None):
    parts, length, columns = left.shape
    width = right.shape[1]
    tile = 256 * wraps
    begin = place // (wraps * width)
    before = [] if into is None else [into]
    return pl.pallas_call(
        outer_kernel,
        grid=(parts, columns // tile),
        in_specs=[
            pl.BlockSpec((1, length, tile), lambda m, n: (m, 0, n)),
            pl.BlockSpec((length, width), lambda m, n: (0, 0)),
        ]
        + [pl.BlockSpec(memory_space=pl.ANY)] * len(before),
        input_output_aliases={2: 0} if before else {},
        out_specs=pl.BlockSpec((1, tile // wraps, wraps * width), lambda m, n: (m, n, begin)),
        out_shape=jax.ShapeDtypeStruct((parts, columns // wraps, room), jnp.bfloat16),
        compiler_params=pltpu.CompilerParams(vmem_limit_bytes=VMEM_LIMIT),
        cost_estimate=pl.CostEstimate(
            flops=2 * parts * length * columns * width,
            bytes_accessed=2 * parts * columns * (length + width),
            transcendentals=0,
        ),
        name="outer_into",
    )(left, right, *before)


def unfold_kernel(in_ref, out_ref):
    count = out_ref.shape[1]
    width = out_ref.shape[2]
    for j in range(count):
        out_ref[:, j, :] = in_ref[:, j * width : (j + 1) * width].astype(jnp.float32)


def unfold(value, count, width):
    rows = value.shape[0]
    step = 128
    return pl.pallas_call(
        unfold_kernel,
        grid=(rows // step,),
        in_specs=[pl.BlockSpec((step, count * width), lambda n: (n, 0))],
        out_specs=pl.BlockSpec((step, count, width), lambda n: (n, 0, 0)),
        out_shape=jax.ShapeDtypeStruct((rows, count, width), jnp.float32),
        compiler_params=pltpu.CompilerParams(vmem_limit_bytes=VMEM_LIMIT),
        cost_estimate=pl.CostEstimate(
            flops=0, bytes_accessed=6 * rows * count * width, transcendentals=0
        ),
        name="unfold",
    )(value)


def ffn_in_kernel(left_ref, gate_w_ref, up_w_ref, gate_ref, up_ref, hidden_ref):
    gate = dot_nn(left_ref[...], gate_w_ref[0])
    upper = dot_nn(left_ref[...], up_w_ref[0])
    gate_ref[0] = gate.astype(jnp.bfloat16)
    up_ref[0] = upper.astype(jnp.bfloat16)
    hidden_ref[0] = (gate * sigmoid(gate) * upper).astype(jnp.bfloat16)


def ffn_forward(left, right, half):
    parts, depth, _ = right.shape
    rows = left.shape[0]
    tile = tile_of(half)
    count = half // tile
    block = pl.BlockSpec((1, rows, tile), lambda m, n: (m, 0, n))
    shape = jax.ShapeDtypeStruct((parts, rows, half), jnp.bfloat16)
    return pl.pallas_call(
        ffn_in_kernel,
        grid=(parts, count),
        in_specs=[
            pl.BlockSpec((rows, depth), lambda m, n: (0, 0)),
            pl.BlockSpec((1, depth, tile), lambda m, n: (m, 0, n)),
            pl.BlockSpec((1, depth, tile), lambda m, n: (m, 0, count + n)),
        ],
        out_specs=[block, block, block],
        out_shape=[shape, shape, shape],
        compiler_params=pltpu.CompilerParams(vmem_limit_bytes=VMEM_LIMIT),
        cost_estimate=pl.CostEstimate(
            flops=4 * parts * rows * depth * half,
            bytes_accessed=parts * half * (4 * depth + 6 * rows),
            transcendentals=0,
        ),
        name="ffn_in",
    )(left, right, right)


def ffn_back_kernel(left_ref, right_ref, gate_ref, up_ref, out_ref):
    grad = dot_nn(left_ref[...], right_ref[0])
    gate = gate_ref[0].astype(jnp.float32)
    sig = sigmoid(gate)
    act = gate * sig
    slope = sig + act * (1.0 - sig)
    out_ref[0, 0] = (grad * up_ref[0].astype(jnp.float32) * slope).astype(jnp.bfloat16)
    out_ref[0, 1] = (grad * act).astype(jnp.bfloat16)


def ffn_backward(left, right, first, gate, upper):
    parts, rows, half = gate.shape
    depth = left.shape[1]
    tile = tile_of(half)
    begin = first // tile
    block = pl.BlockSpec((1, rows, tile), lambda m, n: (m, 0, n))
    return pl.pallas_call(
        ffn_back_kernel,
        grid=(parts, half // tile),
        in_specs=[
            pl.BlockSpec((rows, depth), lambda m, n: (0, 0)),
            pl.BlockSpec((1, depth, tile), lambda m, n: (m, 0, begin + n)),
            block,
            block,
        ],
        out_specs=pl.BlockSpec((1, 2, rows, tile), lambda m, n: (m, 0, 0, n)),
        out_shape=jax.ShapeDtypeStruct((parts, 2, rows, half), jnp.bfloat16),
        compiler_params=pltpu.CompilerParams(vmem_limit_bytes=VMEM_LIMIT),
        cost_estimate=pl.CostEstimate(
            flops=2 * parts * rows * depth * half,
            bytes_accessed=parts * half * (2 * depth + 8 * rows),
            transcendentals=0,
        ),
        name="ffn_back",
    )(left, right, gate, upper)


def span_kernel(col_ref, row_ref, pos_ref, rem_ref):
    length = col_ref.shape[0]
    row = row_ref[...]
    other = lax.broadcasted_iota(jnp.int32, (BLK, length), 1)
    for i in range(length // BLK):
        rows = pl.ds(i * BLK, BLK)
        spot = i * BLK + lax.broadcasted_iota(jnp.int32, (BLK, length), 0)
        same = col_ref[rows, 0:1] == row
        before = jnp.where(same & (other < spot), 1.0, 0.0)
        after = jnp.where(same & (other > spot), 1.0, 0.0)
        before = jnp.sum(before, axis=1, keepdims=True)
        after = jnp.sum(after, axis=1, keepdims=True)
        pos_ref[rows, :] = jnp.broadcast_to(before, (BLK, 128))
        rem_ref[rows, :] = jnp.broadcast_to(after, (BLK, 128))


def spans(seg):
    length = seg.shape[0]
    shape = jax.ShapeDtypeStruct((length, 128), jnp.float32)
    return pl.pallas_call(
        span_kernel,
        out_shape=[shape, shape],
        compiler_params=pltpu.CompilerParams(vmem_limit_bytes=VMEM_LIMIT),
        name="spans",
    )(seg[:, None], seg[None, :])


def refold_kernel(in_ref, out_ref):
    rows, width = in_ref.shape
    count = out_ref.shape[0] // rows
    width = width // count
    piece = 64
    for i in range(rows // piece):
        for j in range(count):
            out_ref[pl.ds((i * count + j) * piece, piece), :] = in_ref[
                i * piece : (i + 1) * piece, j * width : (j + 1) * width
            ].astype(jnp.float32)


def refold(value, first, count, width, step):
    rows = value.shape[0]
    begin = first // (count * width)
    return pl.pallas_call(
        refold_kernel,
        grid=(rows // step,),
        in_specs=[pl.BlockSpec((step, count * width), lambda n: (n, begin))],
        out_specs=pl.BlockSpec((step * count, width), lambda n: (n, 0)),
        out_shape=jax.ShapeDtypeStruct((rows * count, width), jnp.float32),
        compiler_params=pltpu.CompilerParams(vmem_limit_bytes=VMEM_LIMIT),
        cost_estimate=pl.CostEstimate(
            flops=0, bytes_accessed=6 * rows * count * width, transcendentals=0
        ),
        name="refold",
    )(value)


def embed_kernel(ids_ref, mapped_ref, onehot_ref, out_ref):
    length = ids_ref.shape[1]
    value = lax.broadcasted_iota(jnp.int32, (length, VOCAB), 1)
    total = None
    for p in range(ids_ref.shape[2]):
        span = pl.ds(p * VOCAB, VOCAB)
        hit = jnp.where(ids_ref[0, :, p : p + 1] == value, 1.0, 0.0).astype(jnp.bfloat16)
        onehot_ref[0, :, span] = hit
        part = dot_nt(hit, mapped_ref[0, :, span])
        total = part if total is None else total + part

    @pl.when(pl.program_id(0) == 0)
    def _():
        out_ref[...] = total

    @pl.when(pl.program_id(0) > 0)
    def _():
        out_ref[...] += total


def embed_rows(ids, mapped):
    parts, length, count = ids.shape
    width = mapped.shape[1]
    return pl.pallas_call(
        embed_kernel,
        grid=(parts,),
        in_specs=[
            pl.BlockSpec((1, length, count), lambda m: (m, 0, 0)),
            pl.BlockSpec((1, width, count * VOCAB), lambda m: (m, 0, 0)),
        ],
        out_specs=[
            pl.BlockSpec((1, length, count * VOCAB), lambda m: (m, 0, 0)),
            pl.BlockSpec((length, width), lambda m: (0, 0)),
        ],
        out_shape=[
            jax.ShapeDtypeStruct((parts, length, count * VOCAB), jnp.bfloat16),
            jax.ShapeDtypeStruct((length, width), jnp.float32),
        ],
        compiler_params=pltpu.CompilerParams(vmem_limit_bytes=VMEM_LIMIT),
        cost_estimate=pl.CostEstimate(
            flops=2 * parts * length * width * count * VOCAB,
            bytes_accessed=12 * length * width,
            transcendentals=0,
        ),
        name="embed_rows",
    )(ids, mapped)


def bit_of(index, bit):
    return (index >> bit) & 1


def swap(value, stage):
    if stage is None:
        return lax.ppermute(value, "mp", [(0, 1), (1, 0)])
    count = lax.axis_size("dp")
    return lax.ppermute(value, "dp", [(i, i ^ (1 << stage)) for i in range(count)])


def my_bit(stage):
    if stage is None:
        return lax.axis_index("mp")
    return bit_of(lax.axis_index("dp"), stage)


def take_half(value, which):
    half = value.shape[0] // 2
    return lax.dynamic_slice_in_dim(value, which * half, half, 0)


def join(own, other, bit):
    first = jnp.where(bit == 0, own, other)
    second = jnp.where(bit == 0, other, own)
    return jnp.concatenate([first, second], axis=0)


def add_low(left, right):
    return (left.astype(jnp.float32) + right.astype(jnp.float32)).astype(jnp.bfloat16)


def dp_bits():
    return lax.axis_size("dp").bit_length() - 1


def ring_order():
    order = []
    layers = lax.axis_size("dp") // 4
    for side in range(2):
        for spot in range(layers):
            layer = spot if side == 0 else layers - 1 - spot
            for core in range(2):
                order.append(layer * 4 + side * 2 + core)
    return order


def block_of(device, bits):
    value = 0
    for bit in range(bits):
        value = value * 2 + ((device >> bit) & 1)
    return value


def sum_stages(total, order, after=()):
    for turn, stage in enumerate(order):
        mine = my_bit(stage)
        if stage is None:
            received = swap(lax.dynamic_index_in_dim(total, 1 - mine, 0, keepdims=False), None)
            kept = lax.dynamic_index_in_dim(total, mine, 0, keepdims=False)
        else:
            axis = total.ndim - 2
            half = total.shape[axis] // 2
            received = swap(
                lax.dynamic_slice_in_dim(total, (1 - mine) * half, half, axis), stage
            )
            kept = lax.dynamic_slice_in_dim(total, mine * half, half, axis)
        if turn < len(after):
            kept = kept.astype(jnp.float32) + after[turn]
        total = add_low(kept, received)
    return total


def x_first():
    return [None] + list(range(1, dp_bits()))


def y_first():
    return [1, None] + list(range(2, dp_bits()))


def gather_sum(piece, reversed_blocks=True):
    bits = dp_bits()
    order = ring_order()
    ringed = lax.all_gather(piece, "dp", axis=0, axis_index_groups=[order])
    blocks = [None] * len(order)
    for place, device in enumerate(order):
        blocks[block_of(device, bits) if reversed_blocks else device] = ringed[place]
    return jnp.concatenate(blocks, axis=0)


def around_order(part):
    layers = lax.axis_size("dp") // 4
    order = []
    for turn in range(2):
        side = turn if part == 0 else 1 - turn
        for spot in range(layers):
            layer = layers - 1 - spot if turn == 0 else spot
            for core in range(2):
                order.append((layer * 4 + side * 2 + core) * 2 + part)
    return order


def ring_scatter(value):
    order = around_order(0) + around_order(1)
    return lax.psum_scatter(
        value,
        ("dp", "mp"),
        scatter_dimension=0,
        tiled=True,
        axis_index_groups=[order],
    )


def ring_gather(piece):
    return lax.all_gather(
        piece,
        ("dp", "mp"),
        axis=0,
        tiled=True,
        axis_index_groups=[around_order(0), around_order(1)],
    )


def gather_steps(shard, order, peek=None, after=None):
    bits = dp_bits()
    value = shard.reshape((1,) * (bits + 1) + shard.shape)
    seen = None
    for turn, stage in enumerate(order):
        axis = 0 if stage is None else bits - stage
        other = swap(value, stage)
        bit = my_bit(stage)
        if turn == peek:
            seen = value
        if turn == 3 and after is not None:
            value = value + after
        value = jnp.concatenate(
            [jnp.where(bit == 0, value, other), jnp.where(bit == 0, other, value)], axis=axis
        )
    value = value.reshape(2, -1, shard.shape[1])
    return value if peek is None else (value, seen)


def gather_y_last():
    return list(range(dp_bits() - 1, 1, -1)) + [None, 1, 0]


def gather_x_last():
    return list(range(dp_bits() - 1, 1, -1)) + [1, None, 0]


def spread_all(value):
    for stage in [0, 1, None] + list(range(2, dp_bits())):
        value = value + swap(value, stage)
    return value


def reduce_table(value):
    stages = [0, None] + list(range(1, dp_bits()))
    for stage in stages:
        mine = my_bit(stage)
        value = take_half(value, mine) + swap(take_half(value, 1 - mine), stage)
    for stage in reversed(stages):
        value = join(value, swap(value, stage), my_bit(stage))
    return value


def gather_small(shard):
    bits = dp_bits()
    value = shard[None]
    for bit in range(bits):
        value = join(value, swap(value, bit), my_bit(bit))
    return value.reshape((-1,) + shard.shape[1:])


def gather_weight(shard):
    return lax.all_gather(shard, ("mp", "dp"), axis=0, tiled=True).reshape(
        lax.axis_size("mp"), -1, shard.shape[1]
    )


def rms_back(hidden, gain, grad):
    inv = lax.rsqrt(jnp.mean(hidden * hidden, axis=-1, keepdims=True) + 1e-05)
    weighted = grad * gain
    mean = jnp.mean(hidden * weighted, axis=-1, keepdims=True)
    d_gain = jnp.sum(hidden * inv * grad, axis=0)
    return inv * weighted - hidden * (inv * inv * inv * mean), d_gain


def in_groups(per_head, groups):
    length = per_head.shape[0]
    return per_head.reshape(length, groups, -1).transpose(1, 0, 2)


def wide128(column):
    return jnp.broadcast_to(column, (column.shape[0], 128))


def dot_parts(left, right):
    return lax.dot_general(
        left, right, (((1,), (1,)), ((), ())), preferred_element_type=jnp.float32
    ).transpose(1, 0, 2)


def dot_back(left, right):
    total = dot_nt(left[0], right[0])
    for part in range(1, left.shape[0]):
        total = total + dot_nt(left[part], right[part])
    return total


def on_device_rows(
    byte_ids,
    segment_ids,
    embed_table,
    patch_weight,
    norm1_gain,
    mamba_in,
    mamba_dt,
    mamba_bc,
    conv_x,
    conv_bc,
    dt_bias,
    a_log,
    d_skip,
    gate_gain,
    mamba_out,
    norm2_gain,
    attn_qkv,
    attn_out,
    norm3_gain,
    ffn_in,
    ffn_out,
    d_out,
):
    low = jnp.bfloat16
    parts = lax.axis_size("mp")
    part = lax.axis_index("mp")
    shard = mamba_in.shape[0]
    per_pos = PATCH // parts
    inner_width = mamba_in.shape[2]
    heads_part = mamba_dt.shape[1]
    state = mamba_bc.shape[1] // 2
    lanes = 256
    groups = parts * inner_width // lanes

    def exchange(value):
        own = lax.dynamic_index_in_dim(value, part, 0, keepdims=False)
        other = swap(lax.dynamic_index_in_dim(value, 1 - part, 0, keepdims=False), None)
        return join(own, other, part)

    ids = exchange(byte_ids)
    seg = exchange(segment_ids)
    length = seg.shape[0]

    def both_parts(value):
        own = value
        other = swap(value, None)
        return join(own[None], other[None], part)

    conv_full = jnp.concatenate(list(both_parts(conv_x)), axis=1)
    vectors = both_parts(jnp.concatenate([dt_bias, a_log, d_skip, gate_gain]))
    heads = parts * heads_part
    bias_full, alog_full, skip_full = (
        vectors[:, i * heads_part : (i + 1) * heads_part].reshape(heads) for i in range(3)
    )
    ggain_full = vectors[:, 3 * heads_part :].reshape(parts * inner_width)

    bc_half = lax.dynamic_slice_in_dim(mamba_bc, part * state, state, 1)
    pad = (-heads_part) % 128
    shard_z = mamba_in[:, 0]
    shard_x = jnp.concatenate(
        [mamba_in[:, 1], bc_half, mamba_dt, jnp.zeros((shard, pad), low)], axis=1
    )
    shard_qkv = attn_qkv.reshape(shard, -1)
    shard_mid = jnp.concatenate([mamba_out.T, shard_qkv, attn_out.T], axis=1)
    shard_ffn = jnp.concatenate([ffn_in.reshape(shard, -1), ffn_out.T], axis=1)
    width_in = ffn_in.shape[1] * ffn_in.shape[2]

    table = gather_small(embed_table)
    rows_by_pos = patch_weight.reshape(per_pos, -1, patch_weight.shape[1])
    mapped = lax.dot_general(
        rows_by_pos, table, (((1,), (1,)), ((), ())), preferred_element_type=jnp.float32
    ).astype(low)
    mapped = mapped.transpose(1, 0, 2).reshape(rows_by_pos.shape[2], -1)
    table_ready = table[0, 0] * 0
    posb, remb = spans(seg)
    ids_parts = ids.reshape(length, parts, per_pos).transpose(1, 0, 2)
    prepared = posb[0, 0] + ids_parts[0, 0, 0].astype(jnp.float32)
    prepared = ((prepared + conv_full[0, 0] + ggain_full[0]) * 0).astype(low)
    mapped, early = gather_steps(mapped, gather_y_last(), peek=3, after=prepared)
    early = early.reshape(-1)[0] * 0
    w_z = gather_steps(shard_z + table_ready, gather_x_last())
    w_x = gather_steps(shard_x + table_ready, gather_y_last())
    mapped_ready = mapped[0, 0, 0] * 0
    ready = (w_z[0, 0, 0] + w_x[0, 0, 0]) * 0 + mapped_ready
    w_mid = gather_weight(shard_mid + early)
    w_ffn = gather_weight(shard_ffn + ready)
    width_qkv = shard_qkv.shape[1]

    onehot, resid0 = embed_rows(ids_parts, mapped)

    spots = jnp.arange(length, dtype=jnp.int32)
    pos = posb[:, 0]
    rem = remb[:, 0]

    u1 = rms_apply(resid0, norm1_gain).astype(low)
    gate = part_product(u1, w_z, jnp.float32)
    fed = part_product(u1, w_x, jnp.float32)
    first_dt = inner_width + state
    bc = jnp.concatenate([fed[p, :, inner_width:first_dt] for p in range(parts)], axis=1)
    dtr = jnp.concatenate([fed[p, :, first_dt : first_dt + heads_part] for p in range(parts)], 1)
    bc_act, pull_bc = jax.vjp(
        lambda signal, taps: jax.nn.silu(conv_rows(signal, taps, seg)), bc, conv_bc
    )
    bcs = bc_act.astype(low)
    bs = bcs[:, :state]
    cs = bcs[:, state:]
    steps = jax.nn.softplus(dtr + bias_full)
    rate = -jnp.exp(alog_full)
    lower = (spots[:, None] >= spots[None, :]).astype(jnp.float32)
    cum = lax.dot_general(
        lower, rate * steps, (((1,), (0,)), ((), ())), precision=lax.Precision.HIGHEST
    )
    chunk = spots // BLK
    chunk_first = chunk * BLK
    ends = cum.reshape(length // BLK, BLK, heads)[:, BLK - 1]
    starts = jnp.concatenate([jnp.zeros((1, heads), jnp.float32), ends[:-1]], axis=0)
    start_wide = jnp.repeat(starts, BLK, axis=0)
    end_wide = jnp.repeat(ends, BLK, axis=0)
    carried = (pos > (spots - chunk_first).astype(jnp.float32)) & (chunk > 0)
    carry = jnp.where(carried[:, None], jnp.exp(cum - start_wide), 0.0)
    lasting = rem >= (chunk_first + BLK - 1 - spots).astype(jnp.float32)
    last = jnp.where(lasting[:, None], jnp.exp(end_wide - cum), 0.0)
    cum2 = cum * LOG2E
    cols = jnp.concatenate([steps, cum2, carry, last], axis=1)
    cumt = cum2.T.reshape(groups, -1, length)
    skip_wide = jnp.repeat(skip_full, PM)[None]
    ssm, scaled, states, squares = mix_forward(
        gate, fed, cols, cumt, conv_full, skip_wide, ggain_full[None], posb, bs, cs, bs.T
    )
    factor = lax.rsqrt(jnp.sum(squares, axis=1, keepdims=True) / DIN + 1e-05)
    gain_parts = ggain_full.reshape(parts, 1, inner_width)
    resid1 = part_back(scaled, w_mid, start=resid0, scale=wide128(factor))

    u2 = rms_apply(resid1, norm2_gain).astype(low)
    qkv = part_product(u2, w_mid, low, first=inner_width, columns=width_qkv)
    attended, logs = attn_forward(qkv, posb)
    resid2 = part_back(attended, w_mid, first=width_qkv + inner_width, start=resid1)

    u3 = rms_apply(resid2, norm3_gain).astype(low)
    half = width_in // 2
    gate3, up3, hidden = ffn_forward(u3, w_ffn, half)
    mixed_row = part_back(hidden, w_ffn, first=width_in, start=resid2)

    piece = length // parts
    mine = lax.dynamic_slice_in_dim(mixed_row, part * piece, piece, 0)
    theirs = swap(lax.dynamic_slice_in_dim(mixed_row, (1 - part) * piece, piece, 0), None)
    mixed = join(mine[None], theirs[None], part)

    core = my_bit(0)

    def half_rows(value, which):
        count = value.shape[0] // 2
        return lax.dynamic_slice_in_dim(value, which * count, count, 0)

    def sum_cores(left_t, right, deps=()):
        received = swap(part_product(half_rows(left_t, 1 - core), right, low), 0)
        return part_product(half_rows(left_t, core), right, low, extra=received, deps=deps)

    started = ssm[0, 0, 0] * 0
    ended = hidden[0, 0, 0].astype(jnp.float32) * 0
    cot_own = lax.dynamic_index_in_dim(d_out, part, 0, keepdims=False) + ended
    cot_other = lax.dynamic_index_in_dim(d_out, 1 - part, 0, keepdims=False) + started
    cot = join(cot_own, swap(cot_other, None), part)
    dm3 = cot.astype(low)
    d_gate_up = ffn_backward(dm3, w_ffn, width_in, gate3, up3)
    quarter = d_gate_up.reshape(2 * parts, length, half)
    part_ffn = outer_into(hidden, dm3, 2, width_in, 3 * width_in // 2)
    part_ffn = part_product(u3.T, quarter, low, fold=2, into=part_ffn)
    sum_ffn = ring_scatter(part_ffn.reshape(-1, part_ffn.shape[2]))
    back_u3 = part_back(quarter, w_ffn, deps=[part_ffn])
    back, d_gain3 = rms_back(resid2, norm3_gain, back_u3)
    cot = cot + back

    dm2 = cot.astype(low)
    d_att = part_product(dm2, w_mid, low, first=width_qkv + inner_width)
    part_mid = part_product(
        dm2.T, attended, low, place=inner_width + width_qkv, room=inner_width + width_qkv + width_qkv // 3
    )
    log_rows = jnp.pad(logs[:, :, :4].transpose(0, 2, 1), ((0, 0), (0, 4), (0, 0)))
    d_qkv = attn_backward(
        qkv, attended, d_att, log_rows, remb, []
    )
    part_mid = part_product(u2.T, d_qkv, low, into=part_mid, place=inner_width)
    back, d_gain2 = rms_back(resid1, norm2_gain, part_back(d_qkv, w_mid, first=inner_width, deps=[part_mid]))
    cot = cot + back

    dm1 = cot.astype(low)
    d_gn = part_product(dm1, w_mid, jnp.float32, columns=inner_width)
    part_mid = outer_into(scaled, (cot * factor).astype(low), 1, 0, part_mid.shape[2], into=part_mid)
    sum_mid = ring_scatter(part_mid.reshape(-1, part_mid.shape[2]))
    gated = ssm * gate * sigmoid(gate)
    cross = jnp.sum(jnp.sum(gated * gain_parts * d_gn, axis=2), axis=0)[:, None]
    cross = factor * factor * factor * cross / DIN
    d_z, d_fed, d_cols, sums, d_bs, d_cs = mix_backward(
        gate,
        fed,
        ssm,
        d_gn,
        cols,
        cumt,
        conv_full,
        skip_wide,
        ggain_full[None],
        posb,
        remb,
        wide128(factor),
        wide128(cross),
        bs,
        cs,
        cs.T,
        states,
        [part_mid, sum_ffn],
    )
    d_cum = d_cols[:, :heads]
    d_step = d_cols[:, heads : 2 * heads]
    d_decay = lax.dot_general(
        lower, d_cum, (((0,), (0,)), ((), ())), precision=lax.Precision.HIGHEST
    )
    d_alog = jnp.sum(d_decay * rate * steps, axis=0)
    d_dtr = (d_step + d_decay * rate) * sigmoid(dtr + bias_full)
    d_bias = jnp.sum(d_dtr, axis=0)
    d_bcs = jnp.concatenate([d_bs, d_cs], axis=1).astype(low).astype(jnp.float32)
    d_bc, d_convbc = pull_bc(d_bcs)
    d_rest = jnp.stack(
        [
            jnp.concatenate(
                [
                    d_bc[:, p * state : (p + 1) * state].astype(low),
                    d_dtr[:, p * heads_part : (p + 1) * heads_part].astype(low),
                    jnp.zeros((length, pad), low),
                ],
                axis=1,
            )
            for p in range(parts)
        ]
    )
    d_fed = lax.dynamic_update_slice(d_fed, d_rest, (0, 0, inner_width))
    bits = dp_bits()
    devices = lax.axis_size("dp")
    u1_t = u1.T
    rank = {device: place for place, device in enumerate(ring_order())}
    source = {block_of(device, bits): rank[device] for device in range(devices)}
    u1_t = jnp.concatenate(
        [u1_t[source[b] * shard : (source[b] + 1) * shard] for b in range(devices)], axis=0
    )
    part_z = sum_cores(u1_t, d_z)
    part_x = sum_cores(u1_t, d_fed)
    back_u1 = part_back(d_z, w_z, deps=[part_z, part_x, sum_mid])
    back_u1 = part_back(d_fed, w_x, start=back_u1)
    back, d_gain1 = rms_back(resid0, norm1_gain, back_u1)
    cot = cot + back

    columns = cot.T.astype(low).reshape((2,) * bits + (shard, length))
    columns = columns.transpose(tuple(range(bits - 1, -1, -1)) + (bits, bits + 1))
    grad_ffn = ring_gather(sum_ffn)
    grad_mid = ring_gather(sum_mid)
    counted = sum_cores(columns.reshape(-1, length), onehot, deps=[grad_ffn])
    later = (counted[0, 0, 0].astype(jnp.float32) + mixed_row[0, 0]) * 0
    after_theirs = theirs[0, 0] * 0
    piece_z = sum_stages(part_z, x_first(), [later])
    piece_x = sum_stages(part_x, y_first(), [later, 0.0, 0.0, after_theirs])
    counted = sum_stages(counted, y_first())
    grad_mix = lax.all_gather(
        jnp.concatenate([piece_z, piece_x], axis=1),
        "dp",
        axis=0,
        tiled=True,
        axis_index_groups=[ring_order()],
    )
    first_dt = 2 * inner_width + state
    counted_all = gather_sum(counted, reversed_blocks=False)
    grad_patch = jnp.einsum(
        "vd,cpv->pdc",
        table,
        counted_all.reshape(-1, per_pos, VOCAB),
        preferred_element_type=jnp.float32,
    ).reshape(patch_weight.shape[0], -1)
    grad_table = reduce_table(
        jnp.einsum(
            "cpv,pdc->vd",
            counted.reshape(-1, per_pos, VOCAB),
            rows_by_pos,
            preferred_element_type=jnp.float32,
        )
    )

    taps = conv_x.shape[0]
    small = [
        d_gain1,
        d_gain2,
        d_gain3,
        d_convbc.reshape(-1),
        d_bias,
        d_alog,
        sums[taps].reshape(heads, PM).sum(axis=1),
        sums[taps + 1],
        sums[:taps].reshape(-1),
    ]
    counts = [item.shape[0] for item in small]
    packed = jnp.concatenate(small)
    fill = (-packed.shape[0]) % 1024
    packed = spread_all(jnp.pad(packed, (0, fill)).reshape(-1, 1024)).reshape(-1)
    split = []
    begin = 0
    for count in counts:
        split.append(packed[begin : begin + count])
        begin += count
    d_gain1, d_gain2, d_gain3, d_convbc, d_bias, d_alog, d_skipped, d_ggain, d_convx = split

    def own_half(vector):
        count = vector.shape[-1] // parts
        return lax.dynamic_slice_in_dim(vector, part * count, count, vector.ndim - 1)

    model_width = grad_mix.shape[0]
    wide = jnp.float32
    half_bc = grad_mix[:, 2 * inner_width : 2 * inner_width + state]
    grad_bc = jnp.concatenate(list(both_parts(half_bc)), axis=1).astype(wide)
    return (
        mixed,
        grad_table,
        grad_patch,
        d_gain1,
        unfold(grad_mix, 2, inner_width),
        grad_mix[:, first_dt : first_dt + heads_part].astype(wide),
        grad_bc,
        own_half(d_convx.reshape(taps, -1)),
        d_convbc.reshape(conv_bc.shape),
        own_half(d_bias),
        own_half(d_alog),
        own_half(d_skipped),
        own_half(d_ggain),
        refold(grad_mid, 0, 1, inner_width, 256),
        d_gain2,
        grad_mid[:, inner_width : inner_width + width_qkv]
        .astype(wide)
        .reshape(model_width, attn_qkv.shape[1], -1),
        grad_mid[:, inner_width + width_qkv :].T.astype(wide),
        d_gain3,
        unfold(grad_ffn, ffn_in.shape[1], half),
        refold(grad_ffn, width_in, 2, model_width, 256),
    )


def product(left, right):
    return jnp.dot(left, right, preferred_element_type=jnp.float32)


def product_left(left, right):
    return lax.dot_general(
        left, right, (((0,), (0,)), ((), ())), preferred_element_type=jnp.float32
    )


def product_right(left, right):
    return lax.dot_general(
        left, right, (((1,), (1,)), ((), ())), preferred_element_type=jnp.float32
    )


def rms_apply(hidden, gain):
    return hidden * lax.rsqrt(jnp.mean(hidden * hidden, axis=-1, keepdims=True) + 1e-05) * gain


def conv_rows(signal, weights, seg):
    taps = weights.shape[0]
    total = weights[taps - 1] * signal
    for lag in range(1, taps):
        moved = jnp.concatenate(
            [jnp.zeros((lag, signal.shape[1]), signal.dtype), signal[:-lag]], axis=0
        )
        same = jnp.concatenate([jnp.zeros((lag,), dtype=bool), seg[lag:] == seg[:-lag]], axis=0)
        total = total + weights[taps - 1 - lag] * moved * same[:, None]
    return total


def mixer_local(packed, seg, conv_x, conv_bc, dt_bias, a_log, d_skip):
    length = packed.shape[0]
    width = conv_x.shape[1]
    state = conv_bc.shape[1] // 2
    heads = dt_bias.shape[0]
    gate_part = packed[:, :width]
    xin = packed[:, width : 2 * width]
    bc = packed[:, 2 * width : 2 * width + 2 * state]
    dtr = packed[:, 2 * width + 2 * state :]
    xs = jax.nn.silu(conv_rows(xin, conv_x, seg))
    bcs = jax.nn.silu(conv_rows(bc, conv_bc, seg)).astype(jnp.bfloat16)
    inner = product_right(bcs[:, state:], bcs[:, :state])
    steps = jax.nn.softplus(dtr + dt_bias)
    cumul = jnp.cumsum(-jnp.exp(a_log) * steps, axis=0).T
    spots = jnp.arange(length)
    keep = ((spots[:, None] >= spots[None, :]) & (seg[:, None] == seg[None, :]))[None]
    spread = cumul[:, :, None] - cumul[:, None, :]
    mixing = (jnp.where(keep, jnp.exp(jnp.where(keep, spread, 0.0)), 0.0) * inner[None]).astype(
        jnp.bfloat16
    )
    channels = xs.reshape(length, heads, -1)
    driven = (steps[:, :, None] * channels).astype(jnp.bfloat16)
    moved = jnp.einsum("hts,shp->thp", mixing, driven, preferred_element_type=jnp.float32)
    result = moved + d_skip[None, :, None] * channels
    return result.reshape(length, width) * jax.nn.silu(gate_part)


def attend_local(packed, seg):
    length = packed.shape[0]
    width = packed.shape[1] // 3
    heads = width // HD
    rounded = packed.astype(jnp.bfloat16)
    query = rounded[:, :width].reshape(length, heads, HD)
    keys = rounded[:, width : 2 * width].reshape(length, heads, HD)
    vals = rounded[:, 2 * width :].reshape(length, heads, HD)
    spots = jnp.arange(length)
    keep = ((spots[:, None] >= spots[None, :]) & (seg[:, None] == seg[None, :]))[None]
    scores = jnp.einsum("thd,shd->hts", query, keys, preferred_element_type=jnp.float32) * HD ** (
        -0.5
    )
    scores = jnp.where(keep, scores, -1e30)
    top = jnp.max(scores, axis=-1, keepdims=True)
    weights = jnp.exp(scores - top)
    weights = (weights / jnp.sum(weights, axis=-1, keepdims=True)).astype(jnp.bfloat16)
    result = jnp.einsum("hts,shd->thd", weights, vals, preferred_element_type=jnp.float32)
    return result.reshape(length, width)


def swiglu_local(packed):
    half = packed.shape[1] // 2
    return jax.nn.silu(packed[:, :half]) * packed[:, half:]


def widen(block):
    return lax.all_gather(block, "mp", axis=0, tiled=True)


def narrow(term, count):
    return lax.psum_scatter(
        term(jnp.int32(0), count * lax.axis_size("mp")), "mp", scatter_dimension=0, tiled=True
    )


def widen_grad(block):
    return lax.all_gather(block, "mp", axis=0, tiled=True)


def narrow_grad(term, count):
    return lax.psum_scatter(
        term(jnp.int32(0), count * lax.axis_size("mp")), "mp", scatter_dimension=0, tiled=True
    )


def arrange(full):
    table, patch_rows, w_mix, w_dt, w_bc, w_mout, w_qkv, w_aout, w_ffin, w_ffout = full
    width = w_mix.shape[0]
    w_proj = jnp.concatenate([w_mix.reshape(width, -1), w_bc, w_dt], axis=1)
    return (
        table,
        patch_rows,
        w_proj,
        w_mout,
        w_qkv.reshape(width, -1),
        w_aout,
        w_ffin.reshape(width, -1),
        w_ffout,
    )


def table_terms(onehot, d_embed):
    upper = d_embed.astype(jnp.bfloat16)
    lower = (d_embed - upper.astype(jnp.float32)).astype(jnp.bfloat16)
    first = jnp.einsum("lpv,lpd->vd", onehot, upper, preferred_element_type=jnp.float32)
    return first + jnp.einsum("lpv,lpd->vd", onehot, lower, preferred_element_type=jnp.float32)


def on_device(
    byte_ids,
    segment_ids,
    embed_table,
    patch_weight,
    norm1_gain,
    mamba_in,
    mamba_dt,
    mamba_bc,
    conv_x,
    conv_bc,
    dt_bias,
    a_log,
    d_skip,
    gate_gain,
    mamba_out,
    norm2_gain,
    attn_qkv,
    attn_out,
    norm3_gain,
    ffn_in,
    ffn_out,
    d_out,
):
    parts = lax.axis_size("mp")
    index = lax.axis_index("mp")
    piece = byte_ids.shape[1]
    length = piece * parts
    per_pos = PATCH // parts
    inner_width = mamba_in.shape[2]
    state = mamba_bc.shape[1] // 2
    sharded = (
        embed_table,
        patch_weight,
        mamba_in,
        mamba_dt,
        mamba_bc,
        mamba_out,
        attn_qkv,
        attn_out,
        ffn_in,
        ffn_out,
    )
    fetched = (
        lax.all_gather(sharded[0], "dp", axis=0, tiled=True),
        lax.all_gather(sharded[1], "dp", axis=1, tiled=True),
        lax.all_gather(sharded[2], "dp", axis=0, tiled=True),
        lax.all_gather(sharded[3], "dp", axis=0, tiled=True),
        lax.all_gather(sharded[4], "dp", axis=0, tiled=True),
        lax.all_gather(sharded[5], "dp", axis=1, tiled=True),
        lax.all_gather(sharded[6], "dp", axis=0, tiled=True),
        lax.all_gather(sharded[7], "dp", axis=1, tiled=True),
        lax.all_gather(sharded[8], "dp", axis=0, tiled=True),
        lax.all_gather(sharded[9], "dp", axis=1, tiled=True),
    )
    table, patch_rows, w_proj, w_mout, w_qkv, w_aout, w_ffin, w_ffout = arrange(fetched)
    kept = []
    outputs = []
    for batch in range(MB):
        ids_all, seg_all = (
            lax.all_gather(byte_ids[batch], "mp", axis=0, tiled=True),
            lax.all_gather(segment_ids[batch], "mp", axis=0, tiled=True),
        )
        local_ids = lax.dynamic_slice_in_dim(ids_all, index * per_pos, per_pos, 1)
        onehot = (
            local_ids[:, :, None] == jnp.arange(VOCAB, dtype=jnp.int32)[None, None, :]
        ).astype(jnp.bfloat16)
        embedded = jnp.einsum("lpv,vd->lpd", onehot, table, preferred_element_type=jnp.float32)
        embedded = embedded.astype(jnp.bfloat16).reshape(length, -1)
        resid0 = narrow(lambda start, count: product(embedded, patch_rows), piece)
        wide1 = widen(rms_apply(resid0, norm1_gain).astype(jnp.bfloat16))
        proj = product(wide1, w_proj)
        gated = mixer_local(proj, seg_all, conv_x, conv_bc, dt_bias, a_log, d_skip)
        total = lax.psum(jnp.sum(gated * gated, axis=1), "mp")
        factor = lax.rsqrt(total / DIN + 1e-05)[:, None]
        gnormed = (gated * factor * gate_gain).astype(jnp.bfloat16)
        resid1 = resid0 + narrow(lambda start, count: product(gnormed, w_mout), piece)
        wide2 = widen(rms_apply(resid1, norm2_gain).astype(jnp.bfloat16))
        qkv = product(wide2, w_qkv)
        attended = attend_local(qkv, seg_all).astype(jnp.bfloat16)
        resid2 = resid1 + narrow(lambda start, count: product(attended, w_aout), piece)
        wide3 = widen(rms_apply(resid2, norm3_gain).astype(jnp.bfloat16))
        gate_up = product(wide3, w_ffin)
        hidden = swiglu_local(gate_up).astype(jnp.bfloat16)
        outputs.append(resid2 + narrow(lambda start, count: product(hidden, w_ffout), piece))
        kept.append(
            (
                seg_all,
                onehot,
                embedded,
                resid0,
                resid1,
                resid2,
                wide1,
                proj,
                gated,
                factor,
                gnormed,
                wide2,
                qkv,
                attended,
                wide3,
                gate_up,
                hidden,
            )
        )
    mixed = jnp.stack(outputs, axis=0)
    grad_resid = [d_out[batch] for batch in range(MB)]
    acc_ffin = jnp.zeros(w_ffin.shape, jnp.float32)
    acc_ffout = jnp.zeros(w_ffout.shape, jnp.float32)
    acc_gain3 = jnp.zeros(norm3_gain.shape, jnp.float32)
    for batch in range(MB):
        saved = kept[batch]
        wide_grad = widen_grad(grad_resid[batch].astype(jnp.bfloat16))
        acc_ffout = acc_ffout + product_left(saved[16], wide_grad)
        d_hidden = product_right(wide_grad, w_ffout)
        d_gate_up = jax.vjp(swiglu_local, saved[15])[1](d_hidden)[0].astype(jnp.bfloat16)
        acc_ffin = acc_ffin + product_left(saved[14], d_gate_up)
        d_norm = narrow_grad(lambda start, count: product_right(d_gate_up, w_ffin), piece)
        d_back, d_gain = jax.vjp(rms_apply, saved[5], norm3_gain)[1](d_norm)
        grad_resid[batch] = grad_resid[batch] + d_back
        acc_gain3 = acc_gain3 + d_gain
    acc_qkv = jnp.zeros(w_qkv.shape, jnp.float32)
    acc_aout = jnp.zeros(w_aout.shape, jnp.float32)
    acc_gain2 = jnp.zeros(norm2_gain.shape, jnp.float32)
    for batch in range(MB):
        saved = kept[batch]
        seg_all = saved[0]
        wide_grad = widen_grad(grad_resid[batch].astype(jnp.bfloat16))
        acc_aout = acc_aout + product_left(saved[13], wide_grad)
        d_att = product_right(wide_grad, w_aout)
        d_qkv = jax.vjp(lambda packed: attend_local(packed, seg_all), saved[12])[1](d_att)[0]
        d_qkv = d_qkv.astype(jnp.bfloat16)
        acc_qkv = acc_qkv + product_left(saved[11], d_qkv)
        d_norm = narrow_grad(lambda start, count: product_right(d_qkv, w_qkv), piece)
        d_back, d_gain = jax.vjp(rms_apply, saved[4], norm2_gain)[1](d_norm)
        grad_resid[batch] = grad_resid[batch] + d_back
        acc_gain2 = acc_gain2 + d_gain
    acc_proj = jnp.zeros(w_proj.shape, jnp.float32)
    acc_mout = jnp.zeros(w_mout.shape, jnp.float32)
    acc_ggain = jnp.zeros(gate_gain.shape, jnp.float32)
    acc_convx = jnp.zeros(conv_x.shape, jnp.float32)
    acc_convbc = jnp.zeros(conv_bc.shape, jnp.float32)
    acc_bias = jnp.zeros(dt_bias.shape, jnp.float32)
    acc_alog = jnp.zeros(a_log.shape, jnp.float32)
    acc_skip = jnp.zeros(d_skip.shape, jnp.float32)
    acc_gain1 = jnp.zeros(norm1_gain.shape, jnp.float32)
    for batch in range(MB):
        saved = kept[batch]
        seg_all = saved[0]
        gated = saved[8]
        factor = saved[9]
        wide_grad = widen_grad(grad_resid[batch].astype(jnp.bfloat16))
        acc_mout = acc_mout + product_left(saved[10], wide_grad)
        d_gn = product_right(wide_grad, w_mout)
        weighted = d_gn * gate_gain
        acc_ggain = acc_ggain + jnp.sum(gated * factor * d_gn, axis=0)
        cross = lax.psum(jnp.sum(gated * weighted, axis=1), "mp")
        d_gated = weighted * factor - gated * factor**3 * (cross / DIN)[:, None]
        pull = jax.vjp(
            lambda packed, taps_x, taps_bc, bias, decay, skip: mixer_local(
                packed, seg_all, taps_x, taps_bc, bias, decay, skip
            ),
            saved[7],
            conv_x,
            conv_bc,
            dt_bias,
            a_log,
            d_skip,
        )[1]
        d_proj, d_convx, d_convbc, d_bias, d_alog, d_skipped = pull(d_gated)
        d_proj = d_proj.astype(jnp.bfloat16)
        acc_convx = acc_convx + d_convx
        acc_convbc = acc_convbc + d_convbc
        acc_bias = acc_bias + d_bias
        acc_alog = acc_alog + d_alog
        acc_skip = acc_skip + d_skipped
        acc_proj = acc_proj + product_left(saved[6], d_proj)
        d_norm = narrow_grad(lambda start, count: product_right(d_proj, w_proj), piece)
        d_back, d_gain = jax.vjp(rms_apply, saved[3], norm1_gain)[1](d_norm)
        grad_resid[batch] = grad_resid[batch] + d_back
        acc_gain1 = acc_gain1 + d_gain
    acc_patch = jnp.zeros(patch_rows.shape, jnp.float32)
    acc_table = jnp.zeros(table.shape, jnp.float32)
    for batch in range(MB):
        saved = kept[batch]
        wide_grad = widen_grad(grad_resid[batch].astype(jnp.bfloat16))
        acc_patch = acc_patch + product_left(saved[2], wide_grad)
        d_embed = product_right(wide_grad, patch_rows).reshape(length, per_pos, -1)
        acc_table = acc_table + table_terms(saved[1], d_embed)
    model_width = w_proj.shape[0]
    grad_mix = acc_proj[:, : 2 * inner_width].reshape(model_width, 2, inner_width)
    grad_bc = acc_proj[:, 2 * inner_width : 2 * inner_width + 2 * state]
    grad_dt = acc_proj[:, 2 * inner_width + 2 * state :]
    (
        acc_patch,
        grad_mix,
        grad_dt,
        acc_mout,
        acc_convx,
        acc_bias,
        acc_alog,
        acc_skip,
        acc_ggain,
        acc_qkv,
        acc_aout,
        acc_ffin,
        acc_ffout,
    ) = lax.psum(
        (
            acc_patch,
            grad_mix,
            grad_dt,
            acc_mout,
            acc_convx,
            acc_bias,
            acc_alog,
            acc_skip,
            acc_ggain,
            acc_qkv,
            acc_aout,
            acc_ffin,
            acc_ffout,
        ),
        "dp",
    )
    acc_table, grad_bc, acc_convbc, acc_gain1, acc_gain2, acc_gain3 = lax.psum(
        (acc_table, grad_bc, acc_convbc, acc_gain1, acc_gain2, acc_gain3), ("dp", "mp")
    )
    grad_qkv = acc_qkv.reshape(model_width, 3, -1)
    grad_ffin = acc_ffin.reshape(model_width, 2, -1)
    return (
        mixed,
        acc_table,
        acc_patch,
        acc_gain1,
        grad_mix,
        grad_dt,
        grad_bc,
        acc_convx,
        acc_convbc,
        acc_bias,
        acc_alog,
        acc_skip,
        acc_ggain,
        acc_mout,
        acc_gain2,
        grad_qkv,
        acc_aout,
        acc_gain3,
        grad_ffin,
        acc_ffout,
    )


def solution(mesh):
    sizes = dict(mesh.shape)
    by_rows = sizes["mp"] == MB and sizes["dp"] == 16
    return jax.shard_map(
        on_device_rows if by_rows else on_device,
        mesh=mesh,
        in_specs=(
            P(None, ("dp", "mp"), None),
            P(None, ("dp", "mp")),
            P("dp", None),
            P("mp", "dp"),
            P(),
            P("dp", None, "mp"),
            P("dp", "mp"),
            P("dp", None),
            P(None, "mp"),
            P(),
            P("mp"),
            P("mp"),
            P("mp"),
            P("mp"),
            P("mp", "dp"),
            P(),
            P("dp", None, "mp"),
            P("mp", "dp"),
            P(),
            P("dp", None, "mp"),
            P("mp", "dp"),
            P(None, ("dp", "mp"), None),
        ),
        out_specs=(
            P(None, ("dp", "mp"), None),
            P(),
            P("mp", None),
            P(),
            P(None, None, "mp"),
            P(None, "mp"),
            P(),
            P(None, "mp"),
            P(),
            P("mp"),
            P("mp"),
            P("mp"),
            P("mp"),
            P("mp", None),
            P(),
            P(None, None, "mp"),
            P("mp", None),
            P(),
            P(None, None, "mp"),
            P("mp", None),
        ),
        check_vma=False,
    )
```

```python
import jax
import jax.numpy as jnp
from jax import lax
from jax.experimental import pallas as pl
from jax.experimental.pallas import tpu as pltpu
from jax.sharding import PartitionSpec as P

PATCH = 8
VOCAB = 256
HD = 64
MB = 2
DIN = 2048
PM = 64
TAPS = 4
VMEM_LIMIT = 56 * 1024 * 1024
LOG2E = 1.4426950408889634
BLK = 256


def dot_nn(a, b):
    return lax.dot_general(a, b, (((1,), (0,)), ((), ())), preferred_element_type=jnp.float32)


def dot_nt(a, b):
    return lax.dot_general(a, b, (((1,), (1,)), ((), ())), preferred_element_type=jnp.float32)


def dot_tn(a, b):
    return lax.dot_general(a, b, (((0,), (0,)), ((), ())), preferred_element_type=jnp.float32)


def sigmoid(v):
    return 0.5 * jnp.tanh(0.5 * v) + 0.5


def head_masks(width, size):
    lane = lax.broadcasted_iota(jnp.int32, (1, width), 1) // size
    return [lane == h for h in range(width // size)]


def spread_heads(cols, first, masks, width):
    rows = cols.shape[0]
    out = jnp.broadcast_to(cols[:, first : first + 1], (rows, width))
    for h in range(1, len(masks)):
        piece = jnp.broadcast_to(cols[:, first + h : first + h + 1], (rows, width))
        out = jnp.where(masks[h], piece, out)
    return out


def two_parts(v):
    upper = v.astype(jnp.bfloat16)
    return upper, (v - upper.astype(jnp.float32)).astype(jnp.bfloat16)


def attn_fwd_kernel(q_ref, k_ref, v_ref, pos_ref, o_ref, lse_ref, bias_ref):
    length = pos_ref.shape[0]
    width = q_ref.shape[2]

    @pl.when(pl.program_id(0) == 0)
    def _():
        for i in range(length // BLK):
            rows = pl.ds(i * BLK, BLK)
            n = (i + 1) * BLK
            spot = i * BLK + lax.broadcasted_iota(jnp.int32, (BLK, n), 0)
            other = lax.broadcasted_iota(jnp.int32, (BLK, n), 1)
            gap = (spot - other).astype(jnp.float32)
            keep = (gap >= 0.0) & (gap <= pos_ref[rows, 0:1])
            bias_ref[rows, 0:n] = jnp.where(keep, 0.0, -1e30)

    masks = head_masks(width, HD)
    spots = lax.broadcasted_iota(jnp.int32, (1, 128), 1)
    for i in range(length // BLK):
        rows = pl.ds(i * BLK, BLK)
        n = (i + 1) * BLK
        query = q_ref[0, rows, :] * jnp.bfloat16(HD**-0.5)
        keys = k_ref[0, 0:n, :]
        vals = v_ref[0, 0:n, :]
        bias = bias_ref[rows, 0:n]
        total = jnp.zeros((BLK, width), jnp.float32)
        logs = jnp.zeros((BLK, 128), jnp.float32)
        for h, mask in enumerate(masks):
            scores = dot_nt(jnp.where(mask, query, jnp.bfloat16(0)), keys) + bias
            top = jnp.max(scores, axis=1, keepdims=True)
            weights = jnp.exp(scores - top)
            norm = jnp.sum(weights, axis=1, keepdims=True)
            probs = (weights * (1.0 / norm)).astype(jnp.bfloat16)
            total = jnp.where(mask, dot_nn(probs, vals), total)
            logs = jnp.where(spots == h, top + jnp.log(norm), logs)
        o_ref[0, rows, :] = total.astype(jnp.bfloat16)
        lse_ref[0, rows, :] = logs


def attn_forward(qkv, posb):
    parts, length, width3 = qkv.shape
    width = width3 // 3
    lanes = min(256, width)
    per = width // lanes
    groups = parts * per
    block = (1, length, lanes)
    return pl.pallas_call(
        attn_fwd_kernel,
        grid=(groups,),
        in_specs=[
            pl.BlockSpec(block, lambda g: (g // per, 0, g % per)),
            pl.BlockSpec(block, lambda g: (g // per, 0, per + g % per)),
            pl.BlockSpec(block, lambda g: (g // per, 0, 2 * per + g % per)),
            pl.BlockSpec((length, 128), lambda g: (0, 0)),
        ],
        out_specs=[
            pl.BlockSpec(block, lambda g: (g // per, 0, g % per)),
            pl.BlockSpec((1, length, 128), lambda g: (g, 0, 0)),
        ],
        out_shape=[
            jax.ShapeDtypeStruct((parts, length, width), jnp.bfloat16),
            jax.ShapeDtypeStruct((groups, length, 128), jnp.float32),
        ],
        scratch_shapes=[pltpu.VMEM((length, length), jnp.float32)],
        compiler_params=pltpu.CompilerParams(vmem_limit_bytes=VMEM_LIMIT),
        cost_estimate=pl.CostEstimate(
            flops=30_000_000_000, bytes_accessed=10_000_000, transcendentals=0
        ),
        name="attn_fwd",
    )(qkv, qkv, qkv, posb)


def attn_bwd_kernel(
    q_ref, k_ref, v_ref, o_ref, do_ref, lse_ref, rem_ref, *others
):
    out_ref, bias_ref, dk_ref, dv_ref = others[-4:]
    length = rem_ref.shape[0]
    width = q_ref.shape[2]
    per = out_ref.shape[2] // (3 * width)
    step = pl.program_id(0)

    @pl.when(step == 0)
    def _():
        for i in range(length // BLK):
            cols = pl.ds(i * BLK, BLK)
            n = (i + 1) * BLK
            other = lax.broadcasted_iota(jnp.int32, (n, BLK), 0)
            spot = i * BLK + lax.broadcasted_iota(jnp.int32, (n, BLK), 1)
            gap = (spot - other).astype(jnp.float32)
            keep = (gap >= 0.0) & (gap <= rem_ref[0:n, 0:1])
            bias_ref[0:n, cols] = jnp.where(keep, 0.0, -1e30)

    masks = head_masks(width, HD)
    heads = len(masks)
    rows8 = lax.broadcasted_iota(jnp.int32, (8, width), 0)
    lane8 = lax.broadcasted_iota(jnp.int32, (8, width), 1) // HD
    picks = jnp.where(rows8 == lane8, 1.0, 0.0).astype(jnp.bfloat16)
    scale = jnp.bfloat16(HD**-0.5)
    zero = jnp.bfloat16(0)
    offset = pl.multiple_of((step % per) * width, width)
    nblocks = length // BLK
    for i in reversed(range(nblocks)):
        rows = pl.ds(i * BLK, BLK)
        n = (i + 1) * BLK
        query = q_ref[0, rows, :] * scale
        grad = do_ref[0, rows, :]
        prod = grad.astype(jnp.float32) * o_ref[0, rows, :].astype(jnp.float32)
        upper, lower = two_parts(prod)
        delta = dot_nt(picks, upper) + dot_nt(picks, lower)
        keys = k_ref[0, 0:n, :]
        vals = v_ref[0, 0:n, :]
        bias = bias_ref[0:n, rows]
        d_query = jnp.zeros((BLK, width), jnp.float32)
        d_keys = jnp.zeros((n, width), jnp.float32)
        d_vals = jnp.zeros((n, width), jnp.float32)
        for h, mask in enumerate(masks):
            q_head = jnp.where(mask, query, zero)
            g_head = jnp.where(mask, grad, zero)
            probs = jnp.exp(dot_nt(keys, q_head) + bias - lse_ref[0, h : h + 1, rows])
            d_probs = dot_nt(vals, g_head)
            d_scores = (probs * (d_probs - delta[h : h + 1, :])).astype(jnp.bfloat16)
            d_vals = d_vals + dot_nn(probs.astype(jnp.bfloat16), g_head)
            d_keys = d_keys + dot_nn(d_scores, q_head)
            d_query = jnp.where(mask, dot_tn(d_scores, keys), d_query)
        out_ref[0, rows, pl.ds(offset, width)] = (d_query * (HD**-0.5)).astype(jnp.bfloat16)
        if i == nblocks - 1:
            dk_ref[...] = d_keys
            dv_ref[...] = d_vals
        else:
            dk_ref[0:n, :] += d_keys
            dv_ref[0:n, :] += d_vals
    out_ref[0, :, pl.ds(per * width + offset, width)] = dk_ref[...].astype(jnp.bfloat16)
    out_ref[0, :, pl.ds(2 * per * width + offset, width)] = dv_ref[...].astype(jnp.bfloat16)


def attn_backward(qkv, attended, d_att, lse_rows, remb, deps):
    parts, length, width3 = qkv.shape
    width = width3 // 3
    lanes = min(256, width)
    per = width // lanes
    groups = parts * per
    block = (1, length, lanes)
    return pl.pallas_call(
        attn_bwd_kernel,
        grid=(groups,),
        in_specs=[
            pl.BlockSpec(block, lambda g: (g // per, 0, g % per)),
            pl.BlockSpec(block, lambda g: (g // per, 0, per + g % per)),
            pl.BlockSpec(block, lambda g: (g // per, 0, 2 * per + g % per)),
            pl.BlockSpec(block, lambda g: (g // per, 0, g % per)),
            pl.BlockSpec(block, lambda g: (g // per, 0, g % per)),
            pl.BlockSpec((1, 8, length), lambda g: (g, 0, 0)),
            pl.BlockSpec((length, 128), lambda g: (0, 0)),
        ]
        + [pl.BlockSpec(memory_space=pl.ANY)] * len(deps),
        out_specs=pl.BlockSpec((1, length, width3), lambda g: (g // per, 0, 0)),
        out_shape=jax.ShapeDtypeStruct(qkv.shape, jnp.bfloat16),
        scratch_shapes=[
            pltpu.VMEM((length, length), jnp.float32),
            pltpu.VMEM((length, lanes), jnp.float32),
            pltpu.VMEM((length, lanes), jnp.float32),
        ],
        compiler_params=pltpu.CompilerParams(vmem_limit_bytes=VMEM_LIMIT),
        cost_estimate=pl.CostEstimate(
            flops=70_000_000_000, bytes_accessed=20_000_000, transcendentals=0
        ),
        name="attn_bwd",
    )(qkv, qkv, qkv, attended, d_att, lse_rows, remb, *deps)


def conv_moved(ref, part, rows, first, pos):
    width = ref.shape[2]
    if first == 0:
        before = jnp.zeros((8, width), jnp.float32)
    else:
        before = ref[part, pl.ds(first - 8, 8), :]
    signal = jnp.concatenate([before, ref[part, pl.ds(first, rows), :]], axis=0)
    moved = [signal[8:]]
    for lag in range(1, TAPS):
        shifted = pltpu.roll(signal, lag, 0)[8:]
        moved.append(jnp.where(pos >= lag, shifted, 0.0))
    return moved


def wide_rows(ref, first, rows, width):
    block = ref[pl.ds(first, rows), :]
    return jnp.concatenate([block] * (width // block.shape[1]), axis=1)


def mix_fwd_kernel(
    z_ref, x_ref, cols_ref, cumt_ref, conv_ref, skip_ref, gain_ref, pos_ref, bs_ref, cs_ref,
    bst_ref, ssm_ref, scaled_ref, state_ref, ssq_ref, inner_ref,
):
    length = pos_ref.shape[0]
    width = x_ref.shape[2]
    step = pl.program_id(0)
    chunks = length // BLK

    @pl.when(step == 0)
    def _():
        for k in range(chunks):
            rows = pl.ds(k * BLK, BLK)
            spot = lax.broadcasted_iota(jnp.int32, (BLK, BLK), 0)
            other = lax.broadcasted_iota(jnp.int32, (BLK, BLK), 1)
            gap = (spot - other).astype(jnp.float32)
            keep = (gap >= 0.0) & (gap <= pos_ref[rows, 0:1])
            inner_ref[k] = jnp.where(keep, dot_nt(cs_ref[rows, :], bs_ref[rows, :]), 0.0)

    masks = head_masks(width, PM)
    heads = len(masks)
    span = cols_ref.shape[1] // 4
    turn = lax.rem(4 * span - step * heads, 4 * span)
    state = jnp.zeros((bs_ref.shape[1], width), jnp.float32)
    for k in range(chunks):
        first = k * BLK
        rows = pl.ds(first, BLK)
        pos = wide_rows(pos_ref, first, BLK, width)
        moved = conv_moved(x_ref, 0, BLK, first, pos)
        pre = conv_ref[TAPS - 1 : TAPS, :] * moved[0]
        for lag in range(1, TAPS):
            pre = pre + conv_ref[TAPS - 1 - lag : TAPS - lag, :] * moved[lag]
        xs = pre * sigmoid(pre)
        cols = pltpu.roll(cols_ref[rows, :], turn, 1)
        driven = (spread_heads(cols, 0, masks, width) * xs).astype(jnp.bfloat16)
        out = skip_ref[...] * xs
        inner = inner_ref[k]
        for h, mask in enumerate(masks):
            gap = cols[:, span + h : span + h + 1] - cumt_ref[0, h : h + 1, rows]
            mixing = (jnp.exp2(jnp.minimum(gap, 0.0)) * inner).astype(jnp.bfloat16)
            out = out + dot_nn(mixing, jnp.where(mask, driven, jnp.bfloat16(0)))
        state_bf, state_rest = two_parts(state)
        state_ref[k] = state_bf
        if k > 0:
            carry = spread_heads(cols, 2 * span, masks, width)
            recalled = dot_nn(cs_ref[rows, :], state_bf) + dot_nn(cs_ref[rows, :], state_rest)
            out = out + carry * recalled
        if k < chunks - 1:
            last = spread_heads(cols, 3 * span, masks, width)
            fed, fed_rest = two_parts(last * driven.astype(jnp.float32))
            fresh = dot_nn(bst_ref[:, rows], fed) + dot_nn(bst_ref[:, rows], fed_rest)
            if k > 0:
                fresh = fresh + carry[BLK - 1 : BLK, :] * state
            state = fresh
        ssm_ref[0, rows, :] = out
        gate = z_ref[0, rows, :]
        gated = out * gate * sigmoid(gate)
        scaled_ref[0, rows, :] = (gated * gain_ref[...]).astype(jnp.bfloat16)
        square = gated * gated
        total = square[:, 0:128]
        for lane in range(128, width, 128):
            total = total + square[:, lane : lane + 128]

        @pl.when(step == 0)
        def _():
            ssq_ref[rows, :] = total

        @pl.when(step > 0)
        def _():
            ssq_ref[rows, :] += total


def mix_forward(z, x, cols, cumt, conv, skip, gain, posb, bs, cs, bst):
    parts, length, inner_width = z.shape
    state = bs.shape[1]
    lanes = 256
    per = inner_width // lanes
    groups = parts * per
    block = (1, length, lanes)
    whole = lambda g: (0, 0)
    return pl.pallas_call(
        mix_fwd_kernel,
        grid=(groups,),
        in_specs=[
            pl.BlockSpec(block, lambda g: (g // per, 0, g % per)),
            pl.BlockSpec(block, lambda g: (g // per, 0, g % per)),
            pl.BlockSpec(cols.shape, whole),
            pl.BlockSpec((1,) + cumt.shape[1:], lambda g: (g, 0, 0)),
            pl.BlockSpec((TAPS, lanes), lambda g: (0, g)),
            pl.BlockSpec((1, lanes), lambda g: (0, g)),
            pl.BlockSpec((1, lanes), lambda g: (0, g)),
            pl.BlockSpec((length, 128), whole),
            pl.BlockSpec((length, state), whole),
            pl.BlockSpec((length, state), whole),
            pl.BlockSpec((state, length), whole),
        ],
        out_specs=[
            pl.BlockSpec(block, lambda g: (g // per, 0, g % per)),
            pl.BlockSpec(block, lambda g: (g // per, 0, g % per)),
            pl.BlockSpec((length // BLK, state, lanes), lambda g: (0, 0, g)),
            pl.BlockSpec((length, 128), whole),
        ],
        out_shape=[
            jax.ShapeDtypeStruct((parts, length, inner_width), jnp.float32),
            jax.ShapeDtypeStruct((parts, length, inner_width), jnp.bfloat16),
            jax.ShapeDtypeStruct((length // BLK, state, parts * inner_width), jnp.bfloat16),
            jax.ShapeDtypeStruct((length, 128), jnp.float32),
        ],
        scratch_shapes=[pltpu.VMEM((length // BLK, BLK, BLK), jnp.float32)],
        compiler_params=pltpu.CompilerParams(vmem_limit_bytes=VMEM_LIMIT),
        cost_estimate=pl.CostEstimate(
            flops=20_000_000_000, bytes_accessed=30_000_000, transcendentals=0
        ),
        name="mix_fwd",
    )(z, x, cols, cumt, conv, skip, gain, posb, bs, cs, bst)


def mix_bwd_kernel(
    z_ref, x_ref, ssm_ref, dgn_ref, cols_ref, cumt_ref, conv_ref, skip_ref, gain_ref,
    pos_ref, rem_ref, rg_ref, cross_ref, bs_ref, cs_ref, cst_ref, state_ref, *others,
):
    dz_ref, dx_ref, dcols_ref, sums_ref, dbs_ref, dcs_ref = others[-9:-3]
    inner_ref, dinner_ref, dpre_ref = others[-3:]
    length = pos_ref.shape[0]
    width = x_ref.shape[2]
    step = pl.program_id(0)
    chunks = length // BLK
    spot = lax.broadcasted_iota(jnp.int32, (BLK, BLK), 1)
    other = lax.broadcasted_iota(jnp.int32, (BLK, BLK), 0)
    gap = (spot - other).astype(jnp.float32)

    @pl.when(step == 0)
    def _():
        for k in range(chunks):
            rows = pl.ds(k * BLK, BLK)
            keep = (gap >= 0.0) & (gap <= rem_ref[rows, 0:1])
            inner_ref[k] = jnp.where(keep, dot_nt(bs_ref[rows, :], cs_ref[rows, :]), 0.0)
        dinner_ref[...] = jnp.zeros(dinner_ref.shape, jnp.float32)
        dbs_ref[...] = jnp.zeros(dbs_ref.shape, jnp.float32)
        dcs_ref[...] = jnp.zeros(dcs_ref.shape, jnp.float32)
        dcols_ref[...] = jnp.zeros(dcols_ref.shape, jnp.float32)

    masks = head_masks(width, PM)
    heads = len(masks)
    zero = jnp.bfloat16(0)
    head_of = lax.broadcasted_iota(jnp.int32, (width, 128), 0) // PM
    lane_of = lax.broadcasted_iota(jnp.int32, (width, 128), 1)
    span = cols_ref.shape[1] // 4
    turn = lax.rem(4 * span - step * heads, 4 * span)
    lane_of = lane_of - step * heads
    pick_cum = jnp.where(head_of == lane_of, 1.0, 0.0).astype(jnp.bfloat16)
    pick_step = jnp.where(head_of + span == lane_of, 1.0, 0.0).astype(jnp.bfloat16)
    dpre_ref[pl.ds(length, 8), :] = jnp.zeros((8, width), jnp.float32)
    sums_ref[...] = jnp.zeros(sums_ref.shape, jnp.float32)
    d_state = jnp.zeros((bs_ref.shape[1], width), jnp.float32)
    skip = skip_ref[...]
    gain = gain_ref[...]
    for k in reversed(range(chunks)):
        first = k * BLK
        rows = pl.ds(first, BLK)
        pos = wide_rows(pos_ref, first, BLK, width)
        moved = conv_moved(x_ref, 0, BLK, first, pos)
        pre = conv_ref[TAPS - 1 : TAPS, :] * moved[0]
        for lag in range(1, TAPS):
            pre = pre + conv_ref[TAPS - 1 - lag : TAPS - lag, :] * moved[lag]
        sig = sigmoid(pre)
        xs = pre * sig
        cols = pltpu.roll(cols_ref[rows, :], turn, 1)
        step_wide = spread_heads(cols, 0, masks, width)
        driven = (step_wide * xs).astype(jnp.bfloat16)
        gate = z_ref[0, rows, :]
        sig_z = sigmoid(gate)
        silu_z = gate * sig_z
        ssm = ssm_ref[0, rows, :]
        gated = ssm * silu_z
        d_gn = dgn_ref[0, rows, :]
        rg = wide_rows(rg_ref, first, BLK, width)
        cross = wide_rows(cross_ref, first, BLK, width)
        scaled = rg * d_gn
        d_gated = gain * scaled - gated * cross
        sums_ref[5:6, :] += jnp.sum(gated * scaled, axis=0, keepdims=True)
        dz_ref[0, rows, :] = (d_gated * ssm * (sig_z + silu_z * (1.0 - sig_z))).astype(jnp.bfloat16)
        d_out = d_gated * silu_z
        d_low = d_out.astype(jnp.bfloat16)
        sums_ref[4:5, :] += jnp.sum(d_out * xs, axis=0, keepdims=True)
        inner = inner_ref[k]
        d_inner = dinner_ref[k]
        d_driven = jnp.zeros((BLK, width), jnp.float32)
        for h, mask in enumerate(masks):
            gap_h = cumt_ref[0, h : h + 1, rows] - cols[:, span + h : span + h + 1]
            decay = jnp.exp2(jnp.minimum(gap_h, 0.0))
            mixing = (decay * inner).astype(jnp.bfloat16)
            d_driven = d_driven + dot_nn(mixing, jnp.where(mask, d_low, zero))
            d_inner = d_inner + decay * dot_nt(jnp.where(mask, driven, zero), d_low)
        dinner_ref[k] = d_inner
        if k > 0:
            carry = spread_heads(cols, 2 * span, masks, width)
            carried, carried_rest = two_parts(carry * d_low.astype(jnp.float32))
            dcs_ref[rows, :] += dot_nt(carried, state_ref[k])
        if k < chunks - 1:
            last = spread_heads(cols, 3 * span, masks, width)
            fed = (last * driven.astype(jnp.float32)).astype(jnp.bfloat16)
            d_state_bf, d_state_rest = two_parts(d_state)
            dbs_ref[rows, :] += dot_nt(fed, d_state_bf)
            recalled = dot_nn(bs_ref[rows, :], d_state_bf) + dot_nn(bs_ref[rows, :], d_state_rest)
            d_driven = d_driven + last * recalled
        if k > 0:
            fresh = dot_nn(cst_ref[:, rows], carried) + dot_nn(cst_ref[:, rows], carried_rest)
            if k < chunks - 1:
                fresh = fresh + carry[BLK - 1 : BLK, :] * d_state
            d_state = fresh
        moved_out = ssm - skip * xs
        balance = d_low.astype(jnp.float32) * moved_out - driven.astype(jnp.float32) * d_driven
        upper, lower = two_parts(balance)
        d_cum = dot_nn(upper, pick_cum) + dot_nn(lower, pick_cum)
        d_driven = d_driven.astype(jnp.bfloat16).astype(jnp.float32)
        upper, lower = two_parts(d_driven * xs)
        dcols_ref[rows, :] += d_cum + dot_nn(upper, pick_step) + dot_nn(lower, pick_step)
        d_xs = skip * d_out + step_wide * d_driven
        d_pre = d_xs * (sig + xs * (1.0 - sig))
        dpre_ref[rows, :] = d_pre
        for lag in range(TAPS):
            sums_ref[TAPS - 1 - lag : TAPS - lag, :] += jnp.sum(
                d_pre * moved[lag], axis=0, keepdims=True
            )
        after = jnp.concatenate([d_pre, dpre_ref[pl.ds(first + BLK, 8), :]], axis=0)
        rem = wide_rows(rem_ref, first, BLK, width)
        d_x = conv_ref[TAPS - 1 : TAPS, :] * d_pre
        for lag in range(1, TAPS):
            shifted = pltpu.roll(after, BLK + 8 - lag, 0)[0:BLK]
            d_x = d_x + conv_ref[TAPS - 1 - lag : TAPS - lag, :] * jnp.where(
                rem >= lag, shifted, 0.0
            )
        dx_ref[0, rows, :] = d_x.astype(jnp.bfloat16)

    @pl.when(step == pl.num_programs(0) - 1)
    def _():
        for k in range(chunks):
            rows = pl.ds(k * BLK, BLK)
            keep = (gap >= 0.0) & (gap <= rem_ref[rows, 0:1])
            d_inner = jnp.where(keep, dinner_ref[k], 0.0)
            dbs_ref[rows, :] += dot_nn(d_inner.astype(jnp.bfloat16), cs_ref[rows, :])
            dcs_ref[rows, :] += dot_nn(d_inner.T.astype(jnp.bfloat16), bs_ref[rows, :])


def mix_backward(
    z, x, ssm, d_gn, cols, cumt, conv, skip, gain, posb, remb, rgb, crossb, bs, cs, cst, states, deps
):
    parts, length, inner_width = ssm.shape
    state = bs.shape[1]
    lanes = 256
    per = inner_width // lanes
    groups = parts * per
    block = (1, length, lanes)
    whole = lambda g: (0, 0)
    own = lambda g: (g // per, 0, g % per)
    return pl.pallas_call(
        mix_bwd_kernel,
        grid=(groups,),
        in_specs=[
            pl.BlockSpec(block, own),
            pl.BlockSpec(block, own),
            pl.BlockSpec(block, own),
            pl.BlockSpec(block, own),
            pl.BlockSpec(cols.shape, whole),
            pl.BlockSpec((1,) + cumt.shape[1:], lambda g: (g, 0, 0)),
            pl.BlockSpec((TAPS, lanes), lambda g: (0, g)),
            pl.BlockSpec((1, lanes), lambda g: (0, g)),
            pl.BlockSpec((1, lanes), lambda g: (0, g)),
            pl.BlockSpec((length, 128), whole),
            pl.BlockSpec((length, 128), whole),
            pl.BlockSpec((length, 128), whole),
            pl.BlockSpec((length, 128), whole),
            pl.BlockSpec((length, state), whole),
            pl.BlockSpec((length, state), whole),
            pl.BlockSpec((state, length), whole),
            pl.BlockSpec((length // BLK, state, lanes), lambda g: (0, 0, g)),
        ]
        + [pl.BlockSpec(memory_space=pl.ANY)] * len(deps),
        out_specs=[
            pl.BlockSpec(block, own),
            pl.BlockSpec(block, own),
            pl.BlockSpec((length, 128), whole),
            pl.BlockSpec((8, lanes), lambda g: (0, g)),
            pl.BlockSpec((length, state), whole),
            pl.BlockSpec((length, state), whole),
        ],
        out_shape=[
            jax.ShapeDtypeStruct((parts, length, inner_width), jnp.bfloat16),
            jax.ShapeDtypeStruct(x.shape, jnp.bfloat16),
            jax.ShapeDtypeStruct((length, 128), jnp.float32),
            jax.ShapeDtypeStruct((8, parts * inner_width), jnp.float32),
            jax.ShapeDtypeStruct((length, state), jnp.float32),
            jax.ShapeDtypeStruct((length, state), jnp.float32),
        ],
        scratch_shapes=[
            pltpu.VMEM((length // BLK, BLK, BLK), jnp.float32),
            pltpu.VMEM((length // BLK, BLK, BLK), jnp.float32),
            pltpu.VMEM((length + 8, lanes), jnp.float32),
        ],
        compiler_params=pltpu.CompilerParams(vmem_limit_bytes=VMEM_LIMIT),
        cost_estimate=pl.CostEstimate(
            flops=50_000_000_000, bytes_accessed=50_000_000, transcendentals=0
        ),
        name="mix_bwd",
    )(
        z, x, ssm, d_gn, cols, cumt, conv, skip, gain, posb, remb, rgb, crossb, bs, cs, cst,
        states, *deps,
    )


def tile_of(columns, limit=512):
    size = limit
    while columns % size:
        size -= 128
    return size


def part_product(
    left, right, dtype, first=0, columns=None, extra=None, deps=(), fold=1, into=None, place=0, room=None
):
    parts, depth, whole = right.shape
    rows = left.shape[0]
    columns = whole - first if columns is None else columns
    tile = tile_of(columns)
    while first % tile or place % tile:
        tile = tile_of(columns, tile - 128)
    begin = first // tile
    count = columns // tile
    block = (1, rows, tile)
    shift = place // tile
    room = fold * columns if room is None else room
    in_specs = [
        pl.BlockSpec((rows, depth), lambda m, n: (0, 0)),
        pl.BlockSpec((1, depth, tile), lambda m, n: (m, 0, begin + n)),
    ]
    operands = [left, right]
    if extra is not None:
        in_specs.append(pl.BlockSpec(block, lambda m, n: (m, 0, n)))
        operands.append(extra)
    aliases = {}
    if into is not None:
        aliases = {len(operands): 0}
        deps = (into,) + tuple(deps)
        room = into.shape[2]
    in_specs += [pl.BlockSpec(memory_space=pl.ANY)] * len(deps)

    def body(left_ref, right_ref, *others):
        total = dot_nn(left_ref[...], right_ref[0])
        if extra is not None:
            total = total + others[0][0].astype(jnp.float32)
        others[-1][0] = total.astype(dtype)

    return pl.pallas_call(
        body,
        grid=(parts, count),
        in_specs=in_specs,
        out_specs=pl.BlockSpec(
            block, lambda m, n: (m // fold, 0, shift + (m % fold) * count + n)
        ),
        out_shape=jax.ShapeDtypeStruct((parts // fold, rows, room), dtype),
        input_output_aliases=aliases,
        compiler_params=pltpu.CompilerParams(vmem_limit_bytes=VMEM_LIMIT),
        cost_estimate=pl.CostEstimate(
            flops=2 * parts * rows * depth * columns,
            bytes_accessed=parts * depth * columns * 2 + parts * rows * columns * 4,
            transcendentals=0,
        ),
        name="part_product",
    )(*operands, *deps)


def part_back(left, right, first=0, start=None, scale=None, deps=()):
    parts, rows, columns = left.shape
    width = right.shape[1]
    fold = parts // right.shape[0]
    tile = tile_of(columns)
    while first % tile:
        tile = tile_of(columns, tile - 128)
    begin = first // tile
    count = columns // tile
    in_specs = [
        pl.BlockSpec((1, rows, tile), lambda m, n: (m, 0, n)),
        pl.BlockSpec(
            (1, width, tile), lambda m, n: (m // fold, 0, begin + (m % fold) * count + n)
        ),
    ]
    operands = [left, right]
    if start is not None:
        in_specs.append(pl.BlockSpec((rows, width), lambda m, n: (0, 0)))
        operands.append(start)
    if scale is not None:
        in_specs.append(pl.BlockSpec(scale.shape, lambda m, n: (0, 0)))
        operands.append(scale)
    in_specs += [pl.BlockSpec(memory_space=pl.ANY)] * len(deps)

    def body(left_ref, right_ref, *others):
        out_ref = others[-1]
        total = dot_nt(left_ref[0], right_ref[0])
        opening = (pl.program_id(0) == 0) & (pl.program_id(1) == 0)

        if scale is not None:
            total = total * others[1][:, 0:1]

        @pl.when(opening)
        def _():
            out_ref[...] = total if start is None else total + others[0][...]

        @pl.when(jnp.logical_not(opening))
        def _():
            out_ref[...] += total

    return pl.pallas_call(
        body,
        grid=(parts, count),
        in_specs=in_specs,
        out_specs=pl.BlockSpec((rows, width), lambda m, n: (0, 0)),
        out_shape=jax.ShapeDtypeStruct((rows, width), jnp.float32),
        compiler_params=pltpu.CompilerParams(vmem_limit_bytes=VMEM_LIMIT),
        cost_estimate=pl.CostEstimate(
            flops=2 * parts * rows * columns * width,
            bytes_accessed=2 * parts * columns * (rows + width) + 4 * rows * width,
            transcendentals=0,
        ),
        name="part_back",
    )(*operands, *deps)


def outer_kernel(left_ref, right_ref, *others):
    out_ref = others[-1]
    total = dot_tn(left_ref[0], right_ref[...]).astype(jnp.bfloat16)
    rows = out_ref.shape[1]
    width = right_ref.shape[1]
    wraps = total.shape[0] // rows
    piece = 64
    for i in range(rows // piece):
        for w in range(wraps):
            begin = (i * wraps + w) * piece
            out_ref[0, pl.ds(i * piece, piece), pl.ds(w * width, width)] = total[
                begin : begin + piece
            ]


def outer_into(left, right, wraps, place, room, into=None, deps=()):
    parts, length, columns = left.shape
    width = right.shape[1]
    tile = 256 * wraps
    begin = place // (wraps * width)
    before = ([] if into is None else [into]) + list(deps)
    return pl.pallas_call(
        outer_kernel,
        grid=(parts, columns // tile),
        in_specs=[
            pl.BlockSpec((1, length, tile), lambda m, n: (m, 0, n)),
            pl.BlockSpec((length, width), lambda m, n: (0, 0)),
        ]
        + [pl.BlockSpec(memory_space=pl.ANY)] * len(before),
        input_output_aliases={} if into is None else {2: 0},
        out_specs=pl.BlockSpec((1, tile // wraps, wraps * width), lambda m, n: (m, n, begin)),
        out_shape=jax.ShapeDtypeStruct((parts, columns // wraps, room), jnp.bfloat16),
        compiler_params=pltpu.CompilerParams(vmem_limit_bytes=VMEM_LIMIT),
        cost_estimate=pl.CostEstimate(
            flops=2 * parts * length * columns * width,
            bytes_accessed=2 * parts * columns * (length + width),
            transcendentals=0,
        ),
        name="outer_into",
    )(left, right, *before)


def unfold_kernel(in_ref, out_ref):
    count = out_ref.shape[1]
    width = out_ref.shape[2]
    for j in range(count):
        out_ref[:, j, :] = in_ref[:, j * width : (j + 1) * width].astype(jnp.float32)


def unfold(value, count, width):
    rows = value.shape[0]
    step = 128
    return pl.pallas_call(
        unfold_kernel,
        grid=(rows // step,),
        in_specs=[pl.BlockSpec((step, count * width), lambda n: (n, 0))],
        out_specs=pl.BlockSpec((step, count, width), lambda n: (n, 0, 0)),
        out_shape=jax.ShapeDtypeStruct((rows, count, width), jnp.float32),
        compiler_params=pltpu.CompilerParams(vmem_limit_bytes=VMEM_LIMIT),
        cost_estimate=pl.CostEstimate(
            flops=0, bytes_accessed=6 * rows * count * width, transcendentals=0
        ),
        name="unfold",
    )(value)


def ffn_in_kernel(left_ref, gate_w_ref, up_w_ref, gate_ref, up_ref, hidden_ref):
    gate = dot_nn(left_ref[...], gate_w_ref[0])
    upper = dot_nn(left_ref[...], up_w_ref[0])
    gate_ref[0] = gate.astype(jnp.bfloat16)
    up_ref[0] = upper.astype(jnp.bfloat16)
    hidden_ref[0] = (gate * sigmoid(gate) * upper).astype(jnp.bfloat16)


def ffn_forward(left, right, half):
    parts, depth, _ = right.shape
    rows = left.shape[0]
    tile = tile_of(half)
    count = half // tile
    block = pl.BlockSpec((1, rows, tile), lambda m, n: (m, 0, n))
    shape = jax.ShapeDtypeStruct((parts, rows, half), jnp.bfloat16)
    return pl.pallas_call(
        ffn_in_kernel,
        grid=(parts, count),
        in_specs=[
            pl.BlockSpec((rows, depth), lambda m, n: (0, 0)),
            pl.BlockSpec((1, depth, tile), lambda m, n: (m, 0, n)),
            pl.BlockSpec((1, depth, tile), lambda m, n: (m, 0, count + n)),
        ],
        out_specs=[block, block, block],
        out_shape=[shape, shape, shape],
        compiler_params=pltpu.CompilerParams(vmem_limit_bytes=VMEM_LIMIT),
        cost_estimate=pl.CostEstimate(
            flops=4 * parts * rows * depth * half,
            bytes_accessed=parts * half * (4 * depth + 6 * rows),
            transcendentals=0,
        ),
        name="ffn_in",
    )(left, right, right)


def ffn_back_kernel(left_ref, right_ref, gate_ref, up_ref, out_ref):
    grad = dot_nn(left_ref[...], right_ref[0])
    gate = gate_ref[0].astype(jnp.float32)
    sig = sigmoid(gate)
    act = gate * sig
    slope = sig + act * (1.0 - sig)
    out_ref[0, 0] = (grad * up_ref[0].astype(jnp.float32) * slope).astype(jnp.bfloat16)
    out_ref[0, 1] = (grad * act).astype(jnp.bfloat16)


def ffn_backward(left, right, first, gate, upper):
    parts, rows, half = gate.shape
    depth = left.shape[1]
    tile = tile_of(half)
    begin = first // tile
    block = pl.BlockSpec((1, rows, tile), lambda m, n: (m, 0, n))
    return pl.pallas_call(
        ffn_back_kernel,
        grid=(parts, half // tile),
        in_specs=[
            pl.BlockSpec((rows, depth), lambda m, n: (0, 0)),
            pl.BlockSpec((1, depth, tile), lambda m, n: (m, 0, begin + n)),
            block,
            block,
        ],
        out_specs=pl.BlockSpec((1, 2, rows, tile), lambda m, n: (m, 0, 0, n)),
        out_shape=jax.ShapeDtypeStruct((parts, 2, rows, half), jnp.bfloat16),
        compiler_params=pltpu.CompilerParams(vmem_limit_bytes=VMEM_LIMIT),
        cost_estimate=pl.CostEstimate(
            flops=2 * parts * rows * depth * half,
            bytes_accessed=parts * half * (2 * depth + 8 * rows),
            transcendentals=0,
        ),
        name="ffn_back",
    )(left, right, gate, upper)


def span_kernel(col_ref, row_ref, pos_ref, rem_ref):
    length = col_ref.shape[0]
    row = row_ref[...]
    other = lax.broadcasted_iota(jnp.int32, (BLK, length), 1)
    for i in range(length // BLK):
        rows = pl.ds(i * BLK, BLK)
        spot = i * BLK + lax.broadcasted_iota(jnp.int32, (BLK, length), 0)
        same = col_ref[rows, 0:1] == row
        before = jnp.where(same & (other < spot), 1.0, 0.0)
        after = jnp.where(same & (other > spot), 1.0, 0.0)
        before = jnp.sum(before, axis=1, keepdims=True)
        after = jnp.sum(after, axis=1, keepdims=True)
        pos_ref[rows, :] = jnp.broadcast_to(before, (BLK, 128))
        rem_ref[rows, :] = jnp.broadcast_to(after, (BLK, 128))


def spans(seg):
    length = seg.shape[0]
    shape = jax.ShapeDtypeStruct((length, 128), jnp.float32)
    return pl.pallas_call(
        span_kernel,
        out_shape=[shape, shape],
        compiler_params=pltpu.CompilerParams(vmem_limit_bytes=VMEM_LIMIT),
        name="spans",
    )(seg[:, None], seg[None, :])


def refold_kernel(in_ref, out_ref):
    rows, width = in_ref.shape
    count = out_ref.shape[0] // rows
    width = width // count
    piece = 64
    for i in range(rows // piece):
        for j in range(count):
            out_ref[pl.ds((i * count + j) * piece, piece), :] = in_ref[
                i * piece : (i + 1) * piece, j * width : (j + 1) * width
            ].astype(jnp.float32)


def refold(value, first, count, width, step):
    rows = value.shape[0]
    begin = first // (count * width)
    return pl.pallas_call(
        refold_kernel,
        grid=(rows // step,),
        in_specs=[pl.BlockSpec((step, count * width), lambda n: (n, begin))],
        out_specs=pl.BlockSpec((step * count, width), lambda n: (n, 0)),
        out_shape=jax.ShapeDtypeStruct((rows * count, width), jnp.float32),
        compiler_params=pltpu.CompilerParams(vmem_limit_bytes=VMEM_LIMIT),
        cost_estimate=pl.CostEstimate(
            flops=0, bytes_accessed=6 * rows * count * width, transcendentals=0
        ),
        name="refold",
    )(value)


def embed_kernel(ids_ref, first_ref, second_ref, onehot_ref, out_ref):
    length = ids_ref.shape[1]
    value = lax.broadcasted_iota(jnp.int32, (length, VOCAB), 1)
    total = None
    for p in range(ids_ref.shape[2]):
        span = pl.ds(p * VOCAB, VOCAB)
        hit = jnp.where(ids_ref[0, :, p : p + 1] == value, 1.0, 0.0).astype(jnp.bfloat16)
        onehot_ref[0, :, span] = hit
        half = ids_ref.shape[2] // 2
        source = first_ref if p < half else second_ref
        part = dot_nt(hit, source[0, :, pl.ds((p % half) * VOCAB, VOCAB)])
        total = part if total is None else total + part

    @pl.when(pl.program_id(0) == 0)
    def _():
        out_ref[...] = total

    @pl.when(pl.program_id(0) > 0)
    def _():
        out_ref[...] += total


def embed_rows(ids, first, second):
    parts, length, count = ids.shape
    width = first.shape[1]
    return pl.pallas_call(
        embed_kernel,
        grid=(parts,),
        in_specs=[
            pl.BlockSpec((1, length, count), lambda m: (m, 0, 0)),
            pl.BlockSpec((1,) + first.shape[1:], lambda m: (m, 0, 0)),
            pl.BlockSpec((1,) + second.shape[1:], lambda m: (m, 0, 0)),
        ],
        out_specs=[
            pl.BlockSpec((1, length, count * VOCAB), lambda m: (m, 0, 0)),
            pl.BlockSpec((length, width), lambda m: (0, 0)),
        ],
        out_shape=[
            jax.ShapeDtypeStruct((parts, length, count * VOCAB), jnp.bfloat16),
            jax.ShapeDtypeStruct((length, width), jnp.float32),
        ],
        compiler_params=pltpu.CompilerParams(vmem_limit_bytes=VMEM_LIMIT),
        cost_estimate=pl.CostEstimate(
            flops=2 * parts * length * width * count * VOCAB,
            bytes_accessed=12 * length * width,
            transcendentals=0,
        ),
        name="embed_rows",
    )(ids, first, second)


def bit_of(index, bit):
    return (index >> bit) & 1


def swap(value, stage):
    if stage is None:
        return lax.ppermute(value, "mp", [(0, 1), (1, 0)])
    count = lax.axis_size("dp")
    return lax.ppermute(value, "dp", [(i, i ^ (1 << stage)) for i in range(count)])


def my_bit(stage):
    if stage is None:
        return lax.axis_index("mp")
    return bit_of(lax.axis_index("dp"), stage)


def take_half(value, which):
    half = value.shape[0] // 2
    return lax.dynamic_slice_in_dim(value, which * half, half, 0)


def join(own, other, bit):
    first = jnp.where(bit == 0, own, other)
    second = jnp.where(bit == 0, other, own)
    return jnp.concatenate([first, second], axis=0)


def add_low(left, right):
    return (left.astype(jnp.float32) + right.astype(jnp.float32)).astype(jnp.bfloat16)


def dp_bits():
    return lax.axis_size("dp").bit_length() - 1


def ring_order():
    order = []
    layers = lax.axis_size("dp") // 4
    for side in range(2):
        for spot in range(layers):
            layer = spot if side == 0 else layers - 1 - spot
            for core in range(2):
                order.append(layer * 4 + side * 2 + core)
    return order


def block_of(device, bits):
    value = 0
    for bit in range(bits):
        value = value * 2 + ((device >> bit) & 1)
    return value


def sum_stages(total, order, after=()):
    for turn, stage in enumerate(order):
        mine = my_bit(stage)
        if stage is None:
            received = swap(lax.dynamic_index_in_dim(total, 1 - mine, 0, keepdims=False), None)
            kept = lax.dynamic_index_in_dim(total, mine, 0, keepdims=False)
        else:
            axis = total.ndim - 2
            half = total.shape[axis] // 2
            received = swap(
                lax.dynamic_slice_in_dim(total, (1 - mine) * half, half, axis), stage
            )
            kept = lax.dynamic_slice_in_dim(total, mine * half, half, axis)
        if turn < len(after):
            kept = kept.astype(jnp.float32) + after[turn]
        total = add_low(kept, received)
    return total


def x_first():
    return [None] + list(range(1, dp_bits()))


def y_first():
    return [1, None] + list(range(2, dp_bits()))


def gather_sum(piece, reversed_blocks=True):
    bits = dp_bits()
    order = ring_order()
    ringed = lax.all_gather(piece, "dp", axis=0, axis_index_groups=[order])
    blocks = [None] * len(order)
    for place, device in enumerate(order):
        blocks[block_of(device, bits) if reversed_blocks else device] = ringed[place]
    return jnp.concatenate(blocks, axis=0)


def around_order(part):
    layers = lax.axis_size("dp") // 4
    order = []
    for turn in range(2):
        side = turn if part == 0 else 1 - turn
        for spot in range(layers):
            layer = layers - 1 - spot if turn == 0 else spot
            for core in range(2):
                order.append((layer * 4 + side * 2 + core) * 2 + part)
    return order


def ring_scatter(value):
    order = around_order(0) + around_order(1)
    return lax.psum_scatter(
        value,
        ("dp", "mp"),
        scatter_dimension=0,
        tiled=True,
        axis_index_groups=[order],
    )


def ring_gather(piece):
    return lax.all_gather(
        piece,
        ("dp", "mp"),
        axis=0,
        tiled=True,
        axis_index_groups=[around_order(0), around_order(1)],
    )


def gather_steps(shard, order, peek=None, after=None):
    bits = dp_bits()
    value = shard.reshape((1,) * (bits + 1) + shard.shape)
    seen = None
    for turn, stage in enumerate(order):
        axis = 0 if stage is None else bits - stage
        other = swap(value, stage)
        bit = my_bit(stage)
        if turn == peek:
            seen = value
        if after is not None and turn in after:
            value = value + after[turn].astype(value.dtype)
        value = jnp.concatenate(
            [jnp.where(bit == 0, value, other), jnp.where(bit == 0, other, value)], axis=axis
        )
    value = value.reshape(2, -1, shard.shape[1])
    return value if peek is None else (value, seen)


def gather_y_last():
    return list(range(dp_bits() - 1, 1, -1)) + [None, 1, 0]


def gather_x_last():
    return list(range(dp_bits() - 1, 1, -1)) + [1, None, 0]


def spread_all(value):
    for stage in [0, 1, None] + list(range(2, dp_bits())):
        value = value + swap(value, stage)
    return value


def reduce_table(value):
    stages = [0, None] + list(range(1, dp_bits()))
    for stage in stages:
        mine = my_bit(stage)
        value = take_half(value, mine) + swap(take_half(value, 1 - mine), stage)
    for stage in reversed(stages):
        value = join(value, swap(value, stage), my_bit(stage))
    return value


def gather_small(shard):
    bits = dp_bits()
    value = shard[None]
    for bit in range(bits):
        value = join(value, swap(value, bit), my_bit(bit))
    return value.reshape((-1,) + shard.shape[1:])


def gather_weight(shard):
    return lax.all_gather(shard, ("mp", "dp"), axis=0, tiled=True).reshape(
        lax.axis_size("mp"), -1, shard.shape[1]
    )


def rms_back(hidden, gain, grad):
    inv = lax.rsqrt(jnp.mean(hidden * hidden, axis=-1, keepdims=True) + 1e-05)
    weighted = grad * gain
    mean = jnp.mean(hidden * weighted, axis=-1, keepdims=True)
    d_gain = jnp.sum(hidden * inv * grad, axis=0)
    return inv * weighted - hidden * (inv * inv * inv * mean), d_gain


def in_groups(per_head, groups):
    length = per_head.shape[0]
    return per_head.reshape(length, groups, -1).transpose(1, 0, 2)


def wide128(column):
    return jnp.broadcast_to(column, (column.shape[0], 128))


def dot_parts(left, right):
    return lax.dot_general(
        left, right, (((1,), (1,)), ((), ())), preferred_element_type=jnp.float32
    ).transpose(1, 0, 2)


def dot_back(left, right):
    total = dot_nt(left[0], right[0])
    for part in range(1, left.shape[0]):
        total = total + dot_nt(left[part], right[part])
    return total


def on_device_rows(
    byte_ids,
    segment_ids,
    embed_table,
    patch_weight,
    norm1_gain,
    mamba_in,
    mamba_dt,
    mamba_bc,
    conv_x,
    conv_bc,
    dt_bias,
    a_log,
    d_skip,
    gate_gain,
    mamba_out,
    norm2_gain,
    attn_qkv,
    attn_out,
    norm3_gain,
    ffn_in,
    ffn_out,
    d_out,
):
    low = jnp.bfloat16
    parts = lax.axis_size("mp")
    part = lax.axis_index("mp")
    shard = mamba_in.shape[0]
    per_pos = PATCH // parts
    inner_width = mamba_in.shape[2]
    heads_part = mamba_dt.shape[1]
    state = mamba_bc.shape[1] // 2
    lanes = 256
    groups = parts * inner_width // lanes

    def exchange(value):
        own = lax.dynamic_index_in_dim(value, part, 0, keepdims=False)
        other = swap(lax.dynamic_index_in_dim(value, 1 - part, 0, keepdims=False), None)
        return join(own, other, part)

    ids = exchange(byte_ids)
    seg = exchange(segment_ids)
    length = seg.shape[0]

    def both_parts(value):
        own = value
        other = swap(value, None)
        return join(own[None], other[None], part)

    conv_full = jnp.concatenate(list(both_parts(conv_x)), axis=1)
    vectors = both_parts(jnp.concatenate([dt_bias, a_log, d_skip, gate_gain]))
    heads = parts * heads_part
    bias_full, alog_full, skip_full = (
        vectors[:, i * heads_part : (i + 1) * heads_part].reshape(heads) for i in range(3)
    )
    ggain_full = vectors[:, 3 * heads_part :].reshape(parts * inner_width)

    bc_half = lax.dynamic_slice_in_dim(mamba_bc, part * state, state, 1)
    pad = (-heads_part) % 128
    shard_z = mamba_in[:, 0]
    shard_x = jnp.concatenate(
        [mamba_in[:, 1], bc_half, mamba_dt, jnp.zeros((shard, pad), low)], axis=1
    )
    shard_qkv = attn_qkv.reshape(shard, -1)
    shard_back = jnp.concatenate([mamba_out.T, attn_out.T], axis=1)
    width_qkv = shard_qkv.shape[1]
    shard_ffn = jnp.concatenate([ffn_in.reshape(shard, -1), ffn_out.T], axis=1)
    width_in = ffn_in.shape[1] * ffn_in.shape[2]

    table = gather_small(embed_table)
    rows_by_pos = patch_weight.reshape(per_pos, -1, patch_weight.shape[1])
    mapped = lax.dot_general(
        rows_by_pos, table, (((1,), (1,)), ((), ())), preferred_element_type=jnp.float32
    ).astype(low)
    mapped = mapped.transpose(1, 0, 2).reshape(rows_by_pos.shape[2], -1)
    posb, remb = spans(seg)
    ids_parts = ids.reshape(length, parts, per_pos).transpose(1, 0, 2)
    prepared = posb[0, 0] + ids_parts[0, 0, 0].astype(jnp.float32)
    prepared = (prepared + conv_full[0, 0] + ggain_full[0]) * 0
    half_map = mapped.shape[1] // 2
    mapped_a, early = gather_steps(
        mapped[:, :half_map], gather_y_last(), peek=3, after={3: prepared}
    )
    mapped_b = gather_steps(mapped[:, half_map:], gather_x_last())
    early = early.reshape(-1)[0] * 0
    w_zx = gather_weight(jnp.concatenate([shard_z, shard_qkv, shard_x], axis=1) + early)
    w_ffn = gather_weight(shard_ffn + early)
    mapped_ready = (mapped_a[0, 0, 0] + mapped_b[0, 0, 0]) * 0

    onehot, resid0 = embed_rows(ids_parts, mapped_a, mapped_b)

    spots = jnp.arange(length, dtype=jnp.int32)
    pos = posb[:, 0]
    rem = remb[:, 0]

    u1 = rms_apply(resid0, norm1_gain).astype(low)
    gate = part_product(u1, w_zx, jnp.float32, columns=inner_width)
    fed = part_product(u1, w_zx, jnp.float32, first=inner_width + width_qkv)
    first_dt = inner_width + state
    bc = jnp.concatenate([fed[p, :, inner_width:first_dt] for p in range(parts)], axis=1)
    dtr = jnp.concatenate([fed[p, :, first_dt : first_dt + heads_part] for p in range(parts)], 1)
    bc_act, pull_bc = jax.vjp(
        lambda signal, taps: jax.nn.silu(conv_rows(signal, taps, seg)), bc, conv_bc
    )
    bcs = bc_act.astype(low)
    bs = bcs[:, :state]
    cs = bcs[:, state:]
    steps = jax.nn.softplus(dtr + bias_full)
    rate = -jnp.exp(alog_full)
    lower = (spots[:, None] >= spots[None, :]).astype(jnp.float32)
    cum = lax.dot_general(
        lower, rate * steps, (((1,), (0,)), ((), ())), precision=lax.Precision.HIGHEST
    )
    chunk = spots // BLK
    chunk_first = chunk * BLK
    ends = cum.reshape(length // BLK, BLK, heads)[:, BLK - 1]
    starts = jnp.concatenate([jnp.zeros((1, heads), jnp.float32), ends[:-1]], axis=0)
    start_wide = jnp.repeat(starts, BLK, axis=0)
    end_wide = jnp.repeat(ends, BLK, axis=0)
    carried = (pos > (spots - chunk_first).astype(jnp.float32)) & (chunk > 0)
    carry = jnp.where(carried[:, None], jnp.exp(cum - start_wide), 0.0)
    lasting = rem >= (chunk_first + BLK - 1 - spots).astype(jnp.float32)
    last = jnp.where(lasting[:, None], jnp.exp(end_wide - cum), 0.0)
    cum2 = cum * LOG2E
    cols = jnp.concatenate([steps, cum2, carry, last], axis=1)
    cumt = cum2.T.reshape(groups, -1, length)
    skip_wide = jnp.repeat(skip_full, PM)[None]
    ssm, scaled, states, squares = mix_forward(
        gate, fed, cols, cumt, conv_full, skip_wide, ggain_full[None], posb, bs, cs, bs.T
    )
    after_u1 = u1[0, 0] * 0
    after_fed = fed[0, 0, 0] * 0
    after_mix = ssm[0, 0, 0] * 0
    w_back = gather_steps(
        shard_back + mapped_ready, gather_y_last(), after={2: after_u1, 3: after_fed, 4: after_mix}
    )
    factor = lax.rsqrt(jnp.sum(squares, axis=1, keepdims=True) / DIN + 1e-05)
    gain_parts = ggain_full.reshape(parts, 1, inner_width)
    resid1 = part_back(scaled, w_back, start=resid0, scale=wide128(factor))

    u2 = rms_apply(resid1, norm2_gain).astype(low)
    qkv = part_product(u2, w_zx, low, first=inner_width, columns=width_qkv)
    attended, logs = attn_forward(qkv, posb)
    resid2 = part_back(attended, w_back, first=inner_width, start=resid1)

    u3 = rms_apply(resid2, norm3_gain).astype(low)
    half = width_in // 2
    gate3, up3, hidden = ffn_forward(u3, w_ffn, half)
    mixed_row = part_back(hidden, w_ffn, first=width_in, start=resid2)

    core = my_bit(0)

    def half_rows(value, which):
        count = value.shape[0] // 2
        return lax.dynamic_slice_in_dim(value, which * count, count, 0)

    def sum_cores(left_t, right, before=(), deps=()):
        sent = part_product(half_rows(left_t, 1 - core), right, low, deps=before)
        received = swap(sent, 0)
        return part_product(half_rows(left_t, core), right, low, extra=received, deps=deps)

    started = ssm[0, 0, 0] * 0
    ended = hidden[0, 0, 0].astype(jnp.float32) * 0
    cot_own = lax.dynamic_index_in_dim(d_out, part, 0, keepdims=False) + ended
    cot_other = lax.dynamic_index_in_dim(d_out, 1 - part, 0, keepdims=False) + started
    cot = join(cot_own, swap(cot_other.astype(low), None).astype(jnp.float32), part)
    dm3 = cot.astype(low)
    d_gate_up = ffn_backward(dm3, w_ffn, width_in, gate3, up3)
    quarter = d_gate_up.reshape(2 * parts, length, half)
    part_ffn = outer_into(hidden, dm3, 2, width_in, 3 * width_in // 2)
    part_ffn = part_product(u3.T, quarter, low, fold=2, into=part_ffn)
    sum_ffn = ring_scatter(part_ffn.reshape(-1, part_ffn.shape[2]))
    back_u3 = part_back(quarter, w_ffn, deps=[part_ffn])
    back, d_gain3 = rms_back(resid2, norm3_gain, back_u3)
    cot = cot + back

    dm2 = cot.astype(low)
    d_att = part_product(dm2, w_back, low, first=inner_width)
    part_mid = part_product(
        dm2.T, attended, low, place=inner_width + width_qkv, room=inner_width + width_qkv + width_qkv // 3
    )
    log_rows = jnp.pad(logs[:, :, :4].transpose(0, 2, 1), ((0, 0), (0, 4), (0, 0)))
    d_qkv = attn_backward(
        qkv, attended, d_att, log_rows, remb, []
    )
    part_mid = part_product(u2.T, d_qkv, low, into=part_mid, place=inner_width)
    back, d_gain2 = rms_back(resid1, norm2_gain, part_back(d_qkv, w_zx, first=inner_width, deps=[part_mid]))
    cot = cot + back

    dm1 = cot.astype(low)
    d_gn = part_product(dm1, w_back, jnp.float32, columns=inner_width)
    part_mid = outer_into(scaled, (cot * factor).astype(low), 1, 0, part_mid.shape[2], into=part_mid, deps=[sum_ffn, d_gn])
    sum_mid = ring_scatter(part_mid.reshape(-1, part_mid.shape[2]))
    gated = ssm * gate * sigmoid(gate)
    cross = jnp.sum(jnp.sum(gated * gain_parts * d_gn, axis=2), axis=0)[:, None]
    cross = factor * factor * factor * cross / DIN
    d_z, d_fed, d_cols, sums, d_bs, d_cs = mix_backward(
        gate,
        fed,
        ssm,
        d_gn,
        cols,
        cumt,
        conv_full,
        skip_wide,
        ggain_full[None],
        posb,
        remb,
        wide128(factor),
        wide128(cross),
        bs,
        cs,
        cs.T,
        states,
        [part_mid, sum_ffn],
    )
    d_cum = d_cols[:, :heads]
    d_step = d_cols[:, heads : 2 * heads]
    d_decay = lax.dot_general(
        lower, d_cum, (((0,), (0,)), ((), ())), precision=lax.Precision.HIGHEST
    )
    d_alog = jnp.sum(d_decay * rate * steps, axis=0)
    d_dtr = (d_step + d_decay * rate) * sigmoid(dtr + bias_full)
    d_bias = jnp.sum(d_dtr, axis=0)
    d_bcs = jnp.concatenate([d_bs, d_cs], axis=1).astype(low).astype(jnp.float32)
    d_bc, d_convbc = pull_bc(d_bcs)
    d_rest = jnp.stack(
        [
            jnp.concatenate(
                [
                    d_bc[:, p * state : (p + 1) * state].astype(low),
                    d_dtr[:, p * heads_part : (p + 1) * heads_part].astype(low),
                    jnp.zeros((length, pad), low),
                ],
                axis=1,
            )
            for p in range(parts)
        ]
    )
    d_fed = lax.dynamic_update_slice(d_fed, d_rest, (0, 0, inner_width))
    bits = dp_bits()
    devices = lax.axis_size("dp")
    u1_t = u1.T
    rank = {device: place for place, device in enumerate(ring_order())}
    source = {block_of(device, bits): rank[device] for device in range(devices)}
    u1_t = jnp.concatenate(
        [u1_t[source[b] * shard : (source[b] + 1) * shard] for b in range(devices)], axis=0
    )
    part_z = sum_cores(u1_t, d_z)
    part_x = sum_cores(u1_t, d_fed)
    back_u1 = part_back(d_z, w_zx, deps=[part_z, part_x, sum_mid])
    back_u1 = part_back(d_fed, w_zx, first=inner_width + width_qkv, start=back_u1)
    back, d_gain1 = rms_back(resid0, norm1_gain, back_u1)
    cot = cot + back

    columns = cot.T.astype(low).reshape((2,) * bits + (shard, length))
    columns = columns.transpose(tuple(range(bits - 1, -1, -1)) + (bits, bits + 1))
    grad_ffn = ring_gather(sum_ffn)
    grad_mid = ring_gather(sum_mid)
    after_u1 = back_u1[0, 0] * 0
    piece_z = sum_stages(part_z, x_first()[:1], [after_u1])
    piece_x = sum_stages(part_x, y_first()[:1], [after_u1])
    counted = sum_cores(
        columns.reshape(-1, length), onehot, before=[piece_z, piece_x], deps=[grad_ffn]
    )
    width_in_mid = inner_width + width_qkv
    out_ffn_in = unfold(grad_ffn, ffn_in.shape[1], half)
    out_ffn_out = refold(grad_ffn, width_in, 2, mixed_row.shape[1], 256)
    out_mout = refold(grad_mid, 0, 1, inner_width, 256)
    out_qkv = grad_mid[:, inner_width:width_in_mid].astype(jnp.float32)
    out_qkv = out_qkv.reshape(out_qkv.shape[0], attn_qkv.shape[1], -1)
    out_aout = grad_mid[:, width_in_mid:].T.astype(jnp.float32)
    after_in = out_ffn_in[0, 0, 0] * 0
    after_ffn = out_ffn_out[0, 0] * 0
    piece = length // parts
    mine = lax.dynamic_slice_in_dim(mixed_row, part * piece, piece, 0)
    theirs = lax.dynamic_slice_in_dim(mixed_row, (1 - part) * piece, piece, 0)
    theirs = swap(theirs.astype(low), None).astype(jnp.float32)
    mixed = join(mine[None], theirs[None], part)
    after_theirs = theirs[0, 0] * 0
    after_mout = out_mout[0, 0] * 0

    def nothing(value):
        return value[(0,) * value.ndim].astype(jnp.float32) * 0

    extra = [after_in, after_ffn + after_mout, after_theirs]
    waited = nothing(mixed_row)
    for turn in range(bits):
        counted = sum_stages(counted, y_first()[turn : turn + 1], [waited])
        if turn + 1 < bits:
            held = extra[turn] + nothing(counted)
            piece_z = sum_stages(piece_z, x_first()[turn + 1 : turn + 2], [held])
            piece_x = sum_stages(piece_x, y_first()[turn + 1 : turn + 2], [held])
            waited = nothing(piece_z) + nothing(piece_x)
    grad_mix = lax.all_gather(
        jnp.concatenate([piece_z, piece_x], axis=1),
        "dp",
        axis=0,
        tiled=True,
        axis_index_groups=[ring_order()],
    )
    first_dt = 2 * inner_width + state
    counted_all = gather_sum(counted, reversed_blocks=False)
    grad_patch = jnp.einsum(
        "vd,cpv->pdc",
        table,
        counted_all.reshape(-1, per_pos, VOCAB),
        preferred_element_type=jnp.float32,
    ).reshape(patch_weight.shape[0], -1)
    grad_table = reduce_table(
        jnp.einsum(
            "cpv,pdc->vd",
            counted.reshape(-1, per_pos, VOCAB),
            rows_by_pos,
            preferred_element_type=jnp.float32,
        )
    )

    taps = conv_x.shape[0]
    small = [
        d_gain1,
        d_gain2,
        d_gain3,
        d_convbc.reshape(-1),
        d_bias,
        d_alog,
        sums[taps].reshape(heads, PM).sum(axis=1),
        sums[taps + 1],
        sums[:taps].reshape(-1),
    ]
    counts = [item.shape[0] for item in small]
    packed = jnp.concatenate(small)
    fill = (-packed.shape[0]) % 1024
    packed = spread_all(jnp.pad(packed, (0, fill)).reshape(-1, 1024)).reshape(-1)
    split = []
    begin = 0
    for count in counts:
        split.append(packed[begin : begin + count])
        begin += count
    d_gain1, d_gain2, d_gain3, d_convbc, d_bias, d_alog, d_skipped, d_ggain, d_convx = split

    def own_half(vector):
        count = vector.shape[-1] // parts
        return lax.dynamic_slice_in_dim(vector, part * count, count, vector.ndim - 1)

    model_width = grad_mix.shape[0]
    wide = jnp.float32
    half_bc = grad_mix[:, 2 * inner_width : 2 * inner_width + state]
    grad_bc = jnp.concatenate(list(both_parts(half_bc)), axis=1).astype(wide)
    return (
        mixed,
        grad_table,
        grad_patch,
        d_gain1,
        unfold(grad_mix, 2, inner_width),
        grad_mix[:, first_dt : first_dt + heads_part].astype(wide),
        grad_bc,
        own_half(d_convx.reshape(taps, -1)),
        d_convbc.reshape(conv_bc.shape),
        own_half(d_bias),
        own_half(d_alog),
        own_half(d_skipped),
        own_half(d_ggain),
        out_mout,
        d_gain2,
        out_qkv,
        out_aout,
        d_gain3,
        out_ffn_in,
        out_ffn_out,
    )


def product(left, right):
    return jnp.dot(left, right, preferred_element_type=jnp.float32)


def product_left(left, right):
    return lax.dot_general(
        left, right, (((0,), (0,)), ((), ())), preferred_element_type=jnp.float32
    )


def product_right(left, right):
    return lax.dot_general(
        left, right, (((1,), (1,)), ((), ())), preferred_element_type=jnp.float32
    )


def rms_apply(hidden, gain):
    return hidden * lax.rsqrt(jnp.mean(hidden * hidden, axis=-1, keepdims=True) + 1e-05) * gain


def conv_rows(signal, weights, seg):
    taps = weights.shape[0]
    total = weights[taps - 1] * signal
    for lag in range(1, taps):
        moved = jnp.concatenate(
            [jnp.zeros((lag, signal.shape[1]), signal.dtype), signal[:-lag]], axis=0
        )
        same = jnp.concatenate([jnp.zeros((lag,), dtype=bool), seg[lag:] == seg[:-lag]], axis=0)
        total = total + weights[taps - 1 - lag] * moved * same[:, None]
    return total


def mixer_local(packed, seg, conv_x, conv_bc, dt_bias, a_log, d_skip):
    length = packed.shape[0]
    width = conv_x.shape[1]
    state = conv_bc.shape[1] // 2
    heads = dt_bias.shape[0]
    gate_part = packed[:, :width]
    xin = packed[:, width : 2 * width]
    bc = packed[:, 2 * width : 2 * width + 2 * state]
    dtr = packed[:, 2 * width + 2 * state :]
    xs = jax.nn.silu(conv_rows(xin, conv_x, seg))
    bcs = jax.nn.silu(conv_rows(bc, conv_bc, seg)).astype(jnp.bfloat16)
    inner = product_right(bcs[:, state:], bcs[:, :state])
    steps = jax.nn.softplus(dtr + dt_bias)
    cumul = jnp.cumsum(-jnp.exp(a_log) * steps, axis=0).T
    spots = jnp.arange(length)
    keep = ((spots[:, None] >= spots[None, :]) & (seg[:, None] == seg[None, :]))[None]
    spread = cumul[:, :, None] - cumul[:, None, :]
    mixing = (jnp.where(keep, jnp.exp(jnp.where(keep, spread, 0.0)), 0.0) * inner[None]).astype(
        jnp.bfloat16
    )
    channels = xs.reshape(length, heads, -1)
    driven = (steps[:, :, None] * channels).astype(jnp.bfloat16)
    moved = jnp.einsum("hts,shp->thp", mixing, driven, preferred_element_type=jnp.float32)
    result = moved + d_skip[None, :, None] * channels
    return result.reshape(length, width) * jax.nn.silu(gate_part)


def attend_local(packed, seg):
    length = packed.shape[0]
    width = packed.shape[1] // 3
    heads = width // HD
    rounded = packed.astype(jnp.bfloat16)
    query = rounded[:, :width].reshape(length, heads, HD)
    keys = rounded[:, width : 2 * width].reshape(length, heads, HD)
    vals = rounded[:, 2 * width :].reshape(length, heads, HD)
    spots = jnp.arange(length)
    keep = ((spots[:, None] >= spots[None, :]) & (seg[:, None] == seg[None, :]))[None]
    scores = jnp.einsum("thd,shd->hts", query, keys, preferred_element_type=jnp.float32) * HD ** (
        -0.5
    )
    scores = jnp.where(keep, scores, -1e30)
    top = jnp.max(scores, axis=-1, keepdims=True)
    weights = jnp.exp(scores - top)
    weights = (weights / jnp.sum(weights, axis=-1, keepdims=True)).astype(jnp.bfloat16)
    result = jnp.einsum("hts,shd->thd", weights, vals, preferred_element_type=jnp.float32)
    return result.reshape(length, width)


def swiglu_local(packed):
    half = packed.shape[1] // 2
    return jax.nn.silu(packed[:, :half]) * packed[:, half:]


def widen(block):
    return lax.all_gather(block, "mp", axis=0, tiled=True)


def narrow(term, count):
    return lax.psum_scatter(
        term(jnp.int32(0), count * lax.axis_size("mp")), "mp", scatter_dimension=0, tiled=True
    )


def widen_grad(block):
    return lax.all_gather(block, "mp", axis=0, tiled=True)


def narrow_grad(term, count):
    return lax.psum_scatter(
        term(jnp.int32(0), count * lax.axis_size("mp")), "mp", scatter_dimension=0, tiled=True
    )


def arrange(full):
    table, patch_rows, w_mix, w_dt, w_bc, w_mout, w_qkv, w_aout, w_ffin, w_ffout = full
    width = w_mix.shape[0]
    w_proj = jnp.concatenate([w_mix.reshape(width, -1), w_bc, w_dt], axis=1)
    return (
        table,
        patch_rows,
        w_proj,
        w_mout,
        w_qkv.reshape(width, -1),
        w_aout,
        w_ffin.reshape(width, -1),
        w_ffout,
    )


def table_terms(onehot, d_embed):
    upper = d_embed.astype(jnp.bfloat16)
    lower = (d_embed - upper.astype(jnp.float32)).astype(jnp.bfloat16)
    first = jnp.einsum("lpv,lpd->vd", onehot, upper, preferred_element_type=jnp.float32)
    return first + jnp.einsum("lpv,lpd->vd", onehot, lower, preferred_element_type=jnp.float32)


def on_device(
    byte_ids,
    segment_ids,
    embed_table,
    patch_weight,
    norm1_gain,
    mamba_in,
    mamba_dt,
    mamba_bc,
    conv_x,
    conv_bc,
    dt_bias,
    a_log,
    d_skip,
    gate_gain,
    mamba_out,
    norm2_gain,
    attn_qkv,
    attn_out,
    norm3_gain,
    ffn_in,
    ffn_out,
    d_out,
):
    parts = lax.axis_size("mp")
    index = lax.axis_index("mp")
    piece = byte_ids.shape[1]
    length = piece * parts
    per_pos = PATCH // parts
    inner_width = mamba_in.shape[2]
    state = mamba_bc.shape[1] // 2
    sharded = (
        embed_table,
        patch_weight,
        mamba_in,
        mamba_dt,
        mamba_bc,
        mamba_out,
        attn_qkv,
        attn_out,
        ffn_in,
        ffn_out,
    )
    fetched = (
        lax.all_gather(sharded[0], "dp", axis=0, tiled=True),
        lax.all_gather(sharded[1], "dp", axis=1, tiled=True),
        lax.all_gather(sharded[2], "dp", axis=0, tiled=True),
        lax.all_gather(sharded[3], "dp", axis=0, tiled=True),
        lax.all_gather(sharded[4], "dp", axis=0, tiled=True),
        lax.all_gather(sharded[5], "dp", axis=1, tiled=True),
        lax.all_gather(sharded[6], "dp", axis=0, tiled=True),
        lax.all_gather(sharded[7], "dp", axis=1, tiled=True),
        lax.all_gather(sharded[8], "dp", axis=0, tiled=True),
        lax.all_gather(sharded[9], "dp", axis=1, tiled=True),
    )
    table, patch_rows, w_proj, w_mout, w_qkv, w_aout, w_ffin, w_ffout = arrange(fetched)
    kept = []
    outputs = []
    for batch in range(MB):
        ids_all, seg_all = (
            lax.all_gather(byte_ids[batch], "mp", axis=0, tiled=True),
            lax.all_gather(segment_ids[batch], "mp", axis=0, tiled=True),
        )
        local_ids = lax.dynamic_slice_in_dim(ids_all, index * per_pos, per_pos, 1)
        onehot = (
            local_ids[:, :, None] == jnp.arange(VOCAB, dtype=jnp.int32)[None, None, :]
        ).astype(jnp.bfloat16)
        embedded = jnp.einsum("lpv,vd->lpd", onehot, table, preferred_element_type=jnp.float32)
        embedded = embedded.astype(jnp.bfloat16).reshape(length, -1)
        resid0 = narrow(lambda start, count: product(embedded, patch_rows), piece)
        wide1 = widen(rms_apply(resid0, norm1_gain).astype(jnp.bfloat16))
        proj = product(wide1, w_proj)
        gated = mixer_local(proj, seg_all, conv_x, conv_bc, dt_bias, a_log, d_skip)
        total = lax.psum(jnp.sum(gated * gated, axis=1), "mp")
        factor = lax.rsqrt(total / DIN + 1e-05)[:, None]
        gnormed = (gated * factor * gate_gain).astype(jnp.bfloat16)
        resid1 = resid0 + narrow(lambda start, count: product(gnormed, w_mout), piece)
        wide2 = widen(rms_apply(resid1, norm2_gain).astype(jnp.bfloat16))
        qkv = product(wide2, w_qkv)
        attended = attend_local(qkv, seg_all).astype(jnp.bfloat16)
        resid2 = resid1 + narrow(lambda start, count: product(attended, w_aout), piece)
        wide3 = widen(rms_apply(resid2, norm3_gain).astype(jnp.bfloat16))
        gate_up = product(wide3, w_ffin)
        hidden = swiglu_local(gate_up).astype(jnp.bfloat16)
        outputs.append(resid2 + narrow(lambda start, count: product(hidden, w_ffout), piece))
        kept.append(
            (
                seg_all,
                onehot,
                embedded,
                resid0,
                resid1,
                resid2,
                wide1,
                proj,
                gated,
                factor,
                gnormed,
                wide2,
                qkv,
                attended,
                wide3,
                gate_up,
                hidden,
            )
        )
    mixed = jnp.stack(outputs, axis=0)
    grad_resid = [d_out[batch] for batch in range(MB)]
    acc_ffin = jnp.zeros(w_ffin.shape, jnp.float32)
    acc_ffout = jnp.zeros(w_ffout.shape, jnp.float32)
    acc_gain3 = jnp.zeros(norm3_gain.shape, jnp.float32)
    for batch in range(MB):
        saved = kept[batch]
        wide_grad = widen_grad(grad_resid[batch].astype(jnp.bfloat16))
        acc_ffout = acc_ffout + product_left(saved[16], wide_grad)
        d_hidden = product_right(wide_grad, w_ffout)
        d_gate_up = jax.vjp(swiglu_local, saved[15])[1](d_hidden)[0].astype(jnp.bfloat16)
        acc_ffin = acc_ffin + product_left(saved[14], d_gate_up)
        d_norm = narrow_grad(lambda start, count: product_right(d_gate_up, w_ffin), piece)
        d_back, d_gain = jax.vjp(rms_apply, saved[5], norm3_gain)[1](d_norm)
        grad_resid[batch] = grad_resid[batch] + d_back
        acc_gain3 = acc_gain3 + d_gain
    acc_qkv = jnp.zeros(w_qkv.shape, jnp.float32)
    acc_aout = jnp.zeros(w_aout.shape, jnp.float32)
    acc_gain2 = jnp.zeros(norm2_gain.shape, jnp.float32)
    for batch in range(MB):
        saved = kept[batch]
        seg_all = saved[0]
        wide_grad = widen_grad(grad_resid[batch].astype(jnp.bfloat16))
        acc_aout = acc_aout + product_left(saved[13], wide_grad)
        d_att = product_right(wide_grad, w_aout)
        d_qkv = jax.vjp(lambda packed: attend_local(packed, seg_all), saved[12])[1](d_att)[0]
        d_qkv = d_qkv.astype(jnp.bfloat16)
        acc_qkv = acc_qkv + product_left(saved[11], d_qkv)
        d_norm = narrow_grad(lambda start, count: product_right(d_qkv, w_qkv), piece)
        d_back, d_gain = jax.vjp(rms_apply, saved[4], norm2_gain)[1](d_norm)
        grad_resid[batch] = grad_resid[batch] + d_back
        acc_gain2 = acc_gain2 + d_gain
    acc_proj = jnp.zeros(w_proj.shape, jnp.float32)
    acc_mout = jnp.zeros(w_mout.shape, jnp.float32)
    acc_ggain = jnp.zeros(gate_gain.shape, jnp.float32)
    acc_convx = jnp.zeros(conv_x.shape, jnp.float32)
    acc_convbc = jnp.zeros(conv_bc.shape, jnp.float32)
    acc_bias = jnp.zeros(dt_bias.shape, jnp.float32)
    acc_alog = jnp.zeros(a_log.shape, jnp.float32)
    acc_skip = jnp.zeros(d_skip.shape, jnp.float32)
    acc_gain1 = jnp.zeros(norm1_gain.shape, jnp.float32)
    for batch in range(MB):
        saved = kept[batch]
        seg_all = saved[0]
        gated = saved[8]
        factor = saved[9]
        wide_grad = widen_grad(grad_resid[batch].astype(jnp.bfloat16))
        acc_mout = acc_mout + product_left(saved[10], wide_grad)
        d_gn = product_right(wide_grad, w_mout)
        weighted = d_gn * gate_gain
        acc_ggain = acc_ggain + jnp.sum(gated * factor * d_gn, axis=0)
        cross = lax.psum(jnp.sum(gated * weighted, axis=1), "mp")
        d_gated = weighted * factor - gated * factor**3 * (cross / DIN)[:, None]
        pull = jax.vjp(
            lambda packed, taps_x, taps_bc, bias, decay, skip: mixer_local(
                packed, seg_all, taps_x, taps_bc, bias, decay, skip
            ),
            saved[7],
            conv_x,
            conv_bc,
            dt_bias,
            a_log,
            d_skip,
        )[1]
        d_proj, d_convx, d_convbc, d_bias, d_alog, d_skipped = pull(d_gated)
        d_proj = d_proj.astype(jnp.bfloat16)
        acc_convx = acc_convx + d_convx
        acc_convbc = acc_convbc + d_convbc
        acc_bias = acc_bias + d_bias
        acc_alog = acc_alog + d_alog
        acc_skip = acc_skip + d_skipped
        acc_proj = acc_proj + product_left(saved[6], d_proj)
        d_norm = narrow_grad(lambda start, count: product_right(d_proj, w_proj), piece)
        d_back, d_gain = jax.vjp(rms_apply, saved[3], norm1_gain)[1](d_norm)
        grad_resid[batch] = grad_resid[batch] + d_back
        acc_gain1 = acc_gain1 + d_gain
    acc_patch = jnp.zeros(patch_rows.shape, jnp.float32)
    acc_table = jnp.zeros(table.shape, jnp.float32)
    for batch in range(MB):
        saved = kept[batch]
        wide_grad = widen_grad(grad_resid[batch].astype(jnp.bfloat16))
        acc_patch = acc_patch + product_left(saved[2], wide_grad)
        d_embed = product_right(wide_grad, patch_rows).reshape(length, per_pos, -1)
        acc_table = acc_table + table_terms(saved[1], d_embed)
    model_width = w_proj.shape[0]
    grad_mix = acc_proj[:, : 2 * inner_width].reshape(model_width, 2, inner_width)
    grad_bc = acc_proj[:, 2 * inner_width : 2 * inner_width + 2 * state]
    grad_dt = acc_proj[:, 2 * inner_width + 2 * state :]
    (
        acc_patch,
        grad_mix,
        grad_dt,
        acc_mout,
        acc_convx,
        acc_bias,
        acc_alog,
        acc_skip,
        acc_ggain,
        acc_qkv,
        acc_aout,
        acc_ffin,
        acc_ffout,
    ) = lax.psum(
        (
            acc_patch,
            grad_mix,
            grad_dt,
            acc_mout,
            acc_convx,
            acc_bias,
            acc_alog,
            acc_skip,
            acc_ggain,
            acc_qkv,
            acc_aout,
            acc_ffin,
            acc_ffout,
        ),
        "dp",
    )
    acc_table, grad_bc, acc_convbc, acc_gain1, acc_gain2, acc_gain3 = lax.psum(
        (acc_table, grad_bc, acc_convbc, acc_gain1, acc_gain2, acc_gain3), ("dp", "mp")
    )
    grad_qkv = acc_qkv.reshape(model_width, 3, -1)
    grad_ffin = acc_ffin.reshape(model_width, 2, -1)
    return (
        mixed,
        acc_table,
        acc_patch,
        acc_gain1,
        grad_mix,
        grad_dt,
        grad_bc,
        acc_convx,
        acc_convbc,
        acc_bias,
        acc_alog,
        acc_skip,
        acc_ggain,
        acc_mout,
        acc_gain2,
        grad_qkv,
        acc_aout,
        acc_gain3,
        grad_ffin,
        acc_ffout,
    )


def solution(mesh):
    sizes = dict(mesh.shape)
    by_rows = sizes["mp"] == MB and sizes["dp"] == 16
    return jax.shard_map(
        on_device_rows if by_rows else on_device,
        mesh=mesh,
        in_specs=(
            P(None, ("dp", "mp"), None),
            P(None, ("dp", "mp")),
            P("dp", None),
            P("mp", "dp"),
            P(),
            P("dp", None, "mp"),
            P("dp", "mp"),
            P("dp", None),
            P(None, "mp"),
            P(),
            P("mp"),
            P("mp"),
            P("mp"),
            P("mp"),
            P("mp", "dp"),
            P(),
            P("dp", None, "mp"),
            P("mp", "dp"),
            P(),
            P("dp", None, "mp"),
            P("mp", "dp"),
            P(None, ("dp", "mp"), None),
        ),
        out_specs=(
            P(None, ("dp", "mp"), None),
            P(),
            P("mp", None),
            P(),
            P(None, None, "mp"),
            P(None, "mp"),
            P(),
            P(None, "mp"),
            P(),
            P("mp"),
            P("mp"),
            P("mp"),
            P("mp"),
            P("mp", None),
            P(),
            P(None, None, "mp"),
            P("mp", None),
            P(),
            P(None, None, "mp"),
            P("mp", None),
        ),
        check_vma=False,
    )
```
